128 devices in a mesh: tm: 16 (over y, x), block: 8 (over z, core).
Axes of the slice: x: 4, y: 4, z: 4, core: 2. Of those that a mesh axis runs over, the one named last changes fastest.
Arguments:
- noise: float32 [4096, 64], P('tm'), may hold values from -6 to 6
- retain: float32 [4096, 16], P('tm', 'block'), may hold values from 0.25 to 1
- control_weight: bfloat16 [64, 16, 128, 128], P(None, 'block'), may hold values from -0.0625 to 0.0625
- input_weight: float32 [64, 2048], P(None, 'block'), may hold values from -0.75 to 0.75
- initial_state: float32 [2048], P('block'), may hold values from -6 to 6
- norm_gain: float32 [2048], P('block'), may hold values from 0.5 to 1.5
- gate_weight: bfloat16 [2048, 8192], P(None, 'block'), may hold values from -0.125 to 0.125
- up_weight: bfloat16 [2048, 8192], P(None, 'block'), may hold values from -0.125 to 0.125
- down_weight: bfloat16 [8192, 2048], P('block'), may hold values from -0.09375 to 0.09375
Outputs:
- layer_out: bfloat16 [4096, 2048], P('tm', 'block')
The draws below stay inside these ranges and needn't reach their ends.
All inputs are finite; a program needn't handle non-finite values.
Results may differ from the reference program's by a relative error of at most 0.013.
Values may be sent and summed in bfloat16 or wider, within the bound.
No kernel may reach another device: no remote copies, remote signals or barrier semaphores. Data moves between devices by JAX's collectives and lax.ppermute only.
A program may use at most 192 MiB of HBM per device.

```python
import math
import jax
import jax.numpy as jnp
from jax import lax

NB = 16
BS = 128
CTRL = 64
FF = 8192
D = 2048
STEPS = 4096


def draw_noise(key, part):
    key = jax.random.fold_in(key, 11)
    first, second = jax.random.split(key, 2)
    base = jnp.clip(jax.random.normal(first, (STEPS + 3, CTRL), jnp.float32), -2.5, 2.5)
    rough = jnp.clip(jax.random.normal(second, (STEPS, CTRL), jnp.float32), -3.0, 3.0)
    common = (base[3:] + base[2:-1] + base[1:-2] + base[:-3]) * 0.4
    return (common + 0.6 * rough).astype(jnp.float32)


def draw_retain(key, part):
    key = jax.random.fold_in(key, 7)
    streams = jax.random.split(key, 7)
    slow_limit = 5
    slow = jax.random.randint(streams[0], (NB,), 0, 10) < slow_limit
    slow_rate = jax.random.uniform(streams[1], (NB,), jnp.float32, 0.5, 1.0) / STEPS
    fast_rate = 1.0 / jax.random.uniform(streams[2], (NB,), jnp.float32, 8.0, 20.0)
    rate = jnp.where(slow, slow_rate, fast_rate)
    segment = jnp.exp(jax.random.uniform(streams[3], (STEPS // 32, NB), jnp.float32, -0.7, 0.7))
    segment = jnp.repeat(segment, 32, axis=0)
    jitter = jnp.exp(jax.random.uniform(streams[4], (STEPS, NB), jnp.float32, -0.3, 0.3))
    kept = jnp.exp(-rate[None, :] * segment * jitter)
    positions = jax.random.randint(streams[5], (3, NB), 0, STEPS)
    struck = jnp.any(jnp.arange(STEPS)[:, None, None] == positions[None, :, :], axis=1)
    depth = jax.random.uniform(streams[6], (STEPS, NB), jnp.float32, 0.5, 0.8)
    return (kept * jnp.where(struck, depth, 1.0)).astype(jnp.float32)


def spiked(drawn, own_key, source, target, blocks, factor):
    def block_of(position):
        return (jnp.arange(drawn.shape[position]) // (drawn.shape[position] // blocks)).reshape((-1,) + (1,) * (drawn.ndim - 1 - position))

    one_side = jax.random.permutation(own_key, blocks)[block_of(target)]
    far = (block_of(target) + blocks // 2) % blocks
    return jnp.where((block_of(source) == one_side) | (block_of(source) == far), factor * drawn, drawn)


def level_of(rng, extent, shards, least, largest):
    loudness = 1.0
    for dim, shards_of in shards:
        steps = jax.random.uniform(jax.random.fold_in(jax.random.fold_in(rng, 6), dim), (shards_of,), jnp.float32, least / len(shards), largest / len(shards))
        loudness = loudness * jnp.repeat(jnp.exp(steps), extent[dim] // shards_of).reshape((-1,) + (1,) * (len(extent) - 1 - dim))
    return loudness


def bell_draw(own_key, dims, spread, most, shards=(), held_as=jnp.bfloat16):
    level = level_of(own_key, dims, shards, -0.22, 0.18) if shards else 1.0
    drawn = jax.random.normal(own_key, dims, jnp.float32) * spread * level
    return jnp.minimum(jnp.maximum(drawn, -most), most).astype(held_as)


def bell_draw_with(rng, extent, spread, reach, pieces, heavy, dtype=jnp.bfloat16):
    result = spread * jax.random.normal(rng, extent, jnp.float32)
    if pieces:
        result = result * level_of(rng, extent, pieces, -0.22, 0.18)
    return jnp.clip(spiked(result, jax.random.fold_in(rng, 3), *heavy), -reach, reach).astype(dtype)


def setup_inputs(seed: int = 0) -> dict:
    key_of = jax.random.split(jax.random.key(seed), 10)
    return {
        "noise": draw_noise(jax.random.fold_in(key_of[9], 71), 0),
        "retain": draw_retain(jax.random.fold_in(key_of[9], 71), 0),
        "control_weight": bell_draw(key_of[2], (CTRL, NB, BS, BS), (CTRL * BS) ** -0.5, 0.0625, ((1, 8),)),
        "input_weight": bell_draw(key_of[3], (CTRL, D), CTRL ** -0.5, 0.75, ((1, 8),), jnp.float32),
        "initial_state": bell_draw(key_of[4], (D,), 1.0, 6.0, ((0, 8),), jnp.float32),
        "norm_gain": jnp.clip(1.0 + 0.1 * jax.random.normal(key_of[5], (D,), jnp.float32), 0.5, 1.5),
        "gate_weight": bell_draw(key_of[6], (D, FF), D ** -0.5, 0.125, ((1, 8),)),
        "up_weight": bell_draw(key_of[7], (D, FF), D ** -0.5, 0.125, ((1, 8),)),
        "down_weight": bell_draw_with(key_of[8], (FF, D), FF ** -0.5, 0.09375, ((0, 8),), (0, 1, 8, 2.0)),
    }


def reference(noise, retain, control_weight, input_weight, initial_state, norm_gain, gate_weight, up_weight, down_weight):
    raw = control_weight.astype(jnp.float32)
    skew = ((raw - jnp.swapaxes(raw, 2, 3)) / math.sqrt(2.0)).astype(jnp.bfloat16)
    skew_wide = skew.astype(jnp.float32)
    noise_low = noise.astype(jnp.bfloat16)
    factor = 1.0 / math.sqrt(STEPS)
    drive = jnp.dot(noise, input_weight, precision=lax.Precision.HIGHEST).reshape(STEPS, NB, BS)
    drive = drive * jnp.sqrt(1.0 - retain * retain)[:, :, None]
    outer_count = STEPS // 16
    noise_blocks = noise_low.reshape(outer_count, 16, CTRL)
    retain_blocks = retain.reshape(outer_count, 16, NB)
    drive_blocks = drive.reshape(outer_count, 16, NB, BS)

    def outer(state, inputs):
        weights, kept, pushed = inputs
        summed = jnp.einsum('ti,ibjk->tbjk', weights.astype(jnp.float32), skew_wide, precision=lax.Precision.HIGHEST) * factor

        def inner(current, item):
            matrix, gain_now, push = item
            turned = jnp.einsum('bjk,bk->bj', matrix, current, precision=lax.Precision.HIGHEST)
            fresh = gain_now[:, None] * (current + turned) + push
            return (fresh, fresh)
        state, history = lax.scan(inner, state, (summed, kept, pushed))
        return (state, history)
    start = initial_state.reshape(NB, BS)
    history = lax.scan(outer, start, (noise_blocks, retain_blocks, drive_blocks))[1]
    states = history.reshape(STEPS, NB, BS)
    scaled = states * lax.rsqrt(lax.optimization_barrier(jnp.mean(states * states, axis=-1, keepdims=True)) + 1e-05)
    normed = (scaled * norm_gain.reshape(NB, BS)).reshape(STEPS, NB * BS).astype(jnp.bfloat16)
    gate = jnp.dot(normed, gate_weight, preferred_element_type=jnp.float32)
    upward = jnp.dot(normed, up_weight, preferred_element_type=jnp.float32)
    hidden = (jax.nn.silu(gate) * upward).astype(jnp.bfloat16)
    mixed = jnp.dot(hidden, down_weight, preferred_element_type=jnp.float32)
    return (states.reshape(STEPS, NB * BS) + mixed).astype(jnp.bfloat16)
```

```python
import functools
import math

import jax
import jax.numpy as jnp
from jax import lax
from jax.experimental import pallas as pl
from jax.experimental.pallas import tpu as pltpu
from jax.sharding import PartitionSpec as P

F32 = jnp.float32
BF16 = jnp.bfloat16
GROUPS = 16
SPAN = 16
WIDTH = 128
ROWS = 144
PITCH = 129
MAP_ROWS = 144
VMEM = pl.BlockSpec(memory_space=pltpu.VMEM)
SMEM = pl.BlockSpec(memory_space=pltpu.SMEM)
ANY = pl.BlockSpec(memory_space=pl.ANY)


def split3(v):
    hi = v.astype(BF16)
    rest = v - hi.astype(F32)
    mid = rest.astype(BF16)
    return hi, mid, (rest - mid.astype(F32)).astype(BF16)


def pack_map(ref, b, matrix, offset, kept):
    ref[b, :WIDTH, :] = matrix.astype(BF16)
    row = lax.broadcasted_iota(jnp.int32, (16, WIDTH), 0)
    tail = jnp.zeros((16, WIDTH), F32)
    kept_row = jnp.full((1, WIDTH), 1.0, F32) * kept
    for k, part in enumerate((*split3(offset), *split3(kept_row))):
        tail = jnp.where(row == k, jnp.broadcast_to(part.astype(F32), (16, WIDTH)), tail)
    ref[b, WIDTH:, :] = tail.astype(BF16)


def unpack_map(ref, b):
    matrix = ref[b, :WIDTH, :]
    tail = ref[b, WIDTH:, :].astype(F32)
    offset = tail[0:1] + tail[1:2] + tail[2:3]
    kept = tail[3:4] + tail[4:5] + tail[5:6]
    return matrix, offset, kept


def row_times(h, matrix):
    row = lax.broadcasted_iota(jnp.int32, (16, WIDTH), 0)
    hi = h.astype(BF16).astype(F32)
    lo = h - hi
    both = jnp.where(row == 0, jnp.broadcast_to(hi, (16, WIDTH)), jnp.broadcast_to(lo, (16, WIDTH)))
    out = jnp.dot(both.astype(BF16), matrix, preferred_element_type=F32)
    return out[0:1] + out[1:2]


def compose_kernel(
    noise_ref, retain_s, retain_ref, cw_ref, iw_ref, q_ref, off_ref, send_ref, grp_ref, kept_ref, skw, am, tx, qs, sem
):
    steps = noise_ref.shape[0]
    rows = lax.broadcasted_iota(jnp.int32, (WIDTH, WIDTH), 0)
    cols = lax.broadcasted_iota(jnp.int32, (WIDTH, WIDTH), 1)
    eye = (rows == cols).astype(F32)
    eye_low = eye.astype(BF16)
    noise = noise_ref[...]
    drive = jnp.dot(noise, iw_ref[...], precision=lax.Precision.HIGHEST, preferred_element_type=F32)
    kept = retain_ref[...]
    scale = jnp.sqrt(1.0 - kept * kept)
    for b in range(2):
        off_ref[b * steps : (b + 1) * steps, :] = drive[:, b * WIDTH : (b + 1) * WIDTH] * scale[:, b : b + 1]

    def skew_body(i, carry):
        for b in range(2):
            raw = cw_ref[i, b]
            turned = lax.dot_general(eye_low, raw, (((1,), (1,)), ((), ())), preferred_element_type=F32)
            diff = ((turned - raw.astype(F32)) * (1.0 / math.sqrt(2.0))).astype(BF16).astype(F32)
            skw[pl.ds((b * 64 + i) * PITCH, WIDTH), :] = diff
        return carry

    lax.fori_loop(0, 64, skew_body, 0, unroll=2)
    low = (noise.astype(BF16).astype(F32) * (1.0 / 64.0)).astype(BF16)

    def build_body(j, carry):
        w = jnp.concatenate(
            [skw[pl.ds(b * 64 * PITCH + j, 64, stride=PITCH), :] for b in range(2)], axis=1
        ).astype(BF16)
        out = jnp.dot(low, w, preferred_element_type=F32)
        for b in range(2):
            am[pl.ds(b * steps * PITCH + j, steps, stride=PITCH), :] = out[:, b * WIDTH : (b + 1) * WIDTH]
        return carry

    lax.fori_loop(0, WIDTH, build_body, 0, unroll=2)
    tail_row = lax.broadcasted_iota(jnp.int32, (ROWS - WIDTH, WIDTH), 0)

    def init(c, carry):
        tx[c, :WIDTH, :] = eye
        tx[c, WIDTH:, :] = jnp.zeros((ROWS - WIDTH, WIDTH), F32)
        return carry

    lax.fori_loop(0, 2 * GROUPS, init, 0)

    def step(s, carry):
        slot = lax.rem(s, 2)

        @pl.when(s >= 2)
        def _():
            pltpu.make_async_copy(qs.at[slot], q_ref.at[s], sem.at[slot]).wait()

        def group(g, inner):
            t = g * SPAN + s
            for b in range(2):
                c = g * 2 + b
                x = tx[c]
                w = am[pl.ds((b * steps + t) * PITCH, WIDTH), :].astype(BF16)
                y = (x + jnp.dot(x.astype(BF16), w, preferred_element_type=F32)) * retain_s[t, b]
                push = off_ref[pl.ds(b * steps + t, 1), :]
                tail = y[WIDTH:, :] + jnp.where(
                    tail_row == 0, jnp.broadcast_to(push, (ROWS - WIDTH, WIDTH)), 0.0
                )
                tx[c, :WIDTH, :] = y[:WIDTH]
                tx[c, WIDTH:, :] = tail
                qs[slot, c] = y[:WIDTH].astype(BF16)
                off_ref[pl.ds(b * steps + t, 1), :] = tail[:1]
            return inner

        lax.fori_loop(0, GROUPS, group, 0, unroll=4)
        pltpu.make_async_copy(qs.at[slot], q_ref.at[s], sem.at[slot]).start()
        return carry

    lax.fori_loop(0, SPAN, step, 0)
    for s in (SPAN - 2, SPAN - 1):
        pltpu.make_async_copy(qs.at[s % 2], q_ref.at[s], sem.at[s % 2]).wait()

    keeps = [
        [
            lax.fori_loop(0, SPAN, lambda i, a, g=g, b=b: a * retain_s[g * SPAN + i, b], jnp.float32(1.0))
            for b in range(2)
        ]
        for g in range(GROUPS)
    ]
    for g in range(GROUPS):
        for b in range(2):
            c = g * 2 + b
            kept_ref[g, b] = keeps[g][b]
            m = tx[c, :WIDTH, :] - eye * keeps[g][b]
            tx[c, :WIDTH, :] = m
            grp_ref[c] = m.astype(BF16)
    stride = 1
    while stride < GROUPS:
        for g1 in range(0, GROUPS, 2 * stride):
            g2 = g1 + stride
            for b in range(2):
                first, second = tx[g1 * 2 + b], tx[g2 * 2 + b]
                prod = jnp.dot(first.astype(BF16), second[:WIDTH].astype(BF16), preferred_element_type=F32)
                k1, k2 = keeps[g1][b], keeps[g2][b]
                tx[g1 * 2 + b, :WIDTH, :] = prod[:WIDTH] + first[:WIDTH] * k2 + second[:WIDTH] * k1
                tx[g1 * 2 + b, WIDTH:, :] = prod[WIDTH:] + first[WIDTH:] * k2 + second[WIDTH:]
                keeps[g1][b] = k1 * k2
        stride *= 2
    for b in range(2):
        pack_map(send_ref, b, tx[b, :WIDTH, :], tx[b, WIDTH : WIDTH + 1, :], keeps[0][b])


def compose(noise, retain, control_weight, input_weight):
    steps = noise.shape[0]
    return pl.pallas_call(
        compose_kernel,
        out_shape=(
            jax.ShapeDtypeStruct((SPAN, 2 * GROUPS, WIDTH, WIDTH), BF16),
            jax.ShapeDtypeStruct((2 * steps, WIDTH), F32),
            jax.ShapeDtypeStruct((2, MAP_ROWS, WIDTH), BF16),
            jax.ShapeDtypeStruct((2 * GROUPS, WIDTH, WIDTH), BF16),
            jax.ShapeDtypeStruct((GROUPS, 2), F32),
        ),
        in_specs=[VMEM, SMEM, VMEM, VMEM, VMEM],
        out_specs=(ANY, VMEM, VMEM, VMEM, SMEM),
        scratch_shapes=[
            pltpu.VMEM((128 * PITCH + 8, WIDTH), F32),
            pltpu.VMEM((2 * steps * PITCH + 8, WIDTH), F32),
            pltpu.VMEM((2 * GROUPS, ROWS, WIDTH), F32),
            pltpu.VMEM((2, 2 * GROUPS, WIDTH, WIDTH), BF16),
            pltpu.SemaphoreType.DMA((2,)),
        ],
        compiler_params=pltpu.CompilerParams(vmem_limit_bytes=60 * 1024 * 1024),
        name="compose",
    )(noise, retain, retain, control_weight, input_weight)


def row_kernel(place_s, m0, m1, m2, m3, out_ref, held):
    x = place_s[1]
    for k, ref in enumerate((m0, m1, m2, m3)):
        held[lax.rem(x + 4 - k, 4)] = ref[...]
    for b in range(2):
        parts = []
        for k in range(4):
            matrix, offset, kept = unpack_map(held.at[k], b)
            parts.append((matrix.astype(F32), offset, kept))
        while len(parts) > 1:
            merged = []
            for (m1_, o1, k1), (m2_, o2, k2) in zip(parts[::2], parts[1::2]):
                low = m2_.astype(BF16)
                prod = jnp.dot(m1_.astype(BF16), low, preferred_element_type=F32)
                merged.append((prod + m1_ * k2 + m2_ * k1, row_times(o1, low) + o1 * k2 + o2, k1 * k2))
            parts = merged
        pack_map(out_ref, b, *parts[0])


def row_map(place, maps):
    return pl.pallas_call(
        row_kernel,
        out_shape=jax.ShapeDtypeStruct((2, MAP_ROWS, WIDTH), BF16),
        in_specs=[SMEM] + [VMEM] * 4,
        out_specs=VMEM,
        scratch_shapes=[pltpu.VMEM((4, 2, MAP_ROWS, WIDTH), BF16)],
        name="row_map",
    )(place, *maps)


def replay_kernel(place_s, kept_s, init_ref, y1, y2, y3, x1, x2, x3, off_ref, grp_ref, gain_ref, q_ref,
                  states_ref, normed_ref, start):
    g = pl.program_id(0)
    steps = SPAN * GROUPS

    @pl.when(g == 0)
    def _():
        for b in range(2):
            h = init_ref[b : b + 1, :]
            for place, refs in ((place_s[0], (y1, y2, y3)), (place_s[1], (x1, x2, x3))):
                for k in (3, 2, 1):
                    matrix, offset, kept = unpack_map(refs[k - 1], b)
                    h = jnp.where(k <= place, h * kept + row_times(h, matrix) + offset, h)
            start[b : b + 1, :] = h

    for b in range(2):
        h = start[b : b + 1, :]
        spread = jnp.broadcast_to(h, (WIDTH, WIDTH)).T
        last = off_ref[pl.ds(b * steps + g * SPAN + SPAN - 1, 1), :]
        start[b : b + 1, :] = h * kept_s[g, b] + row_times(h, grp_ref[g * 2 + b]) + last
        rows = []
        for s in range(SPAN):
            rows.append(jnp.sum(q_ref[s, b].astype(F32) * spread, axis=0, keepdims=True))
        base = pl.multiple_of(b * steps + g * SPAN, SPAN)
        states = jnp.concatenate(rows, axis=0) + off_ref[pl.ds(base, SPAN), :]
        states_ref[:, b * WIDTH : (b + 1) * WIDTH] = states
        mean = jnp.mean(states * states, axis=-1, keepdims=True)
        normed = states * lax.rsqrt(mean + 1e-05) * gain_ref[b : b + 1, :]
        normed_ref[:, b * WIDTH : (b + 1) * WIDTH] = normed.astype(BF16)


def replay(place, kept, init, y_maps, x_maps, off, grp, gain, q):
    steps = SPAN * GROUPS
    return pl.pallas_call(
        replay_kernel,
        grid=(GROUPS,),
        out_shape=(
            jax.ShapeDtypeStruct((steps, 2 * WIDTH), F32),
            jax.ShapeDtypeStruct((steps, 2 * WIDTH), BF16),
        ),
        in_specs=[SMEM, SMEM]
        + [VMEM] * 10
        + [pl.BlockSpec((SPAN, 2, WIDTH, WIDTH), lambda g: (0, g, 0, 0))],
        out_specs=(
            pl.BlockSpec((SPAN, 2 * WIDTH), lambda g: (g, 0)),
            pl.BlockSpec((SPAN, 2 * WIDTH), lambda g: (g, 0)),
        ),
        scratch_shapes=[pltpu.VMEM((8, WIDTH), F32)],
        name="replay",
    )(place, kept, init, *y_maps, *x_maps, off, grp, gain, q)


def x_back(v, k):
    return lax.ppermute(v, "tm", [(y * 4 + x, y * 4 + (x + k) % 4) for y in range(4) for x in range(4)])


def y_back(v, k):
    return lax.ppermute(v, "tm", [(y * 4 + x, (y + k) % 4 * 4 + x) for y in range(4) for x in range(4)])


def z_back(v, k):
    return lax.ppermute(v, "block", [(z * 2 + c, (z + k) % 4 * 2 + c) for z in range(4) for c in range(2)])


def other_core(v):
    return lax.ppermute(v, "block", [(s, s ^ 1) for s in range(8)])


def body(
    noise,
    retain,
    control_weight,
    input_weight,
    initial_state,
    norm_gain,
    gate_weight,
    up_weight,
    down_weight,
):
    tm = lax.axis_index("tm")
    block = lax.axis_index("block")
    z, core = block // 2, block % 2
    place = jnp.stack([tm // 4, tm % 4]).astype(jnp.int32)
    q, off, own, grp, kept = compose(noise, retain, control_weight, input_weight)
    x_maps = [x_back(own, k) for k in (1, 2, 3)]
    total = row_map(place, [own, *x_maps])
    y_maps = [y_back(total, k) for k in (1, 2, 3)]
    states, normed = replay(
        place, kept, initial_state.reshape(2, WIDTH), y_maps, x_maps, off, grp, norm_gain.reshape(2, WIDTH), q
    )
    mine = jnp.stack([normed] + [z_back(normed, k) for k in (1, 2, 3)])
    theirs = other_core(mine)
    both = jnp.where(core == 0, jnp.stack([mine, theirs], 1), jnp.stack([theirs, mine], 1))
    both = both[(z - jnp.arange(4)) % 4]
    piece = both.transpose(2, 0, 1, 3).reshape(256, 2048)
    gate = jnp.dot(piece, gate_weight, preferred_element_type=F32)
    upward = jnp.dot(piece, up_weight, preferred_element_type=F32)
    hidden = (jax.nn.silu(gate) * upward).astype(BF16)
    part = jnp.dot(hidden, down_weight, preferred_element_type=F32).astype(BF16)
    part = part.reshape(256, 4, 2, 256).transpose(2, 1, 0, 3)
    kept_half = lax.dynamic_index_in_dim(part, core, 0, keepdims=False)
    sent_half = lax.dynamic_index_in_dim(part, 1 - core, 0, keepdims=False)
    chip = kept_half.astype(F32) + other_core(sent_half).astype(F32)
    mixed = lax.dynamic_index_in_dim(chip, z, 0, keepdims=False)
    chip = chip.astype(BF16)
    for k in (1, 2, 3):
        mixed = mixed + z_back(lax.dynamic_index_in_dim(chip, (z + k) % 4, 0, keepdims=False), k).astype(F32)
    return (states + mixed).astype(BF16)


def solution(mesh):
    placed = (
        P("tm", None),
        P("tm", "block"),
        P(None, "block", None, None),
        P(None, "block"),
        P("block"),
        P("block"),
        P(None, "block"),
        P(None, "block"),
        P("block", None),
    )
    return jax.shard_map(body, mesh=mesh, in_specs=placed, out_specs=P("tm", "block"), check_vma=False)
```

```python
import functools
import math

import jax
import jax.numpy as jnp
from jax import lax
from jax.experimental import pallas as pl
from jax.experimental.pallas import tpu as pltpu
from jax.sharding import PartitionSpec as P

F32 = jnp.float32
BF16 = jnp.bfloat16
GROUPS = 16
SPAN = 16
WIDTH = 128
ROWS = 144
PITCH = 129
MAP_ROWS = 144
VMEM = pl.BlockSpec(memory_space=pltpu.VMEM)
SMEM = pl.BlockSpec(memory_space=pltpu.SMEM)
ANY = pl.BlockSpec(memory_space=pl.ANY)


def split3(v):
    hi = v.astype(BF16)
    rest = v - hi.astype(F32)
    mid = rest.astype(BF16)
    return hi, mid, (rest - mid.astype(F32)).astype(BF16)


def pack_map(ref, b, matrix, offset, kept):
    ref[b, :WIDTH, :] = matrix.astype(BF16)
    row = lax.broadcasted_iota(jnp.int32, (16, WIDTH), 0)
    tail = jnp.zeros((16, WIDTH), F32)
    kept_row = jnp.full((1, WIDTH), 1.0, F32) * kept
    for k, part in enumerate((*split3(offset), *split3(kept_row))):
        tail = jnp.where(row == k, jnp.broadcast_to(part.astype(F32), (16, WIDTH)), tail)
    ref[b, WIDTH:, :] = tail.astype(BF16)


def unpack_map(ref, b):
    matrix = ref[b, :WIDTH, :]
    tail = ref[b, WIDTH:, :].astype(F32)
    offset = tail[0:1] + tail[1:2] + tail[2:3]
    kept = tail[3:4] + tail[4:5] + tail[5:6]
    return matrix, offset, kept


def row_times(h, matrix):
    row = lax.broadcasted_iota(jnp.int32, (16, WIDTH), 0)
    hi = h.astype(BF16).astype(F32)
    lo = h - hi
    both = jnp.where(row == 0, jnp.broadcast_to(hi, (16, WIDTH)), jnp.broadcast_to(lo, (16, WIDTH)))
    out = jnp.dot(both.astype(BF16), matrix, preferred_element_type=F32)
    return out[0:1] + out[1:2]


def compose_kernel(
    place_s, noise_ref, retain_s, retain_ref, cw_ref, iw_ref, q_ref, off_ref, send_ref, grp_ref, kept_ref, skw, am, sem
):
    steps = noise_ref.shape[1]
    loads = [
        pltpu.make_async_copy(cw_ref.at[pl.ds(32 * k, 32)], q_ref.at[k], sem.at[k]) for k in range(4)
    ]
    for load in loads:
        load.start()
    rows = lax.broadcasted_iota(jnp.int32, (WIDTH, WIDTH), 0)
    cols = lax.broadcasted_iota(jnp.int32, (WIDTH, WIDTH), 1)
    eye = (rows == cols).astype(F32)
    noise = noise_ref[...].T
    drive = jnp.dot(noise, iw_ref[...], precision=lax.Precision.HIGHEST, preferred_element_type=F32)
    kept = retain_ref[...]
    scale = jnp.sqrt(1.0 - kept * kept)
    for b in range(2):
        spread = jnp.broadcast_to(scale[b : b + 1, :], (WIDTH, steps)).T
        off_ref[b * steps : (b + 1) * steps, :] = drive[:, b * WIDTH : (b + 1) * WIDTH] * spread

    def skew_body(base, i, carry):
        for b in range(2):
            raw = q_ref[base // 16, i * 2 + b]
            diff = (raw.T.astype(F32) - raw.astype(F32)) * (1.0 / math.sqrt(2.0))
            skw[pl.ds((b * 64 + base + i) * PITCH, WIDTH), :] = diff.astype(BF16).astype(F32)
        return carry

    for k in range(4):
        loads[k].wait()
        lax.fori_loop(0, 16, functools.partial(skew_body, 16 * k), 0, unroll=8)
    low = (noise.astype(BF16).astype(F32) * (1.0 / 64.0)).astype(BF16)

    def build_body(j, carry):
        w = jnp.concatenate(
            [skw[pl.ds(b * 64 * PITCH + j, 64, stride=PITCH), :] for b in range(2)], axis=1
        ).astype(BF16)
        out = jnp.dot(low, w, preferred_element_type=F32)
        for b in range(2):
            am[pl.ds(b * steps * PITCH + j, steps, stride=PITCH), :] = out[:, b * WIDTH : (b + 1) * WIDTH]
        return carry

    lax.fori_loop(0, WIDTH, build_body, 0, unroll=16)
    tail_rows = ROWS - WIDTH
    tail_row = lax.broadcasted_iota(jnp.int32, (tail_rows, WIDTH), 0)
    zero = jnp.zeros((WIDTH, WIDTH), BF16)

    def run(c):
        return skw.at[pl.ds(pl.multiple_of(c * ROWS, 16), ROWS), :]

    def step_matrix(t, b):
        return am[pl.ds((b * steps + t) * PITCH, WIDTH), :]

    def finish(s, g, b, matrix, tail):
        t = g * SPAN + s
        c = g * 2 + b
        rate = retain_s[b, t]
        push = off_ref[pl.ds(b * steps + t, 1), :]
        matrix = matrix * rate
        placed = jnp.where(tail_row == 0, jnp.broadcast_to(push, (tail_rows, WIDTH)), 0.0)
        tail = placed if tail is None else tail * rate + placed
        run(c)[:WIDTH, :] = matrix
        run(c)[WIDTH:, :] = tail
        q_ref[s, c] = matrix.astype(BF16)
        off_ref[pl.ds(b * steps + t, 1), :] = tail[:1]
        return rate

    def first(g, carry):
        for b in range(2):
            kept_ref[g, b] = finish(0, g, b, eye + step_matrix(g * SPAN, b), None)
        return carry

    lax.fori_loop(0, GROUPS, first, 0, unroll=4)

    def step(s, carry):
        def group(g, inner):
            t = g * SPAN + s
            now = [run(g * 2 + b)[...] for b in range(2)]
            low0, low1 = [step_matrix(t, b).astype(BF16) for b in range(2)]
            w = jnp.concatenate(
                [jnp.concatenate([low0, zero], axis=1), jnp.concatenate([zero, low1], axis=1)], axis=0
            )
            both = jnp.concatenate([x.astype(BF16) for x in now], axis=1)
            turned = jnp.dot(both, w, preferred_element_type=F32)
            for b in range(2):
                y = now[b] + turned[:, b * WIDTH : (b + 1) * WIDTH]
                rate = finish(s, g, b, y[:WIDTH], y[WIDTH:])
                kept_ref[g, b] = kept_ref[g, b] * rate
            return inner

        lax.fori_loop(0, GROUPS, group, 0, unroll=16)
        return carry

    lax.fori_loop(1, SPAN, step, 0)

    keeps = [[kept_ref[g, b] for b in range(2)] for g in range(GROUPS)]
    for g in range(GROUPS):
        for b in range(2):
            c = g * 2 + b
            m = run(c)[:WIDTH, :] - eye * keeps[g][b]
            run(c)[:WIDTH, :] = m
            grp_ref[c] = m.astype(BF16)
    stride = 1
    while stride < GROUPS:
        for g1 in range(0, GROUPS, 2 * stride):
            g2 = g1 + stride
            for b in range(2):
                one, two = run(g1 * 2 + b)[...], run(g2 * 2 + b)[...]
                prod = jnp.dot(one.astype(BF16), two[:WIDTH].astype(BF16), preferred_element_type=F32)
                k1, k2 = keeps[g1][b], keeps[g2][b]
                run(g1 * 2 + b)[:WIDTH, :] = prod[:WIDTH] + one[:WIDTH] * k2 + two[:WIDTH] * k1
                run(g1 * 2 + b)[WIDTH:, :] = prod[WIDTH:] + one[WIDTH:] * k2 + two[WIDTH:]
                keeps[g1][b] = k1 * k2
        stride *= 2
    for b in range(2):
        pack_map(send_ref, b, run(b)[:WIDTH, :], run(b)[WIDTH : WIDTH + 1, :], keeps[0][b])


def compose(place, noise, retain, control_weight, input_weight):
    steps = noise.shape[1]
    return pl.pallas_call(
        compose_kernel,
        out_shape=(
            pltpu.VMEM((SPAN, 2 * GROUPS, WIDTH, WIDTH), BF16),
            pltpu.VMEM((2 * steps, WIDTH), F32),
            pltpu.VMEM((2, MAP_ROWS, WIDTH), BF16),
            pltpu.VMEM((2 * GROUPS, WIDTH, WIDTH), BF16),
            jax.ShapeDtypeStruct((GROUPS, 2), F32),
        ),
        in_specs=[SMEM, VMEM, SMEM, VMEM, ANY, VMEM],
        out_specs=(VMEM, VMEM, VMEM, VMEM, SMEM),
        scratch_shapes=[
            pltpu.VMEM((128 * PITCH + 8, WIDTH), F32),
            pltpu.VMEM((2 * steps * PITCH + 8, WIDTH), F32),
            pltpu.SemaphoreType.DMA((4,)),
        ],
        compiler_params=pltpu.CompilerParams(vmem_limit_bytes=44_500_000),
        name="compose",
    )(place, noise, retain, retain, control_weight.reshape(-1, WIDTH, WIDTH), input_weight)


def row_kernel(place_s, m0, m1, m2, m3, out_ref, held):
    x = place_s[1]
    for k, ref in enumerate((m0, m1, m2, m3)):
        held[lax.rem(x + 4 - k, 4)] = ref[...]
    for b in range(2):
        parts = []
        for k in range(4):
            matrix, offset, kept = unpack_map(held.at[k], b)
            parts.append((matrix.astype(F32), offset, kept))
        while len(parts) > 1:
            merged = []
            for (m1_, o1, k1), (m2_, o2, k2) in zip(parts[::2], parts[1::2]):
                low = m2_.astype(BF16)
                prod = jnp.dot(m1_.astype(BF16), low, preferred_element_type=F32)
                merged.append((prod + m1_ * k2 + m2_ * k1, row_times(o1, low) + o1 * k2 + o2, k1 * k2))
            parts = merged
        pack_map(out_ref, b, *parts[0])


def row_map(place, maps):
    return pl.pallas_call(
        row_kernel,
        out_shape=jax.ShapeDtypeStruct((2, MAP_ROWS, WIDTH), BF16),
        in_specs=[SMEM] + [VMEM] * 4,
        out_specs=VMEM,
        scratch_shapes=[pltpu.VMEM((4, 2, MAP_ROWS, WIDTH), BF16)],
        compiler_params=pltpu.CompilerParams(vmem_limit_bytes=8_000_000),
        name="row_map",
    )(place, *maps)


def replay_kernel(place_s, kept_s, init_ref, y1, y2, y3, x1, x2, x3, off_ref, grp_ref, gain_ref, q_ref,
                  states_ref, normed_ref):
    steps = SPAN * GROUPS
    entry = []
    for b in range(2):
        h = init_ref[b : b + 1, :]
        for place, refs in ((place_s[0], (y1, y2, y3)), (place_s[1], (x1, x2, x3))):
            for k in (3, 2, 1):
                matrix, offset, kept = unpack_map(refs[k - 1], b)
                h = jnp.where(k <= place, h * kept + row_times(h, matrix) + offset, h)
        entry.append(h)

    def group(g, starts):
        after = []
        for b in range(2):
            c = g * 2 + b
            h = starts[b]
            spread = jnp.broadcast_to(h, (WIDTH, WIDTH)).T
            last = off_ref[pl.ds(b * steps + g * SPAN + SPAN - 1, 1), :]
            after.append(h * kept_s[g, b] + row_times(h, grp_ref[c]) + last)
            rows = [jnp.sum(q_ref[s, c].astype(F32) * spread, axis=0, keepdims=True) for s in range(SPAN)]
            base = pl.multiple_of(g * SPAN, SPAN)
            states = jnp.concatenate(rows, axis=0) + off_ref[pl.ds(b * steps + base, SPAN), :]
            states_ref[pl.ds(base, SPAN), b * WIDTH : (b + 1) * WIDTH] = states
            mean = jnp.mean(states * states, axis=-1, keepdims=True)
            normed = states * lax.rsqrt(mean + 1e-05) * gain_ref[b : b + 1, :]
            normed_ref[pl.ds(base, SPAN), b * WIDTH : (b + 1) * WIDTH] = normed.astype(BF16)
        return tuple(after)

    lax.fori_loop(0, GROUPS, group, tuple(entry), unroll=2)


def replay(place, kept, init, y_maps, x_maps, off, grp, gain, q):
    steps = SPAN * GROUPS
    return pl.pallas_call(
        replay_kernel,
        out_shape=(
            jax.ShapeDtypeStruct((steps, 2 * WIDTH), F32),
            jax.ShapeDtypeStruct((steps, 2 * WIDTH), BF16),
        ),
        in_specs=[SMEM, SMEM] + [VMEM] * 11,
        out_specs=(VMEM, VMEM),
        compiler_params=pltpu.CompilerParams(vmem_limit_bytes=16_000_000),
        name="replay",
    )(place, kept, init, *y_maps, *x_maps, off, grp, gain, pltpu.with_memory_space_constraint(q, pltpu.VMEM))


def forward_kernel(place_s, m0, m1, m2, m3, theirs_ref, gate_ref, up_ref, down_ref, keep_ref, send_ref, hidden):
    z, core = place_s[2], place_s[3]
    wide = 2 * WIDTH

    def at(k, c):
        return pl.multiple_of((lax.rem(z + k, 4) * 2 + c) * wide, wide)

    parts = [(m0, 0, 0), (m1, 3, 0), (m2, 2, 0), (m3, 1, 0)]
    parts += [(theirs_ref.at[k], (4 - k) % 4, 1) for k in range(4)]
    for n in range(0, gate_ref.shape[1], wide):
        gate = up = None
        for ref, k, other in parts:
            chunk = ref[...]
            row = at(k, 1 - core if other else core)
            g = jnp.dot(chunk, gate_ref[pl.ds(row, wide), n : n + wide], preferred_element_type=F32)
            u = jnp.dot(chunk, up_ref[pl.ds(row, wide), n : n + wide], preferred_element_type=F32)
            gate = g if gate is None else gate + g
            up = u if up is None else up + u
        hidden[:, n : n + wide] = (gate / (1.0 + jnp.exp(-gate)) * up).astype(BF16)
    low = hidden[...]
    for ref, c in ((send_ref, 1 - core), (keep_ref, core)):
        for k in range(4):
            out = jnp.dot(low, down_ref[:, pl.ds(at(k, c), wide)], preferred_element_type=F32)
            ref[k] = out.astype(BF16)


def forward(place, mine, theirs, gate_weight, up_weight, down_weight):
    steps = mine[0].shape[0]
    weights = [pltpu.with_memory_space_constraint(w, pltpu.VMEM) for w in (gate_weight, up_weight, down_weight)]
    half = jax.ShapeDtypeStruct((4, steps, 2 * WIDTH), BF16)
    return pl.pallas_call(
        forward_kernel,
        out_shape=(half, half),
        in_specs=[SMEM] + [VMEM] * 8,
        out_specs=(VMEM, VMEM),
        scratch_shapes=[pltpu.VMEM((steps, gate_weight.shape[1]), BF16)],
        compiler_params=pltpu.CompilerParams(vmem_limit_bytes=16_000_000),
        name="forward",
    )(place, *mine, theirs, *weights)


def x_back(v, k):
    return lax.ppermute(v, "tm", [(y * 4 + x, y * 4 + (x + k) % 4) for y in range(4) for x in range(4)])


def y_back(v, k):
    return lax.ppermute(v, "tm", [(y * 4 + x, (y + k) % 4 * 4 + x) for y in range(4) for x in range(4)])


def z_back(v, k):
    return lax.ppermute(v, "block", [(z * 2 + c, (z + k) % 4 * 2 + c) for z in range(4) for c in range(2)])


def other_core(v):
    return lax.ppermute(v, "block", [(s, s ^ 1) for s in range(8)])


def body(
    noise,
    retain,
    control_weight,
    input_weight,
    initial_state,
    norm_gain,
    gate_weight,
    up_weight,
    down_weight,
):
    tm = lax.axis_index("tm")
    block = lax.axis_index("block")
    z, core = block // 2, block % 2
    place = jnp.stack([tm // 4, tm % 4, z, core]).astype(jnp.int32)
    q, off, own, grp, kept = compose(place, noise.T, retain.T, control_weight, input_weight)
    x_maps = [x_back(own, k) for k in (1, 2, 3)]
    total = row_map(place, [own, *x_maps])
    y_maps = [y_back(total, k) for k in (1, 2, 3)]
    states, normed = replay(
        place, kept, initial_state.reshape(2, WIDTH), y_maps, x_maps, off, grp, norm_gain.reshape(2, WIDTH), q
    )
    mine = [normed] + [z_back(normed, k) for k in (1, 2, 3)]
    theirs = other_core(jnp.stack(mine))
    keep, sent = forward(place, mine, theirs, gate_weight, up_weight, down_weight)
    chip = keep.astype(F32) + other_core(sent).astype(F32)
    low = chip.astype(BF16)
    mixed = chip[0]
    for k in (1, 2, 3):
        mixed = mixed + z_back(low[k], k).astype(F32)
    return (states + mixed).astype(BF16)


def solution(mesh):
    placed = (
        P("tm", None),
        P("tm", "block"),
        P(None, "block", None, None),
        P(None, "block"),
        P("block"),
        P("block"),
        P(None, "block"),
        P(None, "block"),
        P("block", None),
    )
    return jax.shard_map(body, mesh=mesh, in_specs=placed, out_specs=P("tm", "block"), check_vma=False)
```

```python
import functools
import math

import jax
import jax.numpy as jnp
from jax import lax
from jax.experimental import pallas as pl
from jax.experimental.pallas import tpu as pltpu
from jax.sharding import PartitionSpec as P

F32 = jnp.float32
BF16 = jnp.bfloat16
GROUPS = 16
SPAN = 16
WIDTH = 128
ROWS = 144
PITCH = 129
MAP_ROWS = 144
VMEM = pl.BlockSpec(memory_space=pltpu.VMEM)
SMEM = pl.BlockSpec(memory_space=pltpu.SMEM)
ANY = pl.BlockSpec(memory_space=pl.ANY)


def split3(v):
    hi = v.astype(BF16)
    rest = v - hi.astype(F32)
    mid = rest.astype(BF16)
    return hi, mid, (rest - mid.astype(F32)).astype(BF16)


def pack_map(ref, b, matrix, offset, kept):
    ref[b, :WIDTH, :] = matrix.astype(BF16)
    row = lax.broadcasted_iota(jnp.int32, (16, WIDTH), 0)
    tail = jnp.zeros((16, WIDTH), F32)
    kept_row = jnp.full((1, WIDTH), 1.0, F32) * kept
    for k, part in enumerate((*split3(offset), *split3(kept_row))):
        tail = jnp.where(row == k, jnp.broadcast_to(part.astype(F32), (16, WIDTH)), tail)
    ref[b, WIDTH:, :] = tail.astype(BF16)


def unpack_map(ref, b):
    matrix = ref[b, :WIDTH, :]
    tail = ref[b, WIDTH:, :].astype(F32)
    offset = tail[0:1] + tail[1:2] + tail[2:3]
    kept = tail[3:4] + tail[4:5] + tail[5:6]
    return matrix, offset, kept


def row_times(h, matrix):
    row = lax.broadcasted_iota(jnp.int32, (16, WIDTH), 0)
    hi = h.astype(BF16).astype(F32)
    lo = h - hi
    both = jnp.where(row == 0, jnp.broadcast_to(hi, (16, WIDTH)), jnp.broadcast_to(lo, (16, WIDTH)))
    out = jnp.dot(both.astype(BF16), matrix, preferred_element_type=F32)
    return out[0:1] + out[1:2]


def compose_kernel(
    place_s, noise_ref, retain_s, retain_ref, cw_ref, iw_ref, q_ref, off_ref, send_ref, grp_ref, kept_ref, skw, am, sem
):
    steps = noise_ref.shape[1]
    loads = [
        pltpu.make_async_copy(cw_ref.at[pl.ds(32 * k, 32)], q_ref.at[k], sem.at[k]) for k in range(4)
    ]
    for load in loads:
        load.start()
    rows = lax.broadcasted_iota(jnp.int32, (WIDTH, WIDTH), 0)
    cols = lax.broadcasted_iota(jnp.int32, (WIDTH, WIDTH), 1)
    eye = (rows == cols).astype(F32)
    noise = noise_ref[...].T
    drive = jnp.dot(noise, iw_ref[...], precision=lax.Precision.HIGHEST, preferred_element_type=F32)
    kept = retain_ref[...]
    scale = jnp.sqrt(1.0 - kept * kept)
    for b in range(2):
        spread = jnp.broadcast_to(scale[b : b + 1, :], (WIDTH, steps)).T
        off_ref[b * steps : (b + 1) * steps, :] = drive[:, b * WIDTH : (b + 1) * WIDTH] * spread

    def skew_body(base, i, carry):
        for b in range(2):
            raw = q_ref[base // 16, i * 2 + b]
            diff = (raw.T.astype(F32) - raw.astype(F32)) * (1.0 / math.sqrt(2.0))
            skw[pl.ds((b * 64 + base + i) * PITCH, WIDTH), :] = diff.astype(BF16).astype(F32)
        return carry

    for k in range(4):
        loads[k].wait()
        lax.fori_loop(0, 16, functools.partial(skew_body, 16 * k), 0, unroll=8)
    low = (noise.astype(BF16).astype(F32) * (1.0 / 64.0)).astype(BF16)

    def build_body(j, carry):
        w = jnp.concatenate(
            [skw[pl.ds(b * 64 * PITCH + j, 64, stride=PITCH), :] for b in range(2)], axis=1
        ).astype(BF16)
        out = jnp.dot(low, w, preferred_element_type=F32)
        for b in range(2):
            am[pl.ds(b * steps * PITCH + j, steps, stride=PITCH), :] = out[:, b * WIDTH : (b + 1) * WIDTH]
        return carry

    lax.fori_loop(0, WIDTH, build_body, 0, unroll=16)
    tail_rows = ROWS - WIDTH
    tail_row = lax.broadcasted_iota(jnp.int32, (tail_rows, WIDTH), 0)
    zero = jnp.zeros((WIDTH, WIDTH), BF16)

    def run(c):
        return skw.at[pl.ds(pl.multiple_of(c * ROWS, 16), ROWS), :]

    def step_matrix(t, b):
        return am[pl.ds((b * steps + t) * PITCH, WIDTH), :]

    def finish(s, g, b, matrix, tail):
        t = g * SPAN + s
        c = g * 2 + b
        rate = retain_s[b, t]
        push = off_ref[pl.ds(b * steps + t, 1), :]
        matrix = matrix * rate
        placed = jnp.where(tail_row == 0, jnp.broadcast_to(push, (tail_rows, WIDTH)), 0.0)
        tail = placed if tail is None else tail * rate + placed
        run(c)[:WIDTH, :] = matrix
        run(c)[WIDTH:, :] = tail
        q_ref[s, c] = matrix.astype(BF16)
        off_ref[pl.ds(b * steps + t, 1), :] = tail[:1]
        return rate

    def first(g, carry):
        for b in range(2):
            kept_ref[g, b] = finish(0, g, b, eye + step_matrix(g * SPAN, b), None)
        return carry

    lax.fori_loop(0, GROUPS, first, 0, unroll=4)

    def step(s, carry):
        def group(g, inner):
            t = g * SPAN + s
            now = [run(g * 2 + b)[...] for b in range(2)]
            low0, low1 = [step_matrix(t, b).astype(BF16) for b in range(2)]
            w = jnp.concatenate(
                [jnp.concatenate([low0, zero], axis=1), jnp.concatenate([zero, low1], axis=1)], axis=0
            )
            both = jnp.concatenate([x.astype(BF16) for x in now], axis=1)
            turned = jnp.dot(both, w, preferred_element_type=F32)
            for b in range(2):
                y = now[b] + turned[:, b * WIDTH : (b + 1) * WIDTH]
                rate = finish(s, g, b, y[:WIDTH], y[WIDTH:])
                kept_ref[g, b] = kept_ref[g, b] * rate
            return inner

        lax.fori_loop(0, GROUPS, group, 0, unroll=16)
        return carry

    lax.fori_loop(1, SPAN, step, 0)

    keeps = [[kept_ref[g, b] for b in range(2)] for g in range(GROUPS)]
    for g in range(GROUPS):
        for b in range(2):
            c = g * 2 + b
            m = run(c)[:WIDTH, :] - eye * keeps[g][b]
            run(c)[:WIDTH, :] = m
            grp_ref[c] = m.astype(BF16)
    stride = 1
    while stride < GROUPS:
        for g1 in range(0, GROUPS, 2 * stride):
            g2 = g1 + stride
            for b in range(2):
                one, two = run(g1 * 2 + b)[...], run(g2 * 2 + b)[...]
                prod = jnp.dot(one.astype(BF16), two[:WIDTH].astype(BF16), preferred_element_type=F32)
                k1, k2 = keeps[g1][b], keeps[g2][b]
                run(g1 * 2 + b)[:WIDTH, :] = prod[:WIDTH] + one[:WIDTH] * k2 + two[:WIDTH] * k1
                run(g1 * 2 + b)[WIDTH:, :] = prod[WIDTH:] + one[WIDTH:] * k2 + two[WIDTH:]
                keeps[g1][b] = k1 * k2
        stride *= 2
    for b in range(2):
        pack_map(send_ref, b, run(b)[:WIDTH, :], run(b)[WIDTH : WIDTH + 1, :], keeps[0][b])


def compose(place, noise, retain, control_weight, input_weight):
    steps = noise.shape[1]
    return pl.pallas_call(
        compose_kernel,
        out_shape=(
            pltpu.VMEM((SPAN, 2 * GROUPS, WIDTH, WIDTH), BF16),
            pltpu.VMEM((2 * steps, WIDTH), F32),
            pltpu.VMEM((2, MAP_ROWS, WIDTH), BF16),
            pltpu.VMEM((2 * GROUPS, WIDTH, WIDTH), BF16),
            jax.ShapeDtypeStruct((GROUPS, 2), F32),
        ),
        in_specs=[SMEM, VMEM, SMEM, VMEM, ANY, VMEM],
        out_specs=(VMEM, VMEM, VMEM, VMEM, SMEM),
        scratch_shapes=[
            pltpu.VMEM((128 * PITCH + 8, WIDTH), F32),
            pltpu.VMEM((2 * steps * PITCH + 8, WIDTH), F32),
            pltpu.SemaphoreType.DMA((4,)),
        ],
        compiler_params=pltpu.CompilerParams(vmem_limit_bytes=44_500_000),
        name="compose",
    )(place, noise, retain, retain, control_weight.reshape(-1, WIDTH, WIDTH), input_weight)


def order(held, refs, place, sign):
    for k, ref in enumerate(refs):
        held[lax.rem(place + 4 - k * sign, 4)] = ref[...]


def row_kernel(place_s, m0, m1, m2, m3, out_ref, held):
    order(held, (m0, m1, m2, m3), place_s[1], 1 - 2 * place_s[3])
    for b in range(2):
        parts = []
        for k in range(4):
            matrix, offset, kept = unpack_map(held.at[k], b)
            parts.append((matrix.astype(F32), offset, kept))
        while len(parts) > 1:
            merged = []
            for (m1_, o1, k1), (m2_, o2, k2) in zip(parts[::2], parts[1::2]):
                low = m2_.astype(BF16)
                prod = jnp.dot(m1_.astype(BF16), low, preferred_element_type=F32)
                merged.append((prod + m1_ * k2 + m2_ * k1, row_times(o1, low) + o1 * k2 + o2, k1 * k2))
            parts = merged
        pack_map(out_ref, b, *parts[0])


def row_map(place, maps):
    return pl.pallas_call(
        row_kernel,
        out_shape=(
            jax.ShapeDtypeStruct((2, MAP_ROWS, WIDTH), BF16),
            jax.ShapeDtypeStruct((4, 2, MAP_ROWS, WIDTH), BF16),
        ),
        in_specs=[SMEM] + [VMEM] * 4,
        out_specs=(VMEM, VMEM),
        compiler_params=pltpu.CompilerParams(vmem_limit_bytes=8_000_000),
        name="row_map",
    )(place, *maps)


def replay_kernel(place_s, kept_s, init_ref, y0, y1, y2, y3, row_ref, off_ref, grp_ref, gain_ref, q_ref,
                  states_ref, normed_ref, held):
    steps = SPAN * GROUPS
    order(held, (y0, y1, y2, y3), place_s[0], 1 - 2 * place_s[3])
    entry = []
    for b in range(2):
        h = init_ref[b : b + 1, :]
        for place, maps in ((place_s[0], held), (place_s[1], row_ref)):
            for k in range(3):
                matrix, offset, kept = unpack_map(maps.at[k], b)
                h = jnp.where(k < place, h * kept + row_times(h, matrix) + offset, h)
        entry.append(h)

    def group(g, starts):
        after = []
        for b in range(2):
            c = g * 2 + b
            h = starts[b]
            spread = jnp.broadcast_to(h, (WIDTH, WIDTH)).T
            last = off_ref[pl.ds(b * steps + g * SPAN + SPAN - 1, 1), :]
            after.append(h * kept_s[g, b] + row_times(h, grp_ref[c]) + last)
            rows = [jnp.sum(q_ref[s, c].astype(F32) * spread, axis=0, keepdims=True) for s in range(SPAN)]
            base = pl.multiple_of(g * SPAN, SPAN)
            states = jnp.concatenate(rows, axis=0) + off_ref[pl.ds(b * steps + base, SPAN), :]
            states_ref[pl.ds(base, SPAN), b * WIDTH : (b + 1) * WIDTH] = states
            mean = jnp.mean(states * states, axis=-1, keepdims=True)
            normed = states * lax.rsqrt(mean + 1e-05) * gain_ref[b : b + 1, :]
            normed_ref[pl.ds(base, SPAN), b * WIDTH : (b + 1) * WIDTH] = normed.astype(BF16)
        return tuple(after)

    lax.fori_loop(0, GROUPS, group, tuple(entry), unroll=2)


def replay(place, kept, init, y_maps, row, off, grp, gain, q):
    steps = SPAN * GROUPS
    return pl.pallas_call(
        replay_kernel,
        out_shape=(
            jax.ShapeDtypeStruct((steps, 2 * WIDTH), F32),
            jax.ShapeDtypeStruct((steps, 2 * WIDTH), BF16),
        ),
        in_specs=[SMEM, SMEM] + [VMEM] * 10,
        out_specs=(VMEM, VMEM),
        scratch_shapes=[pltpu.VMEM((4, 2, MAP_ROWS, WIDTH), BF16)],
        compiler_params=pltpu.CompilerParams(vmem_limit_bytes=16_000_000),
        name="replay",
    )(place, kept, init, *y_maps, row, off, grp, gain, pltpu.with_memory_space_constraint(q, pltpu.VMEM))


def forward_kernel(place_s, m0, m1, m2, m3, theirs_ref, gate_ref, up_ref, down_ref, keep_ref, send_ref, hidden):
    z, core = place_s[2], place_s[3]
    sign = 1 - 2 * core
    wide = 2 * WIDTH

    def at(k, c):
        return pl.multiple_of((lax.rem(z + 4 + k, 4) * 2 + c) * wide, wide)

    parts = [(ref, at(-k * sign, core)) for k, ref in enumerate((m0, m1, m2, m3))]
    parts += [(theirs_ref.at[k], at(k * sign, 1 - core)) for k in range(4)]
    for n in range(0, gate_ref.shape[1], wide):
        gate = up = None
        for ref, row in parts:
            chunk = ref[...]
            g = jnp.dot(chunk, gate_ref[pl.ds(row, wide), n : n + wide], preferred_element_type=F32)
            u = jnp.dot(chunk, up_ref[pl.ds(row, wide), n : n + wide], preferred_element_type=F32)
            gate = g if gate is None else gate + g
            up = u if up is None else up + u
        hidden[:, n : n + wide] = (gate / (1.0 + jnp.exp(-gate)) * up).astype(BF16)
    low = hidden[...]
    for ref, c, ahead in ((send_ref, 1 - core, -sign), (keep_ref, core, sign)):
        for k in range(4):
            out = jnp.dot(low, down_ref[:, pl.ds(at(k * ahead, c), wide)], preferred_element_type=F32)
            ref[k] = out.astype(BF16)


def forward(place, mine, theirs, gate_weight, up_weight, down_weight):
    steps = mine[0].shape[0]
    weights = [pltpu.with_memory_space_constraint(w, pltpu.VMEM) for w in (gate_weight, up_weight, down_weight)]
    half = jax.ShapeDtypeStruct((4, steps, 2 * WIDTH), BF16)
    return pl.pallas_call(
        forward_kernel,
        out_shape=(half, half),
        in_specs=[SMEM] + [VMEM] * 8,
        out_specs=(VMEM, VMEM),
        scratch_shapes=[pltpu.VMEM((steps, gate_weight.shape[1]), BF16)],
        compiler_params=pltpu.CompilerParams(vmem_limit_bytes=16_000_000),
        name="forward",
    )(place, *mine, theirs, *weights)


def along(v, axis, way):
    pairs = []
    for source in range(128):
        at = [source // 32, source // 8 % 4, source // 2 % 4, source % 2]
        at[axis] = (at[axis] + way * (1 - 2 * at[3])) % 4
        pairs.append((source, at[0] * 32 + at[1] * 8 + at[2] * 2 + at[3]))
    return lax.ppermute(v, ("tm", "block"), pairs)


def gather(v, axis):
    one = along(v, axis, 1)
    three = along(v, axis, -1)
    return [v, one, along(one, axis, 1), three]


def other_core(v):
    return lax.ppermute(v, "block", [(s, s ^ 1) for s in range(8)])


def body(
    noise,
    retain,
    control_weight,
    input_weight,
    initial_state,
    norm_gain,
    gate_weight,
    up_weight,
    down_weight,
):
    tm = lax.axis_index("tm")
    block = lax.axis_index("block")
    z, core = block // 2, block % 2
    place = jnp.stack([tm // 4, tm % 4, z, core]).astype(jnp.int32)
    q, off, own, grp, kept = compose(place, noise.T, retain.T, control_weight, input_weight)
    total, row = row_map(place, gather(own, 1))
    states, normed = replay(
        place, kept, initial_state.reshape(2, WIDTH), gather(total, 0), row, off, grp, norm_gain.reshape(2, WIDTH), q
    )
    mine = gather(normed, 2)
    theirs = other_core(jnp.stack(mine))
    keep, sent = forward(place, mine, theirs, gate_weight, up_weight, down_weight)
    chip = keep.astype(F32) + other_core(sent).astype(F32)
    two = along(chip[2].astype(BF16), 2, 1)
    three = along(chip[3].astype(BF16), 2, -1)
    one = along((chip[1] + two.astype(F32)).astype(BF16), 2, 1)
    return (states + (chip[0] + three.astype(F32) + one.astype(F32))).astype(BF16)


def solution(mesh):
    placed = (
        P("tm", None),
        P("tm", "block"),
        P(None, "block", None, None),
        P(None, "block"),
        P("block"),
        P("block"),
        P(None, "block"),
        P(None, "block"),
        P("block", None),
    )
    return jax.shard_map(body, mesh=mesh, in_specs=placed, out_specs=P("tm", "block"), check_vma=False)
```

```python
import functools
import math

import jax
import jax.numpy as jnp
from jax import lax
from jax.experimental import pallas as pl
from jax.experimental.pallas import tpu as pltpu
from jax.sharding import PartitionSpec as P

F32 = jnp.float32
BF16 = jnp.bfloat16
GROUPS = 16
SPAN = 16
WIDTH = 128
ROWS = 144
PITCH = 129
MAP_ROWS = 144
VMEM = pl.BlockSpec(memory_space=pltpu.VMEM)
SMEM = pl.BlockSpec(memory_space=pltpu.SMEM)
ANY = pl.BlockSpec(memory_space=pl.ANY)


def split3(v):
    hi = v.astype(BF16)
    rest = v - hi.astype(F32)
    mid = rest.astype(BF16)
    return hi, mid, (rest - mid.astype(F32)).astype(BF16)


def pack_map(ref, b, matrix, offset, kept):
    ref[b, :WIDTH, :] = matrix.astype(BF16)
    row = lax.broadcasted_iota(jnp.int32, (16, WIDTH), 0)
    tail = jnp.zeros((16, WIDTH), F32)
    kept_row = jnp.full((1, WIDTH), 1.0, F32) * kept
    for k, part in enumerate((*split3(offset), *split3(kept_row))):
        tail = jnp.where(row == k, jnp.broadcast_to(part.astype(F32), (16, WIDTH)), tail)
    ref[b, WIDTH:, :] = tail.astype(BF16)


def unpack_map(ref, b):
    matrix = ref[b, :WIDTH, :]
    tail = ref[b, WIDTH:, :].astype(F32)
    offset = tail[0:1] + tail[1:2] + tail[2:3]
    kept = tail[3:4] + tail[4:5] + tail[5:6]
    return matrix, offset, kept


def two_parts(h):
    row = lax.broadcasted_iota(jnp.int32, (16, WIDTH), 0)
    hi = h.astype(BF16).astype(F32)
    lo = h - hi
    return jnp.where(
        row == 0, jnp.broadcast_to(hi, (16, WIDTH)), jnp.broadcast_to(lo, (16, WIDTH))
    ).astype(BF16)


def parts_times(parts, matrix):
    out = jnp.dot(parts, matrix, preferred_element_type=F32)
    return out[0:1] + out[1:2]


def row_times(h, matrix):
    return parts_times(two_parts(h), matrix)


def places():
    tm, block = lax.axis_index("tm"), lax.axis_index("block")
    return lax.div(tm, 4), lax.rem(tm, 4), lax.div(block, 2), lax.rem(block, 2)


def compose_kernel(
    noise_ref, retain_s, retain_ref, cw_ref, iw_ref, q_ref, off_ref, send_ref, grp_ref, kept_ref, skw, am, kept_s, sem
):
    steps = noise_ref.shape[1]
    loads = [
        pltpu.make_async_copy(cw_ref.at[pl.ds(32 * k, 32)], q_ref.at[k], sem.at[k]) for k in range(4)
    ]
    for load in loads:
        load.start()
    rows = lax.broadcasted_iota(jnp.int32, (WIDTH, WIDTH), 0)
    cols = lax.broadcasted_iota(jnp.int32, (WIDTH, WIDTH), 1)
    eye = (rows == cols).astype(F32)
    noise = noise_ref[...].T
    drive = jnp.dot(noise, iw_ref[...], precision=lax.Precision.HIGHEST, preferred_element_type=F32)
    kept = retain_ref[...]
    scale = jnp.sqrt(1.0 - kept * kept)
    for b in range(2):
        spread = jnp.broadcast_to(scale[b : b + 1, :], (WIDTH, steps)).T
        off_ref[b * steps : (b + 1) * steps, :] = drive[:, b * WIDTH : (b + 1) * WIDTH] * spread

    def skew_body(base, i, carry):
        for b in range(2):
            raw = q_ref[base // 16, i * 2 + b]
            diff = (raw.T.astype(F32) - raw.astype(F32)) * (1.0 / math.sqrt(2.0))
            skw[pl.ds((b * 64 + base + i) * PITCH, WIDTH), :] = diff
        return carry

    for k in range(4):
        loads[k].wait()
        lax.fori_loop(0, 16, functools.partial(skew_body, 16 * k), 0, unroll=8)
    low = (noise.astype(BF16).astype(F32) * (1.0 / 64.0)).astype(BF16)

    def build_body(j, carry):
        w = jnp.concatenate(
            [skw[pl.ds(b * 64 * PITCH + j, 64, stride=PITCH), :] for b in range(2)], axis=1
        ).astype(BF16)
        out = jnp.dot(low, w, preferred_element_type=F32)
        for b in range(2):
            am[pl.ds(b * steps * PITCH + j, steps, stride=PITCH), :] = out[:, b * WIDTH : (b + 1) * WIDTH]
        return carry

    lax.fori_loop(0, WIDTH, build_body, 0, unroll=16)
    tail_rows = ROWS - WIDTH
    tail_row = lax.broadcasted_iota(jnp.int32, (tail_rows, WIDTH), 0)
    zero = jnp.zeros((WIDTH, WIDTH), BF16)

    def run(c):
        return skw.at[pl.ds(pl.multiple_of(c * ROWS, 16), ROWS), :]

    def step_matrix(t, b):
        return am[pl.ds((b * steps + t) * PITCH, WIDTH), :]

    def finish(s, g, b, matrix, tail):
        t = g * SPAN + s
        c = g * 2 + b
        rate = retain_s[b, t]
        push = off_ref[pl.ds(b * steps + t, 1), :]
        matrix = matrix * rate
        placed = jnp.where(tail_row == 0, jnp.broadcast_to(push, (tail_rows, WIDTH)), 0.0)
        tail = placed if tail is None else tail * rate + placed
        run(c)[:WIDTH, :] = matrix
        run(c)[WIDTH:, :] = tail
        q_ref[s, c] = matrix.astype(BF16)
        off_ref[pl.ds(b * steps + t, 1), :] = tail[:1]
        return rate

    def first(g, carry):
        for b in range(2):
            kept_s[g, b] = finish(0, g, b, eye + step_matrix(g * SPAN, b), None)
        return carry

    lax.fori_loop(0, GROUPS, first, 0, unroll=4)

    def step(s, carry):
        def group(g, inner):
            t = g * SPAN + s
            now = [run(g * 2 + b)[...] for b in range(2)]
            low0, low1 = [step_matrix(t, b).astype(BF16) for b in range(2)]
            w = jnp.concatenate(
                [jnp.concatenate([low0, zero], axis=1), jnp.concatenate([zero, low1], axis=1)], axis=0
            )
            both = jnp.concatenate([x.astype(BF16) for x in now], axis=1)
            turned = jnp.dot(both, w, preferred_element_type=F32)
            for b in range(2):
                y = now[b] + turned[:, b * WIDTH : (b + 1) * WIDTH]
                rate = finish(s, g, b, y[:WIDTH], y[WIDTH:])
                kept_s[g, b] = kept_s[g, b] * rate
            return inner

        lax.fori_loop(0, GROUPS, group, 0, unroll=16)
        return carry

    lax.fori_loop(1, SPAN, step, 0)

    keeps = [[kept_s[g, b] for b in range(2)] for g in range(GROUPS)]
    for g in range(GROUPS):
        for b in range(2):
            c = g * 2 + b
            m = run(c)[:WIDTH, :] - eye * keeps[g][b]
            run(c)[:WIDTH, :] = m
            grp_ref[c] = m.astype(BF16)
            kept_ref[c : c + 1, :] = jnp.full((1, WIDTH), 1.0, F32) * keeps[g][b]
    stride = 1
    while stride < GROUPS:
        for g1 in range(0, GROUPS, 2 * stride):
            g2 = g1 + stride
            for b in range(2):
                one, two = run(g1 * 2 + b)[...], run(g2 * 2 + b)[...]
                prod = jnp.dot(one.astype(BF16), two[:WIDTH].astype(BF16), preferred_element_type=F32)
                k1, k2 = keeps[g1][b], keeps[g2][b]
                run(g1 * 2 + b)[:WIDTH, :] = prod[:WIDTH] + one[:WIDTH] * k2 + two[:WIDTH] * k1
                run(g1 * 2 + b)[WIDTH:, :] = prod[WIDTH:] + one[WIDTH:] * k2 + two[WIDTH:]
                keeps[g1][b] = k1 * k2
        stride *= 2
    for b in range(2):
        pack_map(send_ref, b, run(b)[:WIDTH, :], run(b)[WIDTH : WIDTH + 1, :], keeps[0][b])


def compose(noise, retain, control_weight, input_weight):
    steps = noise.shape[1]
    return pl.pallas_call(
        compose_kernel,
        out_shape=(
            pltpu.VMEM((SPAN, 2 * GROUPS, WIDTH, WIDTH), BF16),
            pltpu.VMEM((2 * steps, WIDTH), F32),
            pltpu.VMEM((2, MAP_ROWS, WIDTH), BF16),
            pltpu.VMEM((2 * GROUPS, WIDTH, WIDTH), BF16),
            pltpu.VMEM((2 * GROUPS, WIDTH), F32),
        ),
        in_specs=[VMEM, SMEM, VMEM, ANY, VMEM],
        out_specs=(VMEM, VMEM, VMEM, VMEM, VMEM),
        scratch_shapes=[
            pltpu.VMEM((128 * PITCH + 8, WIDTH), F32),
            pltpu.VMEM((2 * steps * PITCH + 8, WIDTH), F32),
            pltpu.SMEM((GROUPS, 2), F32),
            pltpu.SemaphoreType.DMA((4,)),
        ],
        compiler_params=pltpu.CompilerParams(vmem_limit_bytes=44_500_000),
        name="compose",
    )(noise, retain, retain, control_weight.reshape(-1, WIDTH, WIDTH), input_weight)


def row_kernel(m0, m1, m2, m3, out_ref, held):
    x = places()[1]
    for k, ref in enumerate((m0, m1, m2, m3)):
        held[lax.rem(x + 4 - k, 4)] = ref[...]
    for b in range(2):
        parts = []
        for k in range(4):
            matrix, offset, kept = unpack_map(held.at[k], b)
            parts.append((matrix.astype(F32), offset, kept))
        while len(parts) > 1:
            merged = []
            for (m1_, o1, k1), (m2_, o2, k2) in zip(parts[::2], parts[1::2]):
                low = m2_.astype(BF16)
                prod = jnp.dot(m1_.astype(BF16), low, preferred_element_type=F32)
                merged.append((prod + m1_ * k2 + m2_ * k1, row_times(o1, low) + o1 * k2 + o2, k1 * k2))
            parts = merged
        pack_map(out_ref, b, *parts[0])


def row_map(maps):
    return pl.pallas_call(
        row_kernel,
        out_shape=jax.ShapeDtypeStruct((2, MAP_ROWS, WIDTH), BF16),
        in_specs=[VMEM] * 4,
        out_specs=VMEM,
        scratch_shapes=[pltpu.VMEM((4, 2, MAP_ROWS, WIDTH), BF16)],
        compiler_params=pltpu.CompilerParams(vmem_limit_bytes=8_000_000),
        name="row_map",
    )(*maps)


def replay_kernel(kept_ref, init_ref, y1, y2, y3, x1, x2, x3, off_ref, grp_ref, gain_ref, q_ref,
                  states_ref, normed_ref):
    steps = SPAN * GROUPS
    y, x = places()[:2]
    entry = []
    for b in range(2):
        h = init_ref[b : b + 1, :]
        for place, refs in ((y, (y1, y2, y3)), (x, (x1, x2, x3))):
            for k in (3, 2, 1):
                matrix, offset, kept = unpack_map(refs[k - 1], b)
                h = jnp.where(k <= place, h * kept + row_times(h, matrix) + offset, h)
        entry.append(h)

    def group(g, starts):
        after = []
        for b in range(2):
            c = g * 2 + b
            h = starts[b]
            spread = jnp.broadcast_to(h, (WIDTH, WIDTH)).T
            last = off_ref[pl.ds(b * steps + g * SPAN + SPAN - 1, 1), :]
            parts = two_parts(h)
            after.append(h * kept_ref[pl.ds(c, 1), :] + parts_times(parts, grp_ref[c]) + last)
            rows = [jnp.sum(q_ref[s, c].astype(F32) * spread, axis=0, keepdims=True) for s in range(4)]
            for s in range(4, SPAN, 2):
                pair = parts_times(parts, jnp.concatenate([q_ref[s, c], q_ref[s + 1, c]], axis=1))
                rows += [pair[:, :WIDTH], pair[:, WIDTH:]]
            base = pl.multiple_of(g * SPAN, SPAN)
            states = jnp.concatenate(rows, axis=0) + off_ref[pl.ds(b * steps + base, SPAN), :]
            states_ref[pl.ds(base, SPAN), b * WIDTH : (b + 1) * WIDTH] = states
            mean = jnp.mean(states * states, axis=-1, keepdims=True)
            normed = states * lax.rsqrt(mean + 1e-05) * gain_ref[b : b + 1, :]
            normed_ref[pl.ds(base, SPAN), b * WIDTH : (b + 1) * WIDTH] = normed.astype(BF16)
        return tuple(after)

    lax.fori_loop(0, GROUPS, group, tuple(entry), unroll=8)


def replay(kept, init, y_maps, x_maps, off, grp, gain, q):
    steps = SPAN * GROUPS
    return pl.pallas_call(
        replay_kernel,
        out_shape=(
            jax.ShapeDtypeStruct((steps, 2 * WIDTH), F32),
            jax.ShapeDtypeStruct((steps, 2 * WIDTH), BF16),
        ),
        in_specs=[VMEM] * 12,
        out_specs=(VMEM, VMEM),
        compiler_params=pltpu.CompilerParams(vmem_limit_bytes=16_000_000),
        name="replay",
    )(kept, init, *y_maps, *x_maps, off, grp, gain, pltpu.with_memory_space_constraint(q, pltpu.VMEM))


def forward_kernel(m0, m1, m2, m3, theirs_ref, gate_ref, up_ref, down_ref, keep_ref, send_ref, hidden):
    z, core = places()[2:]
    wide = 2 * WIDTH

    def at(k, c):
        return pl.multiple_of((lax.rem(z + k, 4) * 2 + c) * wide, wide)

    parts = [(m0, 0, 0), (m1, 3, 0), (m2, 2, 0), (m3, 1, 0)]
    parts += [(theirs_ref.at[k], (4 - k) % 4, 1) for k in range(4)]
    for n in range(0, gate_ref.shape[1], wide):
        gate = up = None
        for ref, k, other in parts:
            chunk = ref[...]
            row = at(k, 1 - core if other else core)
            g = jnp.dot(chunk, gate_ref[pl.ds(row, wide), n : n + wide], preferred_element_type=F32)
            u = jnp.dot(chunk, up_ref[pl.ds(row, wide), n : n + wide], preferred_element_type=F32)
            gate = g if gate is None else gate + g
            up = u if up is None else up + u
        hidden[:, n : n + wide] = (gate / (1.0 + jnp.exp(-gate)) * up).astype(BF16)
    low = hidden[...]
    for ref, c in ((send_ref, 1 - core), (keep_ref, core)):
        for k in range(4):
            out = jnp.dot(low, down_ref[:, pl.ds(at(k, c), wide)], preferred_element_type=F32)
            ref[k] = out.astype(BF16)


def forward(mine, theirs, gate_weight, up_weight, down_weight):
    steps = mine[0].shape[0]
    weights = [pltpu.with_memory_space_constraint(w, pltpu.VMEM) for w in (gate_weight, up_weight, down_weight)]
    half = jax.ShapeDtypeStruct((4, steps, 2 * WIDTH), BF16)
    return pl.pallas_call(
        forward_kernel,
        out_shape=(half, half),
        in_specs=[VMEM] * 8,
        out_specs=(VMEM, VMEM),
        scratch_shapes=[pltpu.VMEM((steps, gate_weight.shape[1]), BF16)],
        compiler_params=pltpu.CompilerParams(vmem_limit_bytes=16_000_000),
        name="forward",
    )(*mine, theirs, *weights)


def x_back(v, k):
    return lax.ppermute(v, "tm", [(y * 4 + x, y * 4 + (x + k) % 4) for y in range(4) for x in range(4)])


def y_back(v, k):
    return lax.ppermute(v, "tm", [(y * 4 + x, (y + k) % 4 * 4 + x) for y in range(4) for x in range(4)])


def z_back(v, k):
    return lax.ppermute(v, "block", [(z * 2 + c, (z + k) % 4 * 2 + c) for z in range(4) for c in range(2)])


def other_core(v):
    return lax.ppermute(v, "block", [(s, s ^ 1) for s in range(8)])


def body(
    noise,
    retain,
    control_weight,
    input_weight,
    initial_state,
    norm_gain,
    gate_weight,
    up_weight,
    down_weight,
):
    q, off, own, grp, kept = compose(noise.T, retain.T, control_weight, input_weight)
    x_maps = [x_back(own, k) for k in (1, 2, 3)]
    total = row_map([own, *x_maps])
    y_maps = [y_back(total, k) for k in (1, 2, 3)]
    states, normed = replay(
        kept, initial_state.reshape(2, WIDTH), y_maps, x_maps, off, grp, norm_gain.reshape(2, WIDTH), q
    )
    mine = [normed] + [z_back(normed, k) for k in (1, 2, 3)]
    theirs = other_core(jnp.stack(mine))
    keep, sent = forward(mine, theirs, gate_weight, up_weight, down_weight)
    chip = keep.astype(F32) + other_core(sent).astype(F32)
    low = chip.astype(BF16)
    mixed = chip[0]
    for k in (1, 2, 3):
        mixed = mixed + z_back(low[k], k).astype(F32)
    return (states + mixed).astype(BF16)


def solution(mesh):
    placed = (
        P("tm", None),
        P("tm", "block"),
        P(None, "block", None, None),
        P(None, "block"),
        P("block"),
        P("block"),
        P(None, "block"),
        P(None, "block"),
        P("block", None),
    )
    return jax.shard_map(body, mesh=mesh, in_specs=placed, out_specs=P("tm", "block"), check_vma=False)
```

```python
import functools
import math

import jax
import jax.numpy as jnp
from jax import lax
from jax.experimental import pallas as pl
from jax.experimental.pallas import tpu as pltpu
from jax.sharding import PartitionSpec as P

F32 = jnp.float32
BF16 = jnp.bfloat16
GROUPS = 16
SPAN = 16
WIDTH = 128
ROWS = 144
PITCH = 129
MAP_ROWS = 144
VMEM = pl.BlockSpec(memory_space=pltpu.VMEM)
SMEM = pl.BlockSpec(memory_space=pltpu.SMEM)
ANY = pl.BlockSpec(memory_space=pl.ANY)


def split3(v):
    hi = v.astype(BF16)
    rest = v - hi.astype(F32)
    mid = rest.astype(BF16)
    return hi, mid, (rest - mid.astype(F32)).astype(BF16)


def pack_map(ref, b, matrix, offset, kept):
    ref[b, :WIDTH, :] = matrix.astype(BF16)
    row = lax.broadcasted_iota(jnp.int32, (16, WIDTH), 0)
    tail = jnp.zeros((16, WIDTH), F32)
    kept_row = jnp.full((1, WIDTH), 1.0, F32) * kept
    for k, part in enumerate((*split3(offset), *split3(kept_row))):
        tail = jnp.where(row == k, jnp.broadcast_to(part.astype(F32), (16, WIDTH)), tail)
    ref[b, WIDTH:, :] = tail.astype(BF16)


def unpack_map(ref, b):
    matrix = ref[b, :WIDTH, :]
    tail = ref[b, WIDTH:, :].astype(F32)
    offset = tail[0:1] + tail[1:2] + tail[2:3]
    kept = tail[3:4] + tail[4:5] + tail[5:6]
    return matrix, offset, kept


def two_parts(h):
    row = lax.broadcasted_iota(jnp.int32, (16, WIDTH), 0)
    hi = h.astype(BF16).astype(F32)
    lo = h - hi
    return jnp.where(
        row == 0, jnp.broadcast_to(hi, (16, WIDTH)), jnp.broadcast_to(lo, (16, WIDTH))
    ).astype(BF16)


def parts_times(parts, matrix):
    out = jnp.dot(parts, matrix, preferred_element_type=F32)
    return out[0:1] + out[1:2]


def row_times(h, matrix):
    return parts_times(two_parts(h), matrix)


def places():
    tm, block = lax.axis_index("tm"), lax.axis_index("block")
    return lax.div(tm, 4), lax.rem(tm, 4), lax.div(block, 2), lax.rem(block, 2)


def compose_kernel(
    noise_ref, retain_s, retain_ref, cw_ref, iw_ref, q_ref, off_ref, send_ref, grp_ref, kept_ref, skw, am, kept_s, sem
):
    steps = noise_ref.shape[1]
    loads = [
        pltpu.make_async_copy(cw_ref.at[pl.ds(32 * k, 32)], q_ref.at[k], sem.at[k]) for k in range(4)
    ]
    for load in loads:
        load.start()
    rows = lax.broadcasted_iota(jnp.int32, (WIDTH, WIDTH), 0)
    cols = lax.broadcasted_iota(jnp.int32, (WIDTH, WIDTH), 1)
    eye = (rows == cols).astype(F32)
    noise = noise_ref[...].T
    drive = jnp.dot(noise, iw_ref[...], precision=lax.Precision.HIGHEST, preferred_element_type=F32)
    kept = retain_ref[...]
    scale = jnp.sqrt(1.0 - kept * kept)
    for b in range(2):
        spread = jnp.broadcast_to(scale[b : b + 1, :], (WIDTH, steps)).T
        off_ref[b * steps : (b + 1) * steps, :] = drive[:, b * WIDTH : (b + 1) * WIDTH] * spread

    def skew_body(base, i, carry):
        for b in range(2):
            raw = q_ref[base // 16, i * 2 + b]
            diff = (raw.T.astype(F32) - raw.astype(F32)) * (1.0 / math.sqrt(2.0))
            skw[pl.ds((b * 64 + base + i) * PITCH, WIDTH), :] = diff
        return carry

    for k in range(4):
        loads[k].wait()
        lax.fori_loop(0, 16, functools.partial(skew_body, 16 * k), 0, unroll=8)
    low = (noise.astype(BF16).astype(F32) * (1.0 / 64.0)).astype(BF16)

    def build_body(j, carry):
        w = jnp.concatenate(
            [skw[pl.ds(b * 64 * PITCH + j, 64, stride=PITCH), :] for b in range(2)], axis=1
        ).astype(BF16)
        out = jnp.dot(low, w, preferred_element_type=F32)
        for b in range(2):
            am[pl.ds(b * steps * PITCH + j, steps, stride=PITCH), :] = out[:, b * WIDTH : (b + 1) * WIDTH]
        return carry

    lax.fori_loop(0, WIDTH, build_body, 0, unroll=16)
    tail_rows = ROWS - WIDTH
    tail_row = lax.broadcasted_iota(jnp.int32, (tail_rows, WIDTH), 0)
    zero = jnp.zeros((WIDTH, WIDTH), BF16)

    def run(c):
        return skw.at[pl.ds(pl.multiple_of(c * ROWS, 16), ROWS), :]

    def step_matrix(t, b):
        return am[pl.ds((b * steps + t) * PITCH, WIDTH), :]

    def finish(s, g, b, matrix, tail):
        t = g * SPAN + s
        c = g * 2 + b
        rate = retain_s[b, t]
        push = off_ref[pl.ds(b * steps + t, 1), :]
        matrix = matrix * rate
        placed = jnp.where(tail_row == 0, jnp.broadcast_to(push, (tail_rows, WIDTH)), 0.0)
        tail = placed if tail is None else tail * rate + placed
        run(c)[:WIDTH, :] = matrix
        run(c)[WIDTH:, :] = tail
        q_ref[s, c] = matrix.astype(BF16)
        off_ref[pl.ds(b * steps + t, 1), :] = tail[:1]
        return rate

    def first(g, carry):
        for b in range(2):
            kept_s[g, b] = finish(0, g, b, eye + step_matrix(g * SPAN, b), None)
        return carry

    lax.fori_loop(0, GROUPS, first, 0, unroll=4)

    def step(s, carry):
        def group(g, inner):
            t = g * SPAN + s
            now = [run(g * 2 + b)[...] for b in range(2)]
            low0, low1 = [step_matrix(t, b).astype(BF16) for b in range(2)]
            w = jnp.concatenate(
                [jnp.concatenate([low0, zero], axis=1), jnp.concatenate([zero, low1], axis=1)], axis=0
            )
            both = jnp.concatenate([x.astype(BF16) for x in now], axis=1)
            turned = jnp.dot(both, w, preferred_element_type=F32)
            for b in range(2):
                y = now[b] + turned[:, b * WIDTH : (b + 1) * WIDTH]
                rate = finish(s, g, b, y[:WIDTH], y[WIDTH:])
                kept_s[g, b] = kept_s[g, b] * rate
            return inner

        lax.fori_loop(0, GROUPS, group, 0, unroll=16)
        return carry

    lax.fori_loop(1, SPAN, step, 0)

    keeps = [[kept_s[g, b] for b in range(2)] for g in range(GROUPS)]
    for g in range(GROUPS):
        for b in range(2):
            c = g * 2 + b
            m = run(c)[:WIDTH, :] - eye * keeps[g][b]
            run(c)[:WIDTH, :] = m
            grp_ref[c] = m.astype(BF16)
            kept_ref[c : c + 1, :] = jnp.full((1, WIDTH), 1.0, F32) * keeps[g][b]
    stride = 1
    while stride < GROUPS:
        for g1 in range(0, GROUPS, 2 * stride):
            g2 = g1 + stride
            for b in range(2):
                one, two = run(g1 * 2 + b)[...], run(g2 * 2 + b)[...]
                prod = jnp.dot(one.astype(BF16), two[:WIDTH].astype(BF16), preferred_element_type=F32)
                k1, k2 = keeps[g1][b], keeps[g2][b]
                run(g1 * 2 + b)[:WIDTH, :] = prod[:WIDTH] + one[:WIDTH] * k2 + two[:WIDTH] * k1
                run(g1 * 2 + b)[WIDTH:, :] = prod[WIDTH:] + one[WIDTH:] * k2 + two[WIDTH:]
                keeps[g1][b] = k1 * k2
        stride *= 2
    for b in range(2):
        pack_map(send_ref, b, run(b)[:WIDTH, :], run(b)[WIDTH : WIDTH + 1, :], keeps[0][b])


def compose(noise, retain, control_weight, input_weight):
    steps = noise.shape[1]
    return pl.pallas_call(
        compose_kernel,
        out_shape=(
            pltpu.VMEM((SPAN, 2 * GROUPS, WIDTH, WIDTH), BF16),
            pltpu.VMEM((2 * steps, WIDTH), F32),
            pltpu.VMEM((2, MAP_ROWS, WIDTH), BF16),
            pltpu.VMEM((2 * GROUPS, WIDTH, WIDTH), BF16),
            pltpu.VMEM((2 * GROUPS, WIDTH), F32),
        ),
        in_specs=[VMEM, SMEM, VMEM, ANY, VMEM],
        out_specs=(VMEM, VMEM, VMEM, VMEM, VMEM),
        scratch_shapes=[
            pltpu.VMEM((128 * PITCH + 8, WIDTH), F32),
            pltpu.VMEM((2 * steps * PITCH + 8, WIDTH), F32),
            pltpu.SMEM((GROUPS, 2), F32),
            pltpu.SemaphoreType.DMA((4,)),
        ],
        compiler_params=pltpu.CompilerParams(vmem_limit_bytes=44_500_000),
        name="compose",
    )(noise, retain, retain, control_weight.reshape(-1, WIDTH, WIDTH), input_weight)


def row_kernel(m0, m1, m3, m2, out_ref, held):
    x = places()[1]
    for k, ref in enumerate((m0, m1, m2, m3)):
        held[lax.rem(x + 4 - k, 4)] = ref[...]
    for b in range(2):
        parts = []
        for k in range(4):
            matrix, offset, kept = unpack_map(held.at[k], b)
            parts.append((matrix.astype(F32), offset, kept))
        while len(parts) > 1:
            merged = []
            for (m1_, o1, k1), (m2_, o2, k2) in zip(parts[::2], parts[1::2]):
                low = m2_.astype(BF16)
                prod = jnp.dot(m1_.astype(BF16), low, preferred_element_type=F32)
                merged.append((prod + m1_ * k2 + m2_ * k1, row_times(o1, low) + o1 * k2 + o2, k1 * k2))
            parts = merged
        pack_map(out_ref, b, *parts[0])


def row_map(maps):
    return pl.pallas_call(
        row_kernel,
        out_shape=jax.ShapeDtypeStruct((2, MAP_ROWS, WIDTH), BF16),
        in_specs=[VMEM] * 4,
        out_specs=VMEM,
        scratch_shapes=[pltpu.VMEM((4, 2, MAP_ROWS, WIDTH), BF16)],
        compiler_params=pltpu.CompilerParams(vmem_limit_bytes=8_000_000),
        name="row_map",
    )(*maps)


def replay_kernel(kept_ref, init_ref, y1, y3, y2, x1, x3, x2, off_ref, grp_ref, gain_ref, q_ref,
                  states_ref, normed_ref):
    steps = SPAN * GROUPS
    y, x = places()[:2]
    entry = []
    for b in range(2):
        h = init_ref[b : b + 1, :]
        for place, refs in ((y, (y1, y2, y3)), (x, (x1, x2, x3))):
            for k in (3, 2, 1):
                matrix, offset, kept = unpack_map(refs[k - 1], b)
                h = jnp.where(k <= place, h * kept + row_times(h, matrix) + offset, h)
        entry.append(h)

    def group(g, starts):
        after = []
        for b in range(2):
            c = g * 2 + b
            h = starts[b]
            spread = jnp.broadcast_to(h, (WIDTH, WIDTH)).T
            last = off_ref[pl.ds(b * steps + g * SPAN + SPAN - 1, 1), :]
            parts = two_parts(h)
            after.append(h * kept_ref[pl.ds(c, 1), :] + parts_times(parts, grp_ref[c]) + last)
            rows = [jnp.sum(q_ref[s, c].astype(F32) * spread, axis=0, keepdims=True) for s in range(4)]
            for s in range(4, SPAN, 2):
                pair = parts_times(parts, jnp.concatenate([q_ref[s, c], q_ref[s + 1, c]], axis=1))
                rows += [pair[:, :WIDTH], pair[:, WIDTH:]]
            base = pl.multiple_of(g * SPAN, SPAN)
            states = jnp.concatenate(rows, axis=0) + off_ref[pl.ds(b * steps + base, SPAN), :]
            states_ref[pl.ds(base, SPAN), b * WIDTH : (b + 1) * WIDTH] = states
            mean = jnp.mean(states * states, axis=-1, keepdims=True)
            normed = states * lax.rsqrt(mean + 1e-05) * gain_ref[b : b + 1, :]
            normed_ref[pl.ds(base, SPAN), b * WIDTH : (b + 1) * WIDTH] = normed.astype(BF16)
        return tuple(after)

    lax.fori_loop(0, GROUPS, group, tuple(entry), unroll=8)


def replay(kept, init, y_maps, x_maps, off, grp, gain, q):
    steps = SPAN * GROUPS
    return pl.pallas_call(
        replay_kernel,
        out_shape=(
            jax.ShapeDtypeStruct((steps, 2 * WIDTH), F32),
            jax.ShapeDtypeStruct((steps, 2 * WIDTH), BF16),
        ),
        in_specs=[VMEM] * 12,
        out_specs=(VMEM, VMEM),
        compiler_params=pltpu.CompilerParams(vmem_limit_bytes=16_000_000),
        name="replay",
    )(kept, init, *y_maps, *x_maps, off, grp, gain, pltpu.with_memory_space_constraint(q, pltpu.VMEM))


def forward_kernel(m0, m1, m3, m2, theirs_ref, gate_ref, up_ref, down_ref, keep_ref, send_ref, hidden):
    z, core = places()[2:]
    wide = 2 * WIDTH

    def at(k, c):
        return pl.multiple_of((lax.rem(z + k, 4) * 2 + c) * wide, wide)

    parts = [(m0, 0, 0), (m1, 3, 0), (m2, 2, 0), (m3, 1, 0)]
    parts += [(theirs_ref.at[i], (4 - k) % 4, 1) for i, k in enumerate((0, 1, 3, 2))]
    for n in range(0, gate_ref.shape[1], wide):
        gate = up = None
        for ref, k, other in parts:
            chunk = ref[...]
            row = at(k, 1 - core if other else core)
            g = jnp.dot(chunk, gate_ref[pl.ds(row, wide), n : n + wide], preferred_element_type=F32)
            u = jnp.dot(chunk, up_ref[pl.ds(row, wide), n : n + wide], preferred_element_type=F32)
            gate = g if gate is None else gate + g
            up = u if up is None else up + u
        hidden[:, n : n + wide] = (gate / (1.0 + jnp.exp(-gate)) * up).astype(BF16)
    low = hidden[...]
    for ref, c in ((send_ref, 1 - core), (keep_ref, core)):
        for k in range(4):
            out = jnp.dot(low, down_ref[:, pl.ds(at(k, c), wide)], preferred_element_type=F32)
            ref[k] = out.astype(BF16)


def forward(mine, theirs, gate_weight, up_weight, down_weight):
    steps = mine[0].shape[0]
    weights = [pltpu.with_memory_space_constraint(w, pltpu.VMEM) for w in (gate_weight, up_weight, down_weight)]
    half = jax.ShapeDtypeStruct((4, steps, 2 * WIDTH), BF16)
    return pl.pallas_call(
        forward_kernel,
        out_shape=(half, half),
        in_specs=[VMEM] * 8,
        out_specs=(VMEM, VMEM),
        scratch_shapes=[pltpu.VMEM((steps, gate_weight.shape[1]), BF16)],
        compiler_params=pltpu.CompilerParams(vmem_limit_bytes=16_000_000),
        name="forward",
    )(*mine, theirs, *weights)


def x_back(v, k):
    return lax.ppermute(v, "tm", [(y * 4 + x, y * 4 + (x + k) % 4) for y in range(4) for x in range(4)])


def y_back(v, k):
    return lax.ppermute(v, "tm", [(y * 4 + x, (y + k) * 4 + x) for y in range(4 - k) for x in range(4)])


def z_back(v, k):
    return lax.ppermute(v, "block", [(z * 2 + c, (z + k) % 4 * 2 + c) for z in range(4) for c in range(2)])


def three(back, v):
    return [back(v, k) for k in (1, 3, 2)]


def other_core(v):
    return lax.ppermute(v, "block", [(s, s ^ 1) for s in range(8)])


def body(
    noise,
    retain,
    control_weight,
    input_weight,
    initial_state,
    norm_gain,
    gate_weight,
    up_weight,
    down_weight,
):
    q, off, own, grp, kept = compose(noise.T, retain.T, control_weight, input_weight)
    x_maps = three(x_back, own)
    total = row_map([own, *x_maps])
    y_maps = three(y_back, total)
    states, normed = replay(
        kept, initial_state.reshape(2, WIDTH), y_maps, x_maps, off, grp, norm_gain.reshape(2, WIDTH), q
    )
    mine = [normed] + three(z_back, normed)
    theirs = other_core(jnp.stack(mine))
    keep, sent = forward(mine, theirs, gate_weight, up_weight, down_weight)
    chip = keep.astype(F32) + other_core(sent).astype(F32)
    low = chip.astype(BF16)
    mixed = chip[0]
    for k in (2, 1, 3):
        mixed = mixed + z_back(low[k], k).astype(F32)
    return (states + mixed).astype(BF16)


def solution(mesh):
    placed = (
        P("tm", None),
        P("tm", "block"),
        P(None, "block", None, None),
        P(None, "block"),
        P("block"),
        P("block"),
        P(None, "block"),
        P(None, "block"),
        P("block", None),
    )
    return jax.shard_map(body, mesh=mesh, in_specs=placed, out_specs=P("tm", "block"), check_vma=False)
```

```python
import functools
import math

import jax
import jax.numpy as jnp
from jax import lax
from jax.experimental import pallas as pl
from jax.experimental.pallas import tpu as pltpu
from jax.sharding import PartitionSpec as P

F32 = jnp.float32
BF16 = jnp.bfloat16
GROUPS = 16
SPAN = 16
WIDTH = 128
ROWS = 144
PITCH = 129
MAP_ROWS = 144
VMEM = pl.BlockSpec(memory_space=pltpu.VMEM)
SMEM = pl.BlockSpec(memory_space=pltpu.SMEM)
ANY = pl.BlockSpec(memory_space=pl.ANY)


def split3(v):
    hi = v.astype(BF16)
    rest = v - hi.astype(F32)
    mid = rest.astype(BF16)
    return hi, mid, (rest - mid.astype(F32)).astype(BF16)


def pack_map(ref, b, matrix, offset, kept):
    ref[b, :WIDTH, :] = matrix.astype(BF16)
    row = lax.broadcasted_iota(jnp.int32, (16, WIDTH), 0)
    tail = jnp.zeros((16, WIDTH), F32)
    kept_row = jnp.full((1, WIDTH), 1.0, F32) * kept
    for k, part in enumerate((*split3(offset), *split3(kept_row))):
        tail = jnp.where(row == k, jnp.broadcast_to(part.astype(F32), (16, WIDTH)), tail)
    ref[b, WIDTH:, :] = tail.astype(BF16)


def unpack_map(ref, b):
    matrix = ref[b, :WIDTH, :]
    tail = ref[b, WIDTH:, :].astype(F32)
    offset = tail[0:1] + tail[1:2] + tail[2:3]
    kept = tail[3:4] + tail[4:5] + tail[5:6]
    return matrix, offset, kept


def two_parts(h):
    row = lax.broadcasted_iota(jnp.int32, (16, WIDTH), 0)
    hi = h.astype(BF16).astype(F32)
    lo = h - hi
    return jnp.where(
        row == 0, jnp.broadcast_to(hi, (16, WIDTH)), jnp.broadcast_to(lo, (16, WIDTH))
    ).astype(BF16)


def parts_times(parts, matrix):
    out = jnp.dot(parts, matrix, preferred_element_type=F32)
    return out[0:1] + out[1:2]


def row_times(h, matrix):
    return parts_times(two_parts(h), matrix)


def places():
    tm, block = lax.axis_index("tm"), lax.axis_index("block")
    return lax.div(tm, 4), lax.rem(tm, 4), lax.div(block, 2), lax.rem(block, 2)


def compose_kernel(
    noise_ref, retain_s, retain_ref, cw_ref, iw_ref, q_ref, off_ref, send_ref, grp_ref, kept_ref, skw, am, kept_s, sem
):
    steps = noise_ref.shape[1]
    loads = [
        pltpu.make_async_copy(cw_ref.at[pl.ds(32 * k, 32)], q_ref.at[k], sem.at[k]) for k in range(4)
    ]
    for load in loads:
        load.start()
    rows = lax.broadcasted_iota(jnp.int32, (WIDTH, WIDTH), 0)
    cols = lax.broadcasted_iota(jnp.int32, (WIDTH, WIDTH), 1)
    eye = (rows == cols).astype(F32)
    noise = noise_ref[...].T
    drive = jnp.dot(noise, iw_ref[...], precision=lax.Precision.HIGHEST, preferred_element_type=F32)
    kept = retain_ref[...]
    scale = jnp.sqrt(1.0 - kept * kept)
    for b in range(2):
        spread = jnp.broadcast_to(scale[b : b + 1, :], (WIDTH, steps)).T
        off_ref[b * steps : (b + 1) * steps, :] = drive[:, b * WIDTH : (b + 1) * WIDTH] * spread

    def skew_body(base, i, carry):
        for b in range(2):
            raw = q_ref[base // 16, i * 2 + b]
            diff = (raw.T.astype(F32) - raw.astype(F32)) * (1.0 / math.sqrt(2.0))
            skw[pl.ds((b * 64 + base + i) * PITCH, WIDTH), :] = diff
        return carry

    for k in range(4):
        loads[k].wait()
        lax.fori_loop(0, 16, functools.partial(skew_body, 16 * k), 0, unroll=8)
    low = (noise.astype(BF16).astype(F32) * (1.0 / 64.0)).astype(BF16)

    def build_body(j, carry):
        w = jnp.concatenate(
            [skw[pl.ds(b * 64 * PITCH + j, 64, stride=PITCH), :] for b in range(2)], axis=1
        ).astype(BF16)
        out = jnp.dot(low, w, preferred_element_type=F32)
        for b in range(2):
            am[pl.ds(b * steps * PITCH + j, steps, stride=PITCH), :] = out[:, b * WIDTH : (b + 1) * WIDTH]
        return carry

    lax.fori_loop(0, WIDTH, build_body, 0, unroll=16)
    tail_rows = ROWS - WIDTH
    tail_row = lax.broadcasted_iota(jnp.int32, (tail_rows, WIDTH), 0)
    zero = jnp.zeros((WIDTH, WIDTH), BF16)

    def run(c):
        return skw.at[pl.ds(pl.multiple_of(c * ROWS, 16), ROWS), :]

    def step_matrix(t, b):
        return am[pl.ds((b * steps + t) * PITCH, WIDTH), :]

    def finish(s, g, b, matrix, tail):
        t = g * SPAN + s
        c = g * 2 + b
        rate = retain_s[b, t]
        push = off_ref[pl.ds(b * steps + t, 1), :]
        matrix = matrix * rate
        placed = jnp.where(tail_row == 0, jnp.broadcast_to(push, (tail_rows, WIDTH)), 0.0)
        tail = placed if tail is None else tail * rate + placed
        run(c)[:WIDTH, :] = matrix
        run(c)[WIDTH:, :] = tail
        q_ref[s, c] = matrix.astype(BF16)
        off_ref[pl.ds(b * steps + t, 1), :] = tail[:1]
        return rate

    def first(g, carry):
        for b in range(2):
            kept_s[g, b] = finish(0, g, b, eye + step_matrix(g * SPAN, b), None)
        return carry

    lax.fori_loop(0, GROUPS, first, 0, unroll=4)

    def step(s, carry):
        def group(g, inner):
            t = g * SPAN + s
            now = [run(g * 2 + b)[...] for b in range(2)]
            low0, low1 = [step_matrix(t, b).astype(BF16) for b in range(2)]
            w = jnp.concatenate(
                [jnp.concatenate([low0, zero], axis=1), jnp.concatenate([zero, low1], axis=1)], axis=0
            )
            both = jnp.concatenate([x.astype(BF16) for x in now], axis=1)
            turned = jnp.dot(both, w, preferred_element_type=F32)
            for b in range(2):
                y = now[b] + turned[:, b * WIDTH : (b + 1) * WIDTH]
                rate = finish(s, g, b, y[:WIDTH], y[WIDTH:])
                kept_s[g, b] = kept_s[g, b] * rate
            return inner

        lax.fori_loop(0, GROUPS, group, 0, unroll=16)
        return carry

    lax.fori_loop(1, SPAN, step, 0)

    keeps = [[kept_s[g, b] for b in range(2)] for g in range(GROUPS)]
    for g in range(GROUPS):
        for b in range(2):
            c = g * 2 + b
            m = run(c)[:WIDTH, :] - eye * keeps[g][b]
            run(c)[:WIDTH, :] = m
            grp_ref[c] = m.astype(BF16)
            kept_ref[c : c + 1, :] = jnp.full((1, WIDTH), 1.0, F32) * keeps[g][b]
    stride = 1
    while stride < GROUPS:
        for g1 in range(0, GROUPS, 2 * stride):
            g2 = g1 + stride
            for b in range(2):
                one, two = run(g1 * 2 + b)[...], run(g2 * 2 + b)[...]
                prod = jnp.dot(one.astype(BF16), two[:WIDTH].astype(BF16), preferred_element_type=F32)
                k1, k2 = keeps[g1][b], keeps[g2][b]
                run(g1 * 2 + b)[:WIDTH, :] = prod[:WIDTH] + one[:WIDTH] * k2 + two[:WIDTH] * k1
                run(g1 * 2 + b)[WIDTH:, :] = prod[WIDTH:] + one[WIDTH:] * k2 + two[WIDTH:]
                keeps[g1][b] = k1 * k2
        stride *= 2
    for b in range(2):
        pack_map(send_ref, b, run(b)[:WIDTH, :], run(b)[WIDTH : WIDTH + 1, :], keeps[0][b])


def compose(noise, retain, control_weight, input_weight):
    steps = noise.shape[1]
    return pl.pallas_call(
        compose_kernel,
        out_shape=(
            pltpu.VMEM((SPAN, 2 * GROUPS, WIDTH, WIDTH), BF16),
            pltpu.VMEM((2 * steps, WIDTH), F32),
            pltpu.VMEM((2, MAP_ROWS, WIDTH), BF16),
            pltpu.VMEM((2 * GROUPS, WIDTH, WIDTH), BF16),
            pltpu.VMEM((2 * GROUPS, WIDTH), F32),
        ),
        in_specs=[VMEM, SMEM, VMEM, ANY, VMEM],
        out_specs=(VMEM, VMEM, VMEM, VMEM, VMEM),
        scratch_shapes=[
            pltpu.VMEM((128 * PITCH + 8, WIDTH), F32),
            pltpu.VMEM((2 * steps * PITCH + 8, WIDTH), F32),
            pltpu.SMEM((GROUPS, 2), F32),
            pltpu.SemaphoreType.DMA((4,)),
        ],
        compiler_params=pltpu.CompilerParams(vmem_limit_bytes=44_500_000),
        name="compose",
    )(noise, retain, retain, control_weight.reshape(-1, WIDTH, WIDTH), input_weight)


def row_kernel(m0, m1, m3, m2, out_ref, held):
    x = places()[1]
    for k, ref in enumerate((m0, m1, m2, m3)):
        held[lax.rem(x + 4 - k, 4)] = ref[...]
    for b in range(2):
        parts = []
        for k in range(4):
            matrix, offset, kept = unpack_map(held.at[k], b)
            parts.append((matrix.astype(F32), offset, kept))
        while len(parts) > 1:
            merged = []
            for (m1_, o1, k1), (m2_, o2, k2) in zip(parts[::2], parts[1::2]):
                low = m2_.astype(BF16)
                prod = jnp.dot(m1_.astype(BF16), low, preferred_element_type=F32)
                merged.append((prod + m1_ * k2 + m2_ * k1, row_times(o1, low) + o1 * k2 + o2, k1 * k2))
            parts = merged
        pack_map(out_ref, b, *parts[0])


def row_map(maps):
    return pl.pallas_call(
        row_kernel,
        out_shape=jax.ShapeDtypeStruct((2, MAP_ROWS, WIDTH), BF16),
        in_specs=[VMEM] * 4,
        out_specs=VMEM,
        scratch_shapes=[pltpu.VMEM((4, 2, MAP_ROWS, WIDTH), BF16)],
        compiler_params=pltpu.CompilerParams(vmem_limit_bytes=8_000_000),
        name="row_map",
    )(*maps)


def replay_kernel(kept_ref, init_ref, y1, y3, y2, x1, x3, x2, off_ref, grp_ref, gain_ref, q_ref,
                  states_ref, normed_ref):
    steps = SPAN * GROUPS
    y, x = places()[:2]
    entry = []
    for b in range(2):
        h = init_ref[b : b + 1, :]
        for place, refs in ((y, (y1, y2, y3)), (x, (x1, x2, x3))):
            for k in (3, 2, 1):
                matrix, offset, kept = unpack_map(refs[k - 1], b)
                h = jnp.where(k <= place, h * kept + row_times(h, matrix) + offset, h)
        entry.append(h)

    def group(g, starts):
        after = []
        for b in range(2):
            c = g * 2 + b
            h = starts[b]
            spread = jnp.broadcast_to(h, (WIDTH, WIDTH)).T
            last = off_ref[pl.ds(b * steps + g * SPAN + SPAN - 1, 1), :]
            parts = two_parts(h)
            after.append(h * kept_ref[pl.ds(c, 1), :] + parts_times(parts, grp_ref[c]) + last)
            rows = [jnp.sum(q_ref[s, c].astype(F32) * spread, axis=0, keepdims=True) for s in range(4)]
            for s in range(4, SPAN, 2):
                pair = parts_times(parts, jnp.concatenate([q_ref[s, c], q_ref[s + 1, c]], axis=1))
                rows += [pair[:, :WIDTH], pair[:, WIDTH:]]
            base = pl.multiple_of(g * SPAN, SPAN)
            states = jnp.concatenate(rows, axis=0) + off_ref[pl.ds(b * steps + base, SPAN), :]
            states_ref[pl.ds(base, SPAN), b * WIDTH : (b + 1) * WIDTH] = states
            mean = jnp.mean(states * states, axis=-1, keepdims=True)
            normed = states * lax.rsqrt(mean + 1e-05) * gain_ref[b : b + 1, :]
            normed_ref[pl.ds(base, SPAN), b * WIDTH : (b + 1) * WIDTH] = normed.astype(BF16)
        return tuple(after)

    lax.fori_loop(0, GROUPS, group, tuple(entry), unroll=8)


def replay(kept, init, y_maps, x_maps, off, grp, gain, q):
    steps = SPAN * GROUPS
    return pl.pallas_call(
        replay_kernel,
        out_shape=(
            jax.ShapeDtypeStruct((steps, 2 * WIDTH), F32),
            jax.ShapeDtypeStruct((steps, 2 * WIDTH), BF16),
        ),
        in_specs=[VMEM] * 12,
        out_specs=(VMEM, VMEM),
        compiler_params=pltpu.CompilerParams(vmem_limit_bytes=16_000_000),
        name="replay",
    )(kept, init, *y_maps, *x_maps, off, grp, gain, pltpu.with_memory_space_constraint(q, pltpu.VMEM))


def weight_rows(k, c):
    z = places()[2]
    return pl.multiple_of((lax.rem(z + k, 4) * 2 + c) * 2 * WIDTH, 2 * WIDTH)


def products(parts, gate_ref, up_ref, n):
    wide = 2 * WIDTH
    gate = up = None
    for ref, row in parts:
        chunk = ref[...]
        g = jnp.dot(chunk, gate_ref[pl.ds(row, wide), n : n + wide], preferred_element_type=F32)
        u = jnp.dot(chunk, up_ref[pl.ds(row, wide), n : n + wide], preferred_element_type=F32)
        gate = g if gate is None else gate + g
        up = u if up is None else up + u
    return gate, up


def early_kernel(m0, m1, m3, theirs_ref, gate_ref, up_ref, gate_out, up_out):
    core = places()[3]
    way = 1 - 2 * core
    parts = [(ref, weight_rows(4 + k * way, core)) for ref, k in zip((m0, m1, m3), (0, -1, 1))]
    parts += [(theirs_ref.at[i], weight_rows(4 + k * way, 1 - core)) for i, k in enumerate((0, 1, -1))]
    wide = 2 * WIDTH
    for n in range(0, gate_ref.shape[1], wide):
        gate_out[:, n : n + wide], up_out[:, n : n + wide] = products(parts, gate_ref, up_ref, n)


def late_kernel(m2, theirs_ref, gate_in, up_in, gate_ref, up_ref, down_ref, keep_ref, send_ref, hidden):
    core = places()[3]
    parts = [(m2, weight_rows(2, core)), (theirs_ref, weight_rows(2, 1 - core))]
    wide = 2 * WIDTH
    for n in range(0, gate_ref.shape[1], wide):
        gate, up = products(parts, gate_ref, up_ref, n)
        gate = gate + gate_in[:, n : n + wide]
        up = up + up_in[:, n : n + wide]
        hidden[:, n : n + wide] = (gate / (1.0 + jnp.exp(-gate)) * up).astype(BF16)
    low = hidden[...]
    for ref, c in ((send_ref, 1 - core), (keep_ref, core)):
        for k in range(4):
            out = jnp.dot(low, down_ref[:, pl.ds(weight_rows(k, c), wide)], preferred_element_type=F32)
            ref[k] = out.astype(BF16)


def forward(normed, gate_weight, up_weight, down_weight):
    steps, units = normed.shape[0], gate_weight.shape[1]
    gate_weight, up_weight, down_weight = [
        pltpu.with_memory_space_constraint(w, pltpu.VMEM) for w in (gate_weight, up_weight, down_weight)
    ]
    one, last = z_round(normed, 1), z_round(normed, -1)
    two = z_round(one, 1)
    near = other_core(jnp.stack([normed, one, last]))
    wide = pltpu.VMEM((steps, units), F32)
    gate, up = pl.pallas_call(
        early_kernel,
        out_shape=(wide, wide),
        in_specs=[VMEM] * 6,
        out_specs=(VMEM, VMEM),
        compiler_params=pltpu.CompilerParams(vmem_limit_bytes=16_000_000),
        name="early",
    )(normed, one, last, near, gate_weight, up_weight)
    two, gate = lax.optimization_barrier((two, gate))
    half = jax.ShapeDtypeStruct((4, steps, 2 * WIDTH), BF16)
    return pl.pallas_call(
        late_kernel,
        out_shape=(half, half),
        in_specs=[VMEM] * 7,
        out_specs=(VMEM, VMEM),
        scratch_shapes=[pltpu.VMEM((steps, units), BF16)],
        compiler_params=pltpu.CompilerParams(vmem_limit_bytes=16_000_000),
        name="late",
    )(two, other_core(two), gate, up, gate_weight, up_weight, down_weight)


def x_back(v, k):
    return lax.ppermute(v, "tm", [(y * 4 + x, y * 4 + (x + k) % 4) for y in range(4) for x in range(4)])


def y_back(v, k):
    return lax.ppermute(v, "tm", [(y * 4 + x, (y + k) % 4 * 4 + x) for y in range(4) for x in range(4)])


def z_back(v, k):
    return lax.ppermute(v, "block", [(z * 2 + c, (z + k) % 4 * 2 + c) for z in range(4) for c in range(2)])


def three(back, v):
    return [back(v, k) for k in (1, 3, 2)]


def z_round(v, way):
    return lax.ppermute(
        v, "block", [(z * 2 + c, (z + way * (1 - 2 * c)) % 4 * 2 + c) for z in range(4) for c in range(2)]
    )


def other_core(v):
    return lax.ppermute(v, "block", [(s, s ^ 1) for s in range(8)])


def body(
    noise,
    retain,
    control_weight,
    input_weight,
    initial_state,
    norm_gain,
    gate_weight,
    up_weight,
    down_weight,
):
    q, off, own, grp, kept = compose(noise.T, retain.T, control_weight, input_weight)
    x_maps = three(x_back, own)
    total = row_map([own, *x_maps])
    y_maps = three(y_back, total)
    states, normed = replay(
        kept, initial_state.reshape(2, WIDTH), y_maps, x_maps, off, grp, norm_gain.reshape(2, WIDTH), q
    )
    keep, sent = forward(normed, gate_weight, up_weight, down_weight)
    chip = keep.astype(F32) + other_core(sent).astype(F32)
    low = chip.astype(BF16)
    mixed = chip[0]
    for k in (2, 1, 3):
        mixed = mixed + z_back(low[k], k).astype(F32)
    return (states + mixed).astype(BF16)


def solution(mesh):
    placed = (
        P("tm", None),
        P("tm", "block"),
        P(None, "block", None, None),
        P(None, "block"),
        P("block"),
        P("block"),
        P(None, "block"),
        P(None, "block"),
        P("block", None),
    )
    return jax.shard_map(body, mesh=mesh, in_specs=placed, out_specs=P("tm", "block"), check_vma=False)
```

```python
import functools
import math

import jax
import jax.numpy as jnp
from jax import lax
from jax.experimental import pallas as pl
from jax.experimental.pallas import tpu as pltpu
from jax.sharding import PartitionSpec as P

F32 = jnp.float32
BF16 = jnp.bfloat16
GROUPS = 16
SPAN = 16
WIDTH = 128
ROWS = 144
VECTOR_STEPS = 5
PITCH = 129
MAP_ROWS = 144
VMEM = pl.BlockSpec(memory_space=pltpu.VMEM)
SMEM = pl.BlockSpec(memory_space=pltpu.SMEM)
ANY = pl.BlockSpec(memory_space=pl.ANY)


def split3(v):
    hi = v.astype(BF16)
    rest = v - hi.astype(F32)
    mid = rest.astype(BF16)
    return hi, mid, (rest - mid.astype(F32)).astype(BF16)


def pack_map(ref, b, matrix, offset, kept):
    ref[b, :WIDTH, :] = matrix.astype(BF16)
    row = lax.broadcasted_iota(jnp.int32, (16, WIDTH), 0)
    tail = jnp.zeros((16, WIDTH), F32)
    kept_row = jnp.full((1, WIDTH), 1.0, F32) * kept
    for k, part in enumerate((*split3(offset), *split3(kept_row))):
        tail = jnp.where(row == k, jnp.broadcast_to(part.astype(F32), (16, WIDTH)), tail)
    ref[b, WIDTH:, :] = tail.astype(BF16)


def unpack_map(ref, b):
    matrix = ref[b, :WIDTH, :]
    tail = ref[b, WIDTH:, :].astype(F32)
    offset = tail[0:1] + tail[1:2] + tail[2:3]
    kept = tail[3:4] + tail[4:5] + tail[5:6]
    return matrix, offset, kept


def two_parts(h):
    row = lax.broadcasted_iota(jnp.int32, (16, WIDTH), 0)
    hi = h.astype(BF16).astype(F32)
    lo = h - hi
    return jnp.where(
        row == 0, jnp.broadcast_to(hi, (16, WIDTH)), jnp.broadcast_to(lo, (16, WIDTH))
    ).astype(BF16)


def parts_times(parts, matrix):
    out = jnp.dot(parts, matrix, preferred_element_type=F32)
    return out[0:1] + out[1:2]


def row_times(h, matrix):
    return parts_times(two_parts(h), matrix)


def places():
    tm, block = lax.axis_index("tm"), lax.axis_index("block")
    return lax.div(tm, 4), lax.rem(tm, 4), lax.div(block, 2), lax.rem(block, 2)


def compose_kernel(
    noise_ref, retain_s, retain_ref, cw_ref, iw_ref, q_ref, off_ref, send_ref, grp_ref, kept_ref, skw, am, kept_s, sem
):
    steps = noise_ref.shape[1]
    loads = [
        pltpu.make_async_copy(cw_ref.at[pl.ds(32 * k, 32)], q_ref.at[k], sem.at[k]) for k in range(4)
    ]
    for load in loads:
        load.start()
    rows = lax.broadcasted_iota(jnp.int32, (WIDTH, WIDTH), 0)
    cols = lax.broadcasted_iota(jnp.int32, (WIDTH, WIDTH), 1)
    eye = (rows == cols).astype(F32)
    noise = noise_ref[...].T
    drive = jnp.dot(noise, iw_ref[...], precision=lax.Precision.HIGHEST, preferred_element_type=F32)
    kept = retain_ref[...]
    scale = jnp.sqrt(1.0 - kept * kept)
    for b in range(2):
        spread = jnp.broadcast_to(scale[b : b + 1, :], (WIDTH, steps)).T
        off_ref[b * steps : (b + 1) * steps, :] = drive[:, b * WIDTH : (b + 1) * WIDTH] * spread

    def skew_body(base, i, carry):
        for b in range(2):
            raw = q_ref[base // 16, i * 2 + b]
            diff = (raw.T.astype(F32) - raw.astype(F32)) * (1.0 / math.sqrt(2.0))
            skw[pl.ds((b * 64 + base + i) * PITCH, WIDTH), :] = diff
        return carry

    for k in range(4):
        loads[k].wait()
        lax.fori_loop(0, 16, functools.partial(skew_body, 16 * k), 0, unroll=8)
    low = (noise.astype(BF16).astype(F32) * (1.0 / 64.0)).astype(BF16)

    def build_body(j, carry):
        w = jnp.concatenate(
            [skw[pl.ds(b * 64 * PITCH + j, 64, stride=PITCH), :] for b in range(2)], axis=1
        ).astype(BF16)
        out = jnp.dot(low, w, preferred_element_type=F32)
        for b in range(2):
            am[pl.ds(b * steps * PITCH + j, steps, stride=PITCH), :] = out[:, b * WIDTH : (b + 1) * WIDTH]
        return carry

    lax.fori_loop(0, WIDTH, build_body, 0, unroll=16)
    tail_rows = ROWS - WIDTH
    tail_row = lax.broadcasted_iota(jnp.int32, (tail_rows, WIDTH), 0)
    zero = jnp.zeros((WIDTH, WIDTH), BF16)

    def run(c):
        return skw.at[pl.ds(pl.multiple_of(c * ROWS, 16), ROWS), :]

    def step_matrix(t, b):
        return am[pl.ds((b * steps + t) * PITCH, WIDTH), :]

    def finish(s, g, b, matrix, tail):
        t = g * SPAN + s
        c = g * 2 + b
        rate = retain_s[b, t]
        push = off_ref[pl.ds(b * steps + t, 1), :]
        matrix = matrix * rate
        placed = jnp.where(tail_row == 0, jnp.broadcast_to(push, (tail_rows, WIDTH)), 0.0)
        tail = placed if tail is None else tail * rate + placed
        run(c)[:WIDTH, :] = matrix
        run(c)[WIDTH:, :] = tail
        q_ref[s, c] = matrix.astype(BF16)
        off_ref[pl.ds(b * steps + t, 1), :] = tail[:1]
        return rate

    def first(g, carry):
        for b in range(2):
            kept_s[g, b] = finish(0, g, b, eye + step_matrix(g * SPAN, b), None)
        return carry

    lax.fori_loop(0, GROUPS, first, 0, unroll=4)

    def step(s, carry):
        def group(g, inner):
            t = g * SPAN + s
            now = [run(g * 2 + b)[...] for b in range(2)]
            low0, low1 = [step_matrix(t, b).astype(BF16) for b in range(2)]
            w = jnp.concatenate(
                [jnp.concatenate([low0, zero], axis=1), jnp.concatenate([zero, low1], axis=1)], axis=0
            )
            both = jnp.concatenate([x.astype(BF16) for x in now], axis=1)
            turned = jnp.dot(both, w, preferred_element_type=F32)
            for b in range(2):
                y = now[b] + turned[:, b * WIDTH : (b + 1) * WIDTH]
                rate = finish(s, g, b, y[:WIDTH], y[WIDTH:])
                kept_s[g, b] = kept_s[g, b] * rate
            return inner

        lax.fori_loop(0, GROUPS, group, 0, unroll=16)
        return carry

    lax.fori_loop(1, SPAN, step, 0)

    keeps = [[kept_s[g, b] for b in range(2)] for g in range(GROUPS)]
    for g in range(GROUPS):
        for b in range(2):
            c = g * 2 + b
            m = run(c)[:WIDTH, :] - eye * keeps[g][b]
            run(c)[:WIDTH, :] = m
            grp_ref[c] = m.astype(BF16)
            kept_ref[c : c + 1, :] = jnp.full((1, WIDTH), 1.0, F32) * keeps[g][b]
    stride = 1
    while stride < GROUPS:
        for g1 in range(0, GROUPS, 2 * stride):
            g2 = g1 + stride
            for b in range(2):
                one, two = run(g1 * 2 + b)[...], run(g2 * 2 + b)[...]
                prod = jnp.dot(one.astype(BF16), two[:WIDTH].astype(BF16), preferred_element_type=F32)
                k1, k2 = keeps[g1][b], keeps[g2][b]
                run(g1 * 2 + b)[:WIDTH, :] = prod[:WIDTH] + one[:WIDTH] * k2 + two[:WIDTH] * k1
                run(g1 * 2 + b)[WIDTH:, :] = prod[WIDTH:] + one[WIDTH:] * k2 + two[WIDTH:]
                keeps[g1][b] = k1 * k2
        stride *= 2
    for b in range(2):
        pack_map(send_ref, b, run(b)[:WIDTH, :], run(b)[WIDTH : WIDTH + 1, :], keeps[0][b])


def compose(noise, retain, control_weight, input_weight):
    steps = noise.shape[1]
    return pl.pallas_call(
        compose_kernel,
        out_shape=(
            pltpu.VMEM((SPAN, 2 * GROUPS, WIDTH, WIDTH), BF16),
            pltpu.VMEM((2 * steps, WIDTH), F32),
            pltpu.VMEM((2, MAP_ROWS, WIDTH), BF16),
            pltpu.VMEM((2 * GROUPS, WIDTH, WIDTH), BF16),
            pltpu.VMEM((2 * GROUPS, WIDTH), F32),
        ),
        in_specs=[VMEM, SMEM, VMEM, ANY, VMEM],
        out_specs=(VMEM, VMEM, VMEM, VMEM, VMEM),
        scratch_shapes=[
            pltpu.VMEM((128 * PITCH + 8, WIDTH), F32),
            pltpu.VMEM((2 * steps * PITCH + 8, WIDTH), F32),
            pltpu.SMEM((GROUPS, 2), F32),
            pltpu.SemaphoreType.DMA((4,)),
        ],
        compiler_params=pltpu.CompilerParams(vmem_limit_bytes=44_500_000),
        name="compose",
    )(noise, retain, retain, control_weight.reshape(-1, WIDTH, WIDTH), input_weight)


def row_kernel(m0, m1, m2, m3, out_ref, held):
    x = places()[1]
    for k, ref in enumerate((m0, m1, m2, m3)):
        held[lax.rem(x + 4 - k, 4)] = ref[...]
    for b in range(2):
        parts = []
        for k in range(4):
            matrix, offset, kept = unpack_map(held.at[k], b)
            parts.append((matrix.astype(F32), offset, kept))
        while len(parts) > 1:
            merged = []
            for (m1_, o1, k1), (m2_, o2, k2) in zip(parts[::2], parts[1::2]):
                low = m2_.astype(BF16)
                prod = jnp.dot(m1_.astype(BF16), low, preferred_element_type=F32)
                merged.append((prod + m1_ * k2 + m2_ * k1, row_times(o1, low) + o1 * k2 + o2, k1 * k2))
            parts = merged
        pack_map(out_ref, b, *parts[0])


def row_map(maps):
    return pl.pallas_call(
        row_kernel,
        out_shape=jax.ShapeDtypeStruct((2, MAP_ROWS, WIDTH), BF16),
        in_specs=[VMEM] * 4,
        out_specs=VMEM,
        scratch_shapes=[pltpu.VMEM((4, 2, MAP_ROWS, WIDTH), BF16)],
        compiler_params=pltpu.CompilerParams(vmem_limit_bytes=8_000_000),
        name="row_map",
    )(*maps)


def replay_kernel(kept_ref, init_ref, y1, y2, y3, x1, x2, x3, off_ref, grp_ref, gain_ref, q_ref,
                  states_ref, normed_ref):
    steps = SPAN * GROUPS
    y, x = places()[:2]
    entry = []
    for b in range(2):
        h = init_ref[b : b + 1, :]
        for place, refs in ((y, (y1, y2, y3)), (x, (x1, x2, x3))):
            for k in (3, 2, 1):
                matrix, offset, kept = unpack_map(refs[k - 1], b)
                h = jnp.where(k <= place, h * kept + row_times(h, matrix) + offset, h)
        entry.append(h)

    def group(g, starts):
        after = []
        for b in range(2):
            c = g * 2 + b
            h = starts[b]
            spread = jnp.broadcast_to(h, (WIDTH, WIDTH)).T
            last = off_ref[pl.ds(b * steps + g * SPAN + SPAN - 1, 1), :]
            parts = two_parts(h)
            moved = h * kept_ref[pl.ds(c, 1), :] + parts_times(parts, grp_ref[c])
            after.append(moved + last)
            rows = [jnp.sum(q_ref[s, c].astype(F32) * spread, axis=0, keepdims=True) for s in range(VECTOR_STEPS)]
            for s in range(VECTOR_STEPS, SPAN - 1, 2):
                pair = parts_times(parts, jnp.concatenate([q_ref[s, c], q_ref[s + 1, c]], axis=1))
                rows += [pair[:, :WIDTH], pair[:, WIDTH:]]
            rows.append(moved)
            base = pl.multiple_of(g * SPAN, SPAN)
            states = jnp.concatenate(rows, axis=0) + off_ref[pl.ds(b * steps + base, SPAN), :]
            states_ref[pl.ds(base, SPAN), b * WIDTH : (b + 1) * WIDTH] = states
            mean = jnp.mean(states * states, axis=-1, keepdims=True)
            normed = states * lax.rsqrt(mean + 1e-05) * gain_ref[b : b + 1, :]
            normed_ref[pl.ds(base, SPAN), b * WIDTH : (b + 1) * WIDTH] = normed.astype(BF16)
        return tuple(after)

    lax.fori_loop(0, GROUPS, group, tuple(entry), unroll=8)


def replay(kept, init, y_maps, x_maps, off, grp, gain, q):
    steps = SPAN * GROUPS
    return pl.pallas_call(
        replay_kernel,
        out_shape=(
            jax.ShapeDtypeStruct((steps, 2 * WIDTH), F32),
            jax.ShapeDtypeStruct((steps, 2 * WIDTH), BF16),
        ),
        in_specs=[VMEM] * 12,
        out_specs=(VMEM, VMEM),
        compiler_params=pltpu.CompilerParams(vmem_limit_bytes=16_000_000),
        name="replay",
    )(kept, init, *y_maps, *x_maps, off, grp, gain, pltpu.with_memory_space_constraint(q, pltpu.VMEM))


def forward_kernel(m0, m1, m3, m2, theirs_ref, gate_ref, up_ref, down_ref, send_ref, hidden):
    z, core = places()[2:]
    wide = 2 * WIDTH

    def at(k, c):
        return pl.multiple_of((lax.rem(z + k, 4) * 2 + c) * wide, wide)

    parts = [(m0, 0, 0), (m1, 3, 0), (m2, 2, 0), (m3, 1, 0)]
    parts += [(theirs_ref.at[i], (4 - k) % 4, 1) for i, k in enumerate((0, 1, 3, 2))]
    for n in range(0, gate_ref.shape[1], wide):
        gate = up = None
        for ref, k, other in parts:
            chunk = ref[...]
            row = at(k, 1 - core if other else core)
            g = jnp.dot(chunk, gate_ref[pl.ds(row, wide), n : n + wide], preferred_element_type=F32)
            u = jnp.dot(chunk, up_ref[pl.ds(row, wide), n : n + wide], preferred_element_type=F32)
            gate = g if gate is None else gate + g
            up = u if up is None else up + u
        hidden[:, n : n + wide] = (gate / (1.0 + jnp.exp(-gate)) * up).astype(BF16)
    for k in range(4):
        columns = down_ref[:, pl.ds(at(k, 1 - core), wide)]
        send_ref[k] = jnp.dot(hidden[...], columns, preferred_element_type=F32).astype(BF16)


def keep_kernel(hidden, down_ref, keep_ref):
    z, core = places()[2:]
    wide = 2 * WIDTH
    for k in range(4):
        columns = down_ref[:, pl.ds(pl.multiple_of((lax.rem(z + k, 4) * 2 + core) * wide, wide), wide)]
        keep_ref[k] = jnp.dot(hidden[...], columns, preferred_element_type=F32)


def forward(mine, theirs, gate_weight, up_weight, down_weight):
    steps, units = mine[0].shape[0], gate_weight.shape[1]
    weights = [pltpu.with_memory_space_constraint(w, pltpu.VMEM) for w in (gate_weight, up_weight, down_weight)]
    params = pltpu.CompilerParams(vmem_limit_bytes=16_000_000)
    sent, hidden = pl.pallas_call(
        forward_kernel,
        out_shape=(pltpu.VMEM((4, steps, 2 * WIDTH), BF16), pltpu.VMEM((steps, units), BF16)),
        in_specs=[VMEM] * 8,
        out_specs=(VMEM, VMEM),
        compiler_params=params,
        name="forward",
    )(*mine, theirs, *weights)
    kept = pl.pallas_call(
        keep_kernel,
        out_shape=pltpu.VMEM((4, steps, 2 * WIDTH), F32),
        in_specs=[VMEM] * 2,
        out_specs=VMEM,
        compiler_params=params,
        name="keep",
    )(hidden, weights[2])
    return kept, sent


def x_back(v, k):
    return lax.ppermute(v, "tm", [(y * 4 + x, y * 4 + (x + k) % 4) for y in range(4) for x in range(4)])


def y_back(v, k):
    return lax.ppermute(v, "tm", [(y * 4 + x, (y + k) % 4 * 4 + x) for y in range(4) for x in range(4)])


def z_back(v, k):
    return lax.ppermute(v, "block", [(z * 2 + c, (z + k) % 4 * 2 + c) for z in range(4) for c in range(2)])


def other_core(v):
    return lax.ppermute(v, "block", [(s, s ^ 1) for s in range(8)])


def body(
    noise,
    retain,
    control_weight,
    input_weight,
    initial_state,
    norm_gain,
    gate_weight,
    up_weight,
    down_weight,
):
    q, off, own, grp, kept = compose(noise.T, retain.T, control_weight, input_weight)
    x_maps = [x_back(own, k) for k in (1, 2, 3)]
    total = row_map([own, *x_maps])
    y_maps = [y_back(total, k) for k in (1, 2, 3)]
    states, normed = replay(
        kept, initial_state.reshape(2, WIDTH), y_maps, x_maps, off, grp, norm_gain.reshape(2, WIDTH), q
    )
    mine = [normed] + [z_back(normed, k) for k in (1, 3, 2)]
    theirs = other_core(jnp.stack(mine))
    keep, sent = forward(mine, theirs, gate_weight, up_weight, down_weight)
    chip = keep + other_core(sent).astype(F32)
    low = chip.astype(BF16)
    mixed = chip[0]
    for k in (2, 1, 3):
        mixed = mixed + z_back(low[k], k).astype(F32)
    return (states + mixed).astype(BF16)


def solution(mesh):
    placed = (
        P("tm", None),
        P("tm", "block"),
        P(None, "block", None, None),
        P(None, "block"),
        P("block"),
        P("block"),
        P(None, "block"),
        P(None, "block"),
        P("block", None),
    )
    return jax.shard_map(body, mesh=mesh, in_specs=placed, out_specs=P("tm", "block"), check_vma=False)
```

```python
import functools
import math

import jax
import jax.numpy as jnp
from jax import lax
from jax.experimental import pallas as pl
from jax.experimental.pallas import tpu as pltpu
from jax.sharding import PartitionSpec as P

F32 = jnp.float32
BF16 = jnp.bfloat16
GROUPS = 16
SPAN = 16
WIDTH = 128
ROWS = 144
VECTOR_STEPS = 5
CHIPS = (0, 2, 3, 1)
PITCH = 129
MAP_ROWS = 144
VMEM = pl.BlockSpec(memory_space=pltpu.VMEM)
SMEM = pl.BlockSpec(memory_space=pltpu.SMEM)
ANY = pl.BlockSpec(memory_space=pl.ANY)


def split3(v):
    hi = v.astype(BF16)
    rest = v - hi.astype(F32)
    mid = rest.astype(BF16)
    return hi, mid, (rest - mid.astype(F32)).astype(BF16)


def pack_map(ref, b, matrix, offset, kept):
    ref[b, :WIDTH, :] = matrix.astype(BF16)
    row = lax.broadcasted_iota(jnp.int32, (16, WIDTH), 0)
    tail = jnp.zeros((16, WIDTH), F32)
    kept_row = jnp.full((1, WIDTH), 1.0, F32) * kept
    for k, part in enumerate((*split3(offset), *split3(kept_row))):
        tail = jnp.where(row == k, jnp.broadcast_to(part.astype(F32), (16, WIDTH)), tail)
    ref[b, WIDTH:, :] = tail.astype(BF16)


def unpack_map(ref, b):
    matrix = ref[b, :WIDTH, :]
    tail = ref[b, WIDTH:, :].astype(F32)
    offset = tail[0:1] + tail[1:2] + tail[2:3]
    kept = tail[3:4] + tail[4:5] + tail[5:6]
    return matrix, offset, kept


def two_parts(h):
    row = lax.broadcasted_iota(jnp.int32, (16, WIDTH), 0)
    hi = h.astype(BF16).astype(F32)
    lo = h - hi
    return jnp.where(
        row == 0, jnp.broadcast_to(hi, (16, WIDTH)), jnp.broadcast_to(lo, (16, WIDTH))
    ).astype(BF16)


def parts_times(parts, matrix):
    out = jnp.dot(parts, matrix, preferred_element_type=F32)
    return out[0:1] + out[1:2]


def row_times(h, matrix):
    return parts_times(two_parts(h), matrix)


def places():
    tm, block = lax.axis_index("tm"), lax.axis_index("block")
    return lax.div(tm, 4), lax.rem(tm, 4), lax.div(block, 2), lax.rem(block, 2)


def compose_kernel(
    noise_ref, retain_s, retain_ref, cw_ref, iw_ref, q_ref, off_ref, send_ref, grp_ref, kept_ref, skw, am, kept_s, sem
):
    steps = noise_ref.shape[1]
    loads = [
        pltpu.make_async_copy(cw_ref.at[pl.ds(32 * k, 32)], q_ref.at[k], sem.at[k]) for k in range(4)
    ]
    for load in loads:
        load.start()
    rows = lax.broadcasted_iota(jnp.int32, (WIDTH, WIDTH), 0)
    cols = lax.broadcasted_iota(jnp.int32, (WIDTH, WIDTH), 1)
    eye = (rows == cols).astype(F32)
    noise = noise_ref[...].T
    drive = jnp.dot(noise, iw_ref[...], precision=lax.Precision.HIGHEST, preferred_element_type=F32)
    kept = retain_ref[...]
    scale = jnp.sqrt(1.0 - kept * kept)
    for b in range(2):
        spread = jnp.broadcast_to(scale[b : b + 1, :], (WIDTH, steps)).T
        off_ref[b * steps : (b + 1) * steps, :] = drive[:, b * WIDTH : (b + 1) * WIDTH] * spread

    def skew_body(base, i, carry):
        for b in range(2):
            raw = q_ref[base // 16, i * 2 + b]
            diff = (raw.T.astype(F32) - raw.astype(F32)) * (1.0 / math.sqrt(2.0))
            skw[pl.ds((b * 64 + base + i) * PITCH, WIDTH), :] = diff
        return carry

    for k in range(4):
        loads[k].wait()
        lax.fori_loop(0, 16, functools.partial(skew_body, 16 * k), 0, unroll=8)
    low = (noise.astype(BF16).astype(F32) * (1.0 / 64.0)).astype(BF16)

    def build_body(j, carry):
        w = jnp.concatenate(
            [skw[pl.ds(b * 64 * PITCH + j, 64, stride=PITCH), :] for b in range(2)], axis=1
        ).astype(BF16)
        out = jnp.dot(low, w, preferred_element_type=F32)
        for b in range(2):
            am[pl.ds(b * steps * PITCH + j, steps, stride=PITCH), :] = out[:, b * WIDTH : (b + 1) * WIDTH]
        return carry

    lax.fori_loop(0, WIDTH, build_body, 0, unroll=16)
    tail_rows = ROWS - WIDTH
    tail_row = lax.broadcasted_iota(jnp.int32, (tail_rows, WIDTH), 0)
    zero = jnp.zeros((WIDTH, WIDTH), BF16)

    def run(c):
        return skw.at[pl.ds(pl.multiple_of(c * ROWS, 16), ROWS), :]

    def step_matrix(t, b):
        return am[pl.ds((b * steps + t) * PITCH, WIDTH), :]

    def finish(s, g, b, matrix, tail):
        t = g * SPAN + s
        c = g * 2 + b
        rate = retain_s[b, t]
        push = off_ref[pl.ds(b * steps + t, 1), :]
        matrix = matrix * rate
        placed = jnp.where(tail_row == 0, jnp.broadcast_to(push, (tail_rows, WIDTH)), 0.0)
        tail = placed if tail is None else tail * rate + placed
        run(c)[:WIDTH, :] = matrix
        run(c)[WIDTH:, :] = tail
        q_ref[s, c] = matrix.astype(BF16)
        off_ref[pl.ds(b * steps + t, 1), :] = tail[:1]
        return rate

    def first(g, carry):
        for b in range(2):
            kept_s[g, b] = finish(0, g, b, eye + step_matrix(g * SPAN, b), None)
        return carry

    lax.fori_loop(0, GROUPS, first, 0, unroll=4)

    def step(s, carry):
        def group(g, inner):
            t = g * SPAN + s
            now = [run(g * 2 + b)[...] for b in range(2)]
            low0, low1 = [step_matrix(t, b).astype(BF16) for b in range(2)]
            w = jnp.concatenate(
                [jnp.concatenate([low0, zero], axis=1), jnp.concatenate([zero, low1], axis=1)], axis=0
            )
            both = jnp.concatenate([x.astype(BF16) for x in now], axis=1)
            turned = jnp.dot(both, w, preferred_element_type=F32)
            for b in range(2):
                y = now[b] + turned[:, b * WIDTH : (b + 1) * WIDTH]
                rate = finish(s, g, b, y[:WIDTH], y[WIDTH:])
                kept_s[g, b] = kept_s[g, b] * rate
            return inner

        lax.fori_loop(0, GROUPS, group, 0, unroll=16)
        return carry

    lax.fori_loop(1, SPAN, step, 0)

    keeps = [[kept_s[g, b] for b in range(2)] for g in range(GROUPS)]
    for g in range(GROUPS):
        for b in range(2):
            c = g * 2 + b
            m = run(c)[:WIDTH, :] - eye * keeps[g][b]
            run(c)[:WIDTH, :] = m
            grp_ref[c] = m.astype(BF16)
            kept_ref[c : c + 1, :] = jnp.full((1, WIDTH), 1.0, F32) * keeps[g][b]
    stride = 1
    while stride < GROUPS:
        for g1 in range(0, GROUPS, 2 * stride):
            g2 = g1 + stride
            for b in range(2):
                one, two = run(g1 * 2 + b)[...], run(g2 * 2 + b)[...]
                prod = jnp.dot(one.astype(BF16), two[:WIDTH].astype(BF16), preferred_element_type=F32)
                k1, k2 = keeps[g1][b], keeps[g2][b]
                run(g1 * 2 + b)[:WIDTH, :] = prod[:WIDTH] + one[:WIDTH] * k2 + two[:WIDTH] * k1
                run(g1 * 2 + b)[WIDTH:, :] = prod[WIDTH:] + one[WIDTH:] * k2 + two[WIDTH:]
                keeps[g1][b] = k1 * k2
        stride *= 2
    for b in range(2):
        pack_map(send_ref, b, run(b)[:WIDTH, :], run(b)[WIDTH : WIDTH + 1, :], keeps[0][b])


def compose(noise, retain, control_weight, input_weight):
    steps = noise.shape[1]
    return pl.pallas_call(
        compose_kernel,
        out_shape=(
            pltpu.VMEM((SPAN, 2 * GROUPS, WIDTH, WIDTH), BF16),
            pltpu.VMEM((2 * steps, WIDTH), F32),
            pltpu.VMEM((2, MAP_ROWS, WIDTH), BF16),
            pltpu.VMEM((2 * GROUPS, WIDTH, WIDTH), BF16),
            pltpu.VMEM((2 * GROUPS, WIDTH), F32),
        ),
        in_specs=[VMEM, SMEM, VMEM, ANY, VMEM],
        out_specs=(VMEM, VMEM, VMEM, VMEM, VMEM),
        scratch_shapes=[
            pltpu.VMEM((128 * PITCH + 8, WIDTH), F32),
            pltpu.VMEM((2 * steps * PITCH + 8, WIDTH), F32),
            pltpu.SMEM((GROUPS, 2), F32),
            pltpu.SemaphoreType.DMA((4,)),
        ],
        compiler_params=pltpu.CompilerParams(vmem_limit_bytes=44_500_000),
        name="compose",
    )(noise, retain, retain, control_weight.reshape(-1, WIDTH, WIDTH), input_weight)


def row_kernel(m0, m1, m2, m3, out_ref, held):
    x = places()[1]
    for k, ref in enumerate((m0, m1, m2, m3)):
        held[lax.rem(x + 4 - k, 4)] = ref[...]
    for b in range(2):
        parts = []
        for k in range(4):
            matrix, offset, kept = unpack_map(held.at[k], b)
            parts.append((matrix.astype(F32), offset, kept))
        while len(parts) > 1:
            merged = []
            for (m1_, o1, k1), (m2_, o2, k2) in zip(parts[::2], parts[1::2]):
                low = m2_.astype(BF16)
                prod = jnp.dot(m1_.astype(BF16), low, preferred_element_type=F32)
                merged.append((prod + m1_ * k2 + m2_ * k1, row_times(o1, low) + o1 * k2 + o2, k1 * k2))
            parts = merged
        pack_map(out_ref, b, *parts[0])


def row_map(maps):
    return pl.pallas_call(
        row_kernel,
        out_shape=jax.ShapeDtypeStruct((2, MAP_ROWS, WIDTH), BF16),
        in_specs=[VMEM] * 4,
        out_specs=VMEM,
        scratch_shapes=[pltpu.VMEM((4, 2, MAP_ROWS, WIDTH), BF16)],
        compiler_params=pltpu.CompilerParams(vmem_limit_bytes=8_000_000),
        name="row_map",
    )(*maps)


def replay_kernel(kept_ref, init_ref, y1, y2, y3, x1, x2, x3, off_ref, grp_ref, gain_ref, q_ref,
                  states_ref, normed_ref):
    steps = SPAN * GROUPS
    y, x = places()[:2]
    entry = []
    for b in range(2):
        h = init_ref[b : b + 1, :]
        for place, refs in ((y, (y1, y2, y3)), (x, (x1, x2, x3))):
            for k in (3, 2, 1):
                matrix, offset, kept = unpack_map(refs[k - 1], b)
                h = jnp.where(k <= place, h * kept + row_times(h, matrix) + offset, h)
        entry.append(h)

    def group(g, starts):
        after = []
        for b in range(2):
            c = g * 2 + b
            h = starts[b]
            spread = jnp.broadcast_to(h, (WIDTH, WIDTH)).T
            last = off_ref[pl.ds(b * steps + g * SPAN + SPAN - 1, 1), :]
            parts = two_parts(h)
            moved = h * kept_ref[pl.ds(c, 1), :] + parts_times(parts, grp_ref[c])
            after.append(moved + last)
            rows = [jnp.sum(q_ref[s, c].astype(F32) * spread, axis=0, keepdims=True) for s in range(VECTOR_STEPS)]
            for s in range(VECTOR_STEPS, SPAN - 1, 2):
                pair = parts_times(parts, jnp.concatenate([q_ref[s, c], q_ref[s + 1, c]], axis=1))
                rows += [pair[:, :WIDTH], pair[:, WIDTH:]]
            rows.append(moved)
            base = pl.multiple_of(g * SPAN, SPAN)
            states = jnp.concatenate(rows, axis=0) + off_ref[pl.ds(b * steps + base, SPAN), :]
            states_ref[pl.ds(base, SPAN), b * WIDTH : (b + 1) * WIDTH] = states
            mean = jnp.mean(states * states, axis=-1, keepdims=True)
            normed = states * lax.rsqrt(mean + 1e-05) * gain_ref[b : b + 1, :]
            normed_ref[pl.ds(base, SPAN), b * WIDTH : (b + 1) * WIDTH] = normed.astype(BF16)
        return tuple(after)

    lax.fori_loop(0, GROUPS, group, tuple(entry), unroll=8)


def replay(kept, init, y_maps, x_maps, off, grp, gain, q):
    steps = SPAN * GROUPS
    return pl.pallas_call(
        replay_kernel,
        out_shape=(
            jax.ShapeDtypeStruct((steps, 2 * WIDTH), F32),
            jax.ShapeDtypeStruct((steps, 2 * WIDTH), BF16),
        ),
        in_specs=[VMEM] * 12,
        out_specs=(VMEM, VMEM),
        compiler_params=pltpu.CompilerParams(vmem_limit_bytes=16_000_000),
        name="replay",
    )(kept, init, *y_maps, *x_maps, off, grp, gain, pltpu.with_memory_space_constraint(q, pltpu.VMEM))


def forward_kernel(m0, m2, m3, m1, theirs_ref, gate_ref, up_ref, down_ref, send_ref, hidden):
    z, core = places()[2:]
    wide = 2 * WIDTH

    def at(k, c):
        return pl.multiple_of((lax.bitwise_xor(z, k) * 2 + c) * wide, wide)

    parts = [(ref, k, 0) for k, ref in zip(CHIPS, (m0, m2, m3, m1))]
    parts += [(theirs_ref.at[i], k, 1) for i, k in enumerate(CHIPS)]
    for n in range(0, gate_ref.shape[1], wide):
        gate = up = None
        for ref, k, other in parts:
            chunk = ref[...]
            row = at(k, 1 - core if other else core)
            g = jnp.dot(chunk, gate_ref[pl.ds(row, wide), n : n + wide], preferred_element_type=F32)
            u = jnp.dot(chunk, up_ref[pl.ds(row, wide), n : n + wide], preferred_element_type=F32)
            gate = g if gate is None else gate + g
            up = u if up is None else up + u
        hidden[:, n : n + wide] = (gate / (1.0 + jnp.exp(-gate)) * up).astype(BF16)
    for k in range(4):
        columns = down_ref[:, pl.ds(at(k, 1 - core), wide)]
        send_ref[k] = jnp.dot(hidden[...], columns, preferred_element_type=F32).astype(BF16)


def keep_kernel(hidden, down_ref, keep_ref):
    z, core = places()[2:]
    wide = 2 * WIDTH
    for k in range(4):
        columns = down_ref[:, pl.ds(pl.multiple_of((lax.bitwise_xor(z, k) * 2 + core) * wide, wide), wide)]
        keep_ref[k] = jnp.dot(hidden[...], columns, preferred_element_type=F32)


def forward(mine, theirs, gate_weight, up_weight, down_weight):
    steps, units = mine[0].shape[0], gate_weight.shape[1]
    weights = [pltpu.with_memory_space_constraint(w, pltpu.VMEM) for w in (gate_weight, up_weight, down_weight)]
    params = pltpu.CompilerParams(vmem_limit_bytes=16_000_000)
    sent, hidden = pl.pallas_call(
        forward_kernel,
        out_shape=(pltpu.VMEM((4, steps, 2 * WIDTH), BF16), pltpu.VMEM((steps, units), BF16)),
        in_specs=[VMEM] * 8,
        out_specs=(VMEM, VMEM),
        compiler_params=params,
        name="forward",
    )(*mine, theirs, *weights)
    kept = pl.pallas_call(
        keep_kernel,
        out_shape=pltpu.VMEM((4, steps, 2 * WIDTH), F32),
        in_specs=[VMEM] * 2,
        out_specs=VMEM,
        compiler_params=params,
        name="keep",
    )(hidden, weights[2])
    return kept, sent


def x_back(v, k):
    return lax.ppermute(v, "tm", [(y * 4 + x, y * 4 + (x + k) % 4) for y in range(4) for x in range(4)])


def y_back(v, k):
    return lax.ppermute(v, "tm", [(y * 4 + x, (y + k) % 4 * 4 + x) for y in range(4) for x in range(4)])


def z_exchange(v, k):
    return lax.ppermute(v, "block", [(z * 2 + c, (z ^ k) * 2 + c) for z in range(4) for c in range(2)])


def other_core(v):
    return lax.ppermute(v, "block", [(s, s ^ 1) for s in range(8)])


def body(
    noise,
    retain,
    control_weight,
    input_weight,
    initial_state,
    norm_gain,
    gate_weight,
    up_weight,
    down_weight,
):
    q, off, own, grp, kept = compose(noise.T, retain.T, control_weight, input_weight)
    x_maps = [x_back(own, k) for k in (1, 2, 3)]
    total = row_map([own, *x_maps])
    y_maps = [y_back(total, k) for k in (1, 2, 3)]
    states, normed = replay(
        kept, initial_state.reshape(2, WIDTH), y_maps, x_maps, off, grp, norm_gain.reshape(2, WIDTH), q
    )
    mine = [normed if k == 0 else z_exchange(normed, k) for k in CHIPS]
    theirs = other_core(jnp.stack(mine))
    keep, sent = forward(mine, theirs, gate_weight, up_weight, down_weight)
    chip = keep + other_core(sent).astype(F32)
    low = chip.astype(BF16)
    mixed = chip[0]
    for k in (1, 2, 3):
        mixed = mixed + z_exchange(low[k], k).astype(F32)
    return (states + mixed).astype(BF16)


def solution(mesh):
    placed = (
        P("tm", None),
        P("tm", "block"),
        P(None, "block", None, None),
        P(None, "block"),
        P("block"),
        P("block"),
        P(None, "block"),
        P(None, "block"),
        P("block", None),
    )
    return jax.shard_map(body, mesh=mesh, in_specs=placed, out_specs=P("tm", "block"), check_vma=False)
```

```python
import functools
import math

import jax
import jax.numpy as jnp
from jax import lax
from jax.experimental import pallas as pl
from jax.experimental.pallas import tpu as pltpu
from jax.sharding import PartitionSpec as P

F32 = jnp.float32
BF16 = jnp.bfloat16
GROUPS = 16
SPAN = 16
WIDTH = 128
ROWS = 144
VECTOR_STEPS = 5
PITCH = 129
MAP_ROWS = 144
VMEM = pl.BlockSpec(memory_space=pltpu.VMEM)
SMEM = pl.BlockSpec(memory_space=pltpu.SMEM)
ANY = pl.BlockSpec(memory_space=pl.ANY)


def split3(v):
    hi = v.astype(BF16)
    rest = v - hi.astype(F32)
    mid = rest.astype(BF16)
    return hi, mid, (rest - mid.astype(F32)).astype(BF16)


def pack_map(ref, b, matrix, offset, kept):
    ref[b, :WIDTH, :] = matrix.astype(BF16)
    row = lax.broadcasted_iota(jnp.int32, (16, WIDTH), 0)
    tail = jnp.zeros((16, WIDTH), F32)
    kept_row = jnp.full((1, WIDTH), 1.0, F32) * kept
    for k, part in enumerate((*split3(offset), *split3(kept_row))):
        tail = jnp.where(row == k, jnp.broadcast_to(part.astype(F32), (16, WIDTH)), tail)
    ref[b, WIDTH:, :] = tail.astype(BF16)


def unpack_map(ref, b):
    matrix = ref[b, :WIDTH, :]
    tail = ref[b, WIDTH:, :].astype(F32)
    offset = tail[0:1] + tail[1:2] + tail[2:3]
    kept = tail[3:4] + tail[4:5] + tail[5:6]
    return matrix, offset, kept


def two_parts(h):
    row = lax.broadcasted_iota(jnp.int32, (16, WIDTH), 0)
    hi = h.astype(BF16).astype(F32)
    lo = h - hi
    return jnp.where(
        row == 0, jnp.broadcast_to(hi, (16, WIDTH)), jnp.broadcast_to(lo, (16, WIDTH))
    ).astype(BF16)


def parts_times(parts, matrix):
    out = jnp.dot(parts, matrix, preferred_element_type=F32)
    return out[0:1] + out[1:2]


def row_times(h, matrix):
    return parts_times(two_parts(h), matrix)


def places():
    tm, block = lax.axis_index("tm"), lax.axis_index("block")
    return lax.div(tm, 4), lax.rem(tm, 4), lax.div(block, 2), lax.rem(block, 2)


def compose_kernel(
    noise_ref, retain_s, retain_ref, cw_ref, iw_ref, q_ref, off_ref, send_ref, grp_ref, kept_ref, skw, am, kept_s, sem
):
    steps = noise_ref.shape[1]
    loads = [
        pltpu.make_async_copy(cw_ref.at[pl.ds(32 * k, 32)], q_ref.at[k], sem.at[k]) for k in range(4)
    ]
    for load in loads:
        load.start()
    rows = lax.broadcasted_iota(jnp.int32, (WIDTH, WIDTH), 0)
    cols = lax.broadcasted_iota(jnp.int32, (WIDTH, WIDTH), 1)
    eye = (rows == cols).astype(F32)
    noise = noise_ref[...].T
    drive = jnp.dot(noise, iw_ref[...], precision=lax.Precision.HIGHEST, preferred_element_type=F32)
    kept = retain_ref[...]
    scale = jnp.sqrt(1.0 - kept * kept)
    for b in range(2):
        spread = jnp.broadcast_to(scale[b : b + 1, :], (WIDTH, steps)).T
        off_ref[b * steps : (b + 1) * steps, :] = drive[:, b * WIDTH : (b + 1) * WIDTH] * spread

    def skew_body(base, i, carry):
        for b in range(2):
            raw = q_ref[base // 16, i * 2 + b]
            diff = (raw.T.astype(F32) - raw.astype(F32)) * (1.0 / math.sqrt(2.0))
            skw[pl.ds((b * 64 + base + i) * PITCH, WIDTH), :] = diff
        return carry

    for k in range(4):
        loads[k].wait()
        lax.fori_loop(0, 16, functools.partial(skew_body, 16 * k), 0, unroll=8)
    low = (noise.astype(BF16).astype(F32) * (1.0 / 64.0)).astype(BF16)

    def build_body(j, carry):
        w = jnp.concatenate(
            [skw[pl.ds(b * 64 * PITCH + j, 64, stride=PITCH), :] for b in range(2)], axis=1
        ).astype(BF16)
        out = jnp.dot(low, w, preferred_element_type=F32)
        for b in range(2):
            am[pl.ds(b * steps * PITCH + j, steps, stride=PITCH), :] = out[:, b * WIDTH : (b + 1) * WIDTH]
        return carry

    lax.fori_loop(0, WIDTH, build_body, 0, unroll=16)
    tail_rows = ROWS - WIDTH
    tail_row = lax.broadcasted_iota(jnp.int32, (tail_rows, WIDTH), 0)
    zero = jnp.zeros((WIDTH, WIDTH), BF16)

    def run(c):
        return skw.at[pl.ds(pl.multiple_of(c * ROWS, 16), ROWS), :]

    def step_matrix(t, b):
        return am[pl.ds((b * steps + t) * PITCH, WIDTH), :]

    def finish(s, g, b, matrix, tail):
        t = g * SPAN + s
        c = g * 2 + b
        rate = retain_s[b, t]
        push = off_ref[pl.ds(b * steps + t, 1), :]
        matrix = matrix * rate
        placed = jnp.where(tail_row == 0, jnp.broadcast_to(push, (tail_rows, WIDTH)), 0.0)
        tail = placed if tail is None else tail * rate + placed
        run(c)[:WIDTH, :] = matrix
        run(c)[WIDTH:, :] = tail
        q_ref[s, c] = matrix.astype(BF16)
        off_ref[pl.ds(b * steps + t, 1), :] = tail[:1]
        return rate

    def first(g, carry):
        for b in range(2):
            kept_s[g, b] = finish(0, g, b, eye + step_matrix(g * SPAN, b), None)
        return carry

    lax.fori_loop(0, GROUPS, first, 0, unroll=4)

    def step(s, carry):
        def group(g, inner):
            t = g * SPAN + s
            now = [run(g * 2 + b)[...] for b in range(2)]
            low0, low1 = [step_matrix(t, b).astype(BF16) for b in range(2)]
            w = jnp.concatenate(
                [jnp.concatenate([low0, zero], axis=1), jnp.concatenate([zero, low1], axis=1)], axis=0
            )
            both = jnp.concatenate([x.astype(BF16) for x in now], axis=1)
            turned = jnp.dot(both, w, preferred_element_type=F32)
            for b in range(2):
                y = now[b] + turned[:, b * WIDTH : (b + 1) * WIDTH]
                rate = finish(s, g, b, y[:WIDTH], y[WIDTH:])
                kept_s[g, b] = kept_s[g, b] * rate
            return inner

        lax.fori_loop(0, GROUPS, group, 0, unroll=16)
        return carry

    lax.fori_loop(1, SPAN, step, 0)

    keeps = [[kept_s[g, b] for b in range(2)] for g in range(GROUPS)]
    for g in range(GROUPS):
        for b in range(2):
            c = g * 2 + b
            m = run(c)[:WIDTH, :] - eye * keeps[g][b]
            run(c)[:WIDTH, :] = m
            grp_ref[c] = m.astype(BF16)
            kept_ref[c : c + 1, :] = jnp.full((1, WIDTH), 1.0, F32) * keeps[g][b]
    stride = 1
    while stride < GROUPS:
        for g1 in range(0, GROUPS, 2 * stride):
            g2 = g1 + stride
            for b in range(2):
                one, two = run(g1 * 2 + b)[...], run(g2 * 2 + b)[...]
                prod = jnp.dot(one.astype(BF16), two[:WIDTH].astype(BF16), preferred_element_type=F32)
                k1, k2 = keeps[g1][b], keeps[g2][b]
                run(g1 * 2 + b)[:WIDTH, :] = prod[:WIDTH] + one[:WIDTH] * k2 + two[:WIDTH] * k1
                run(g1 * 2 + b)[WIDTH:, :] = prod[WIDTH:] + one[WIDTH:] * k2 + two[WIDTH:]
                keeps[g1][b] = k1 * k2
        stride *= 2
    for b in range(2):
        pack_map(send_ref, b, run(b)[:WIDTH, :], run(b)[WIDTH : WIDTH + 1, :], keeps[0][b])


def compose(noise, retain, control_weight, input_weight):
    steps = noise.shape[1]
    return pl.pallas_call(
        compose_kernel,
        out_shape=(
            pltpu.VMEM((SPAN, 2 * GROUPS, WIDTH, WIDTH), BF16),
            pltpu.VMEM((2 * steps, WIDTH), F32),
            pltpu.VMEM((2, MAP_ROWS, WIDTH), BF16),
            pltpu.VMEM((2 * GROUPS, WIDTH, WIDTH), BF16),
            pltpu.VMEM((2 * GROUPS, WIDTH), F32),
        ),
        in_specs=[VMEM, SMEM, VMEM, ANY, VMEM],
        out_specs=(VMEM, VMEM, VMEM, VMEM, VMEM),
        scratch_shapes=[
            pltpu.VMEM((128 * PITCH + 8, WIDTH), F32),
            pltpu.VMEM((2 * steps * PITCH + 8, WIDTH), F32),
            pltpu.SMEM((GROUPS, 2), F32),
            pltpu.SemaphoreType.DMA((4,)),
        ],
        compiler_params=pltpu.CompilerParams(vmem_limit_bytes=44_500_000),
        name="compose",
    )(noise, retain, retain, control_weight.reshape(-1, WIDTH, WIDTH), input_weight)


def row_kernel(m0, m1, m2, m3, out_ref, held):
    x = places()[1]
    for k, ref in enumerate((m0, m1, m2, m3)):
        held[lax.rem(x + 4 - k, 4)] = ref[...]
    for b in range(2):
        parts = []
        for k in range(4):
            matrix, offset, kept = unpack_map(held.at[k], b)
            parts.append((matrix.astype(F32), offset, kept))
        while len(parts) > 1:
            merged = []
            for (m1_, o1, k1), (m2_, o2, k2) in zip(parts[::2], parts[1::2]):
                low = m2_.astype(BF16)
                prod = jnp.dot(m1_.astype(BF16), low, preferred_element_type=F32)
                merged.append((prod + m1_ * k2 + m2_ * k1, row_times(o1, low) + o1 * k2 + o2, k1 * k2))
            parts = merged
        pack_map(out_ref, b, *parts[0])


def row_map(maps):
    return pl.pallas_call(
        row_kernel,
        out_shape=jax.ShapeDtypeStruct((2, MAP_ROWS, WIDTH), BF16),
        in_specs=[VMEM] * 4,
        out_specs=VMEM,
        scratch_shapes=[pltpu.VMEM((4, 2, MAP_ROWS, WIDTH), BF16)],
        compiler_params=pltpu.CompilerParams(vmem_limit_bytes=8_000_000),
        name="row_map",
    )(*maps)


def replay_kernel(kept_ref, init_ref, y1, y2, y3, x1, x2, x3, off_ref, grp_ref, gain_ref, q_ref,
                  states_ref, normed_ref):
    steps = SPAN * GROUPS
    y, x = places()[:2]
    entry = []
    for b in range(2):
        h = init_ref[b : b + 1, :]
        for place, refs in ((y, (y1, y2, y3)), (x, (x1, x2, x3))):
            for k in (3, 2, 1):
                matrix, offset, kept = unpack_map(refs[k - 1], b)
                h = jnp.where(k <= place, h * kept + row_times(h, matrix) + offset, h)
        entry.append(h)

    def group(g, starts):
        after = []
        for b in range(2):
            c = g * 2 + b
            h = starts[b]
            spread = jnp.broadcast_to(h, (WIDTH, WIDTH)).T
            last = off_ref[pl.ds(b * steps + g * SPAN + SPAN - 1, 1), :]
            parts = two_parts(h)
            moved = h * kept_ref[pl.ds(c, 1), :] + parts_times(parts, grp_ref[c])
            after.append(moved + last)
            rows = [jnp.sum(q_ref[s, c].astype(F32) * spread, axis=0, keepdims=True) for s in range(VECTOR_STEPS)]
            for s in range(VECTOR_STEPS, SPAN - 1, 2):
                pair = parts_times(parts, jnp.concatenate([q_ref[s, c], q_ref[s + 1, c]], axis=1))
                rows += [pair[:, :WIDTH], pair[:, WIDTH:]]
            rows.append(moved)
            base = pl.multiple_of(g * SPAN, SPAN)
            states = jnp.concatenate(rows, axis=0) + off_ref[pl.ds(b * steps + base, SPAN), :]
            states_ref[pl.ds(base, SPAN), b * WIDTH : (b + 1) * WIDTH] = states
            mean = jnp.mean(states * states, axis=-1, keepdims=True)
            normed = states * lax.rsqrt(mean + 1e-05) * gain_ref[b : b + 1, :]
            normed_ref[pl.ds(base, SPAN), b * WIDTH : (b + 1) * WIDTH] = normed.astype(BF16)
        return tuple(after)

    lax.fori_loop(0, GROUPS, group, tuple(entry), unroll=8)


def replay(kept, init, y_maps, x_maps, off, grp, gain, q):
    steps = SPAN * GROUPS
    return pl.pallas_call(
        replay_kernel,
        out_shape=(
            jax.ShapeDtypeStruct((steps, 2 * WIDTH), F32),
            jax.ShapeDtypeStruct((steps, 2 * WIDTH), BF16),
        ),
        in_specs=[VMEM] * 12,
        out_specs=(VMEM, VMEM),
        compiler_params=pltpu.CompilerParams(vmem_limit_bytes=16_000_000),
        name="replay",
    )(kept, init, *y_maps, *x_maps, off, grp, gain, pltpu.with_memory_space_constraint(q, pltpu.VMEM))


def weight_rows(k, c):
    z = places()[2]
    return pl.multiple_of((lax.rem(z + k, 4) * 2 + c) * 2 * WIDTH, 2 * WIDTH)


def products(parts, gate_ref, up_ref, n):
    wide = 2 * WIDTH
    gate = up = None
    for ref, row in parts:
        chunk = ref[...]
        g = jnp.dot(chunk, gate_ref[pl.ds(row, wide), n : n + wide], preferred_element_type=F32)
        u = jnp.dot(chunk, up_ref[pl.ds(row, wide), n : n + wide], preferred_element_type=F32)
        gate = g if gate is None else gate + g
        up = u if up is None else up + u
    return gate, up


AHEAD = (0, 3, 1, 2)


def mine_kernel(m0, m1, m3, m2, gate_ref, up_ref, gate_out, up_out):
    core = places()[3]
    parts = [(ref, weight_rows(k, core)) for ref, k in zip((m0, m1, m3, m2), AHEAD)]
    wide = 2 * WIDTH
    for n in range(0, gate_ref.shape[1], wide):
        gate_out[:, n : n + wide], up_out[:, n : n + wide] = products(parts, gate_ref, up_ref, n)


def forward_kernel(theirs_ref, gate_in, up_in, gate_ref, up_ref, down_ref, send_ref, hidden):
    core = places()[3]
    parts = [(theirs_ref.at[i], weight_rows(k, 1 - core)) for i, k in enumerate(AHEAD)]
    wide = 2 * WIDTH
    for n in range(0, gate_ref.shape[1], wide):
        gate, up = products(parts, gate_ref, up_ref, n)
        gate = gate + gate_in[:, n : n + wide]
        up = up + up_in[:, n : n + wide]
        hidden[:, n : n + wide] = (gate / (1.0 + jnp.exp(-gate)) * up).astype(BF16)
    for k in range(4):
        columns = down_ref[:, pl.ds(weight_rows(k, 1 - core), wide)]
        send_ref[k] = jnp.dot(hidden[...], columns, preferred_element_type=F32).astype(BF16)


def keep_kernel(hidden, down_ref, keep_ref):
    core = places()[3]
    for k in range(4):
        columns = down_ref[:, pl.ds(weight_rows(k, core), 2 * WIDTH)]
        keep_ref[k] = jnp.dot(hidden[...], columns, preferred_element_type=F32)


def forward(mine, gate_weight, up_weight, down_weight):
    steps, units = mine[0].shape[0], gate_weight.shape[1]
    gate_weight, up_weight, down_weight = [
        pltpu.with_memory_space_constraint(w, pltpu.VMEM) for w in (gate_weight, up_weight, down_weight)
    ]
    params = pltpu.CompilerParams(vmem_limit_bytes=16_000_000)
    theirs = other_core(jnp.stack(mine))
    part = pltpu.VMEM((steps, units), F32)
    gate, up = pl.pallas_call(
        mine_kernel,
        out_shape=(part, part),
        in_specs=[VMEM] * 6,
        out_specs=(VMEM, VMEM),
        compiler_params=params,
        name="mine",
    )(*mine, gate_weight, up_weight)
    sent, hidden = pl.pallas_call(
        forward_kernel,
        out_shape=(pltpu.VMEM((4, steps, 2 * WIDTH), BF16), pltpu.VMEM((steps, units), BF16)),
        in_specs=[VMEM] * 6,
        out_specs=(VMEM, VMEM),
        compiler_params=params,
        name="forward",
    )(theirs, gate, up, gate_weight, up_weight, down_weight)
    kept = pl.pallas_call(
        keep_kernel,
        out_shape=pltpu.VMEM((4, steps, 2 * WIDTH), F32),
        in_specs=[VMEM] * 2,
        out_specs=VMEM,
        compiler_params=params,
        name="keep",
    )(hidden, down_weight)
    return kept, sent


def x_back(v, k):
    return lax.ppermute(v, "tm", [(y * 4 + x, y * 4 + (x + k) % 4) for y in range(4) for x in range(4)])


def y_back(v, k):
    return lax.ppermute(v, "tm", [(y * 4 + x, (y + k) % 4 * 4 + x) for y in range(4) for x in range(4)])


def z_back(v, k):
    return lax.ppermute(v, "block", [(z * 2 + c, (z + k) % 4 * 2 + c) for z in range(4) for c in range(2)])


def other_core(v):
    return lax.ppermute(v, "block", [(s, s ^ 1) for s in range(8)])


def body(
    noise,
    retain,
    control_weight,
    input_weight,
    initial_state,
    norm_gain,
    gate_weight,
    up_weight,
    down_weight,
):
    q, off, own, grp, kept = compose(noise.T, retain.T, control_weight, input_weight)
    x_maps = [x_back(own, k) for k in (1, 2, 3)]
    total = row_map([own, *x_maps])
    y_maps = [y_back(total, k) for k in (1, 2, 3)]
    states, normed = replay(
        kept, initial_state.reshape(2, WIDTH), y_maps, x_maps, off, grp, norm_gain.reshape(2, WIDTH), q
    )
    mine = [normed] + [z_back(normed, k) for k in (1, 3, 2)]
    keep, sent = forward(mine, gate_weight, up_weight, down_weight)
    chip = keep + other_core(sent).astype(F32)
    low = chip.astype(BF16)
    mixed = chip[0]
    for k in (2, 1, 3):
        mixed = mixed + z_back(low[k], k).astype(F32)
    return (states + mixed).astype(BF16)


def solution(mesh):
    placed = (
        P("tm", None),
        P("tm", "block"),
        P(None, "block", None, None),
        P(None, "block"),
        P("block"),
        P("block"),
        P(None, "block"),
        P(None, "block"),
        P("block", None),
    )
    return jax.shard_map(body, mesh=mesh, in_specs=placed, out_specs=P("tm", "block"), check_vma=False)
```

```python
import functools
import math

import jax
import jax.numpy as jnp
from jax import lax
from jax.experimental import pallas as pl
from jax.experimental.pallas import tpu as pltpu
from jax.sharding import PartitionSpec as P

F32 = jnp.float32
BF16 = jnp.bfloat16
GROUPS = 16
SPAN = 16
WIDTH = 128
ROWS = 144
VECTOR_STEPS = 5
PITCH = 129
MAP_ROWS = 144
VMEM = pl.BlockSpec(memory_space=pltpu.VMEM)
SMEM = pl.BlockSpec(memory_space=pltpu.SMEM)
ANY = pl.BlockSpec(memory_space=pl.ANY)


def split3(v):
    hi = v.astype(BF16)
    rest = v - hi.astype(F32)
    mid = rest.astype(BF16)
    return hi, mid, (rest - mid.astype(F32)).astype(BF16)


def pack_map(ref, b, matrix, offset, kept):
    ref[b, :WIDTH, :] = matrix.astype(BF16)
    row = lax.broadcasted_iota(jnp.int32, (16, WIDTH), 0)
    tail = jnp.zeros((16, WIDTH), F32)
    kept_row = jnp.full((1, WIDTH), 1.0, F32) * kept
    for k, part in enumerate((*split3(offset), *split3(kept_row))):
        tail = jnp.where(row == k, jnp.broadcast_to(part.astype(F32), (16, WIDTH)), tail)
    ref[b, WIDTH:, :] = tail.astype(BF16)


def unpack_map(ref, b):
    matrix = ref[b, :WIDTH, :]
    tail = ref[b, WIDTH:, :].astype(F32)
    offset = tail[0:1] + tail[1:2] + tail[2:3]
    kept = tail[3:4] + tail[4:5] + tail[5:6]
    return matrix, offset, kept


def two_parts(h):
    row = lax.broadcasted_iota(jnp.int32, (16, WIDTH), 0)
    hi = h.astype(BF16).astype(F32)
    lo = h - hi
    return jnp.where(
        row == 0, jnp.broadcast_to(hi, (16, WIDTH)), jnp.broadcast_to(lo, (16, WIDTH))
    ).astype(BF16)


def parts_times(parts, matrix):
    out = jnp.dot(parts, matrix, preferred_element_type=F32)
    return out[0:1] + out[1:2]


def row_times(h, matrix):
    return parts_times(two_parts(h), matrix)


def places():
    tm, block = lax.axis_index("tm"), lax.axis_index("block")
    return lax.div(tm, 4), lax.rem(tm, 4), lax.div(block, 2), lax.rem(block, 2)


def compose_kernel(
    noise_ref, retain_s, retain_ref, cw_ref, iw_ref, q_ref, off_ref, send_ref, grp_ref, kept_ref, skw, am, kept_s, sem
):
    steps = noise_ref.shape[1]
    loads = [
        pltpu.make_async_copy(cw_ref.at[pl.ds(32 * k, 32)], q_ref.at[k], sem.at[k]) for k in range(4)
    ]
    for load in loads:
        load.start()
    rows = lax.broadcasted_iota(jnp.int32, (WIDTH, WIDTH), 0)
    cols = lax.broadcasted_iota(jnp.int32, (WIDTH, WIDTH), 1)
    eye = (rows == cols).astype(F32)
    noise = noise_ref[...].T
    def drive_rows():
        drive = jnp.dot(noise, iw_ref[...], precision=lax.Precision.HIGHEST, preferred_element_type=F32)
        kept = retain_ref[...]
        scale = jnp.sqrt(1.0 - kept * kept)
        for b in range(2):
            spread = jnp.broadcast_to(scale[b : b + 1, :], (WIDTH, steps)).T
            off_ref[b * steps : (b + 1) * steps, :] = drive[:, b * WIDTH : (b + 1) * WIDTH] * spread

    def skew_body(base, i, carry):
        for b in range(2):
            raw = q_ref[base // 16, i * 2 + b]
            diff = (raw.T.astype(F32) - raw.astype(F32)) * (1.0 / math.sqrt(2.0))
            skw[pl.ds((b * 64 + base + i) * PITCH, WIDTH), :] = diff
        return carry

    for k in range(4):
        loads[k].wait()
        if k == 1:
            drive_rows()
        lax.fori_loop(0, 16, functools.partial(skew_body, 16 * k), 0, unroll=16)
    low = (noise.astype(BF16).astype(F32) * (1.0 / 64.0)).astype(BF16)

    def build_body(j, carry):
        w = jnp.concatenate(
            [skw[pl.ds(b * 64 * PITCH + j, 64, stride=PITCH), :] for b in range(2)], axis=1
        ).astype(BF16)
        out = jnp.dot(low, w, preferred_element_type=F32)
        for b in range(2):
            am[pl.ds(b * steps * PITCH + j, steps, stride=PITCH), :] = out[:, b * WIDTH : (b + 1) * WIDTH]
        return carry

    lax.fori_loop(0, WIDTH, build_body, 0, unroll=32)
    tail_rows = ROWS - WIDTH
    tail_row = lax.broadcasted_iota(jnp.int32, (tail_rows, WIDTH), 0)
    zero = jnp.zeros((WIDTH, WIDTH), BF16)

    def run(c):
        return skw.at[pl.ds(pl.multiple_of(c * ROWS, 16), ROWS), :]

    def step_matrix(t, b):
        return am[pl.ds((b * steps + t) * PITCH, WIDTH), :]

    def finish(s, g, b, matrix, tail):
        t = g * SPAN + s
        c = g * 2 + b
        rate = retain_s[b, t]
        push = off_ref[pl.ds(b * steps + t, 1), :]
        matrix = matrix * rate
        placed = jnp.where(tail_row == 0, jnp.broadcast_to(push, (tail_rows, WIDTH)), 0.0)
        tail = placed if tail is None else tail * rate + placed
        run(c)[:WIDTH, :] = matrix
        run(c)[WIDTH:, :] = tail
        q_ref[s, c] = matrix.astype(BF16)
        off_ref[pl.ds(b * steps + t, 1), :] = tail[:1]
        return rate

    def first(g, carry):
        for b in range(2):
            kept_s[g, b] = finish(0, g, b, eye + step_matrix(g * SPAN, b), None)
        return carry

    lax.fori_loop(0, GROUPS, first, 0, unroll=4)

    def step(s, carry):
        def group(g, inner):
            t = g * SPAN + s
            now = [run(g * 2 + b)[...] for b in range(2)]
            low0, low1 = [step_matrix(t, b).astype(BF16) for b in range(2)]
            w = jnp.concatenate(
                [jnp.concatenate([low0, zero], axis=1), jnp.concatenate([zero, low1], axis=1)], axis=0
            )
            both = jnp.concatenate([x.astype(BF16) for x in now], axis=1)
            turned = jnp.dot(both, w, preferred_element_type=F32)
            for b in range(2):
                y = now[b] + turned[:, b * WIDTH : (b + 1) * WIDTH]
                rate = finish(s, g, b, y[:WIDTH], y[WIDTH:])
                kept_s[g, b] = kept_s[g, b] * rate
            return inner

        lax.fori_loop(0, GROUPS, group, 0, unroll=16)
        return carry

    lax.fori_loop(1, SPAN, step, 0)

    keeps = [[kept_s[g, b] for b in range(2)] for g in range(GROUPS)]
    for g in range(GROUPS):
        for b in range(2):
            c = g * 2 + b
            m = run(c)[:WIDTH, :] - eye * keeps[g][b]
            run(c)[:WIDTH, :] = m
            grp_ref[c] = m.astype(BF16)
            kept_ref[c : c + 1, :] = jnp.full((1, WIDTH), 1.0, F32) * keeps[g][b]
    stride = 1
    while stride < GROUPS:
        for g1 in range(0, GROUPS, 2 * stride):
            g2 = g1 + stride
            for b in range(2):
                one, two = run(g1 * 2 + b)[...], run(g2 * 2 + b)[...]
                prod = jnp.dot(one.astype(BF16), two[:WIDTH].astype(BF16), preferred_element_type=F32)
                k1, k2 = keeps[g1][b], keeps[g2][b]
                run(g1 * 2 + b)[:WIDTH, :] = prod[:WIDTH] + one[:WIDTH] * k2 + two[:WIDTH] * k1
                run(g1 * 2 + b)[WIDTH:, :] = prod[WIDTH:] + one[WIDTH:] * k2 + two[WIDTH:]
                keeps[g1][b] = k1 * k2
        stride *= 2
    for b in range(2):
        pack_map(send_ref, b, run(b)[:WIDTH, :], run(b)[WIDTH : WIDTH + 1, :], keeps[0][b])


def compose(noise, retain, control_weight, input_weight):
    steps = noise.shape[1]
    return pl.pallas_call(
        compose_kernel,
        out_shape=(
            pltpu.VMEM((SPAN, 2 * GROUPS, WIDTH, WIDTH), BF16),
            pltpu.VMEM((2 * steps, WIDTH), F32),
            pltpu.VMEM((2, MAP_ROWS, WIDTH), BF16),
            pltpu.VMEM((2 * GROUPS, WIDTH, WIDTH), BF16),
            pltpu.VMEM((2 * GROUPS, WIDTH), F32),
        ),
        in_specs=[VMEM, SMEM, VMEM, ANY, VMEM],
        out_specs=(VMEM, VMEM, VMEM, VMEM, VMEM),
        scratch_shapes=[
            pltpu.VMEM((128 * PITCH + 8, WIDTH), F32),
            pltpu.VMEM((2 * steps * PITCH + 8, WIDTH), F32),
            pltpu.SMEM((GROUPS, 2), F32),
            pltpu.SemaphoreType.DMA((4,)),
        ],
        compiler_params=pltpu.CompilerParams(vmem_limit_bytes=44_500_000),
        name="compose",
    )(noise, retain, retain, control_weight.reshape(-1, WIDTH, WIDTH), input_weight)


def row_kernel(m0, m1, m2, m3, out_ref, held):
    x = places()[1]
    for k, ref in enumerate((m0, m1, m2, m3)):
        held[lax.rem(x + 4 - k, 4)] = ref[...]
    for b in range(2):
        parts = []
        for k in range(4):
            matrix, offset, kept = unpack_map(held.at[k], b)
            parts.append((matrix.astype(F32), offset, kept))
        while len(parts) > 1:
            merged = []
            for (m1_, o1, k1), (m2_, o2, k2) in zip(parts[::2], parts[1::2]):
                low = m2_.astype(BF16)
                prod = jnp.dot(m1_.astype(BF16), low, preferred_element_type=F32)
                merged.append((prod + m1_ * k2 + m2_ * k1, row_times(o1, low) + o1 * k2 + o2, k1 * k2))
            parts = merged
        pack_map(out_ref, b, *parts[0])


def row_map(maps):
    return pl.pallas_call(
        row_kernel,
        out_shape=jax.ShapeDtypeStruct((2, MAP_ROWS, WIDTH), BF16),
        in_specs=[VMEM] * 4,
        out_specs=VMEM,
        scratch_shapes=[pltpu.VMEM((4, 2, MAP_ROWS, WIDTH), BF16)],
        compiler_params=pltpu.CompilerParams(vmem_limit_bytes=8_000_000),
        name="row_map",
    )(*maps)


def replay_kernel(kept_ref, init_ref, y1, y2, y3, x1, x2, x3, off_ref, grp_ref, gain_ref, q_ref,
                  states_ref, normed_ref):
    steps = SPAN * GROUPS
    y, x = places()[:2]
    entry = []
    for b in range(2):
        h = init_ref[b : b + 1, :]
        for place, refs in ((y, (y1, y2, y3)), (x, (x1, x2, x3))):
            for k in (3, 2, 1):
                matrix, offset, kept = unpack_map(refs[k - 1], b)
                h = jnp.where(k <= place, h * kept + row_times(h, matrix) + offset, h)
        entry.append(h)

    def group(g, starts):
        after = []
        for b in range(2):
            c = g * 2 + b
            h = starts[b]
            spread = jnp.broadcast_to(h, (WIDTH, WIDTH)).T
            last = off_ref[pl.ds(b * steps + g * SPAN + SPAN - 1, 1), :]
            parts = two_parts(h)
            moved = h * kept_ref[pl.ds(c, 1), :] + parts_times(parts, grp_ref[c])
            after.append(moved + last)
            rows = [jnp.sum(q_ref[s, c].astype(F32) * spread, axis=0, keepdims=True) for s in range(VECTOR_STEPS)]
            for s in range(VECTOR_STEPS, SPAN - 1, 2):
                pair = parts_times(parts, jnp.concatenate([q_ref[s, c], q_ref[s + 1, c]], axis=1))
                rows += [pair[:, :WIDTH], pair[:, WIDTH:]]
            rows.append(moved)
            base = pl.multiple_of(g * SPAN, SPAN)
            states = jnp.concatenate(rows, axis=0) + off_ref[pl.ds(b * steps + base, SPAN), :]
            states_ref[pl.ds(base, SPAN), b * WIDTH : (b + 1) * WIDTH] = states
            mean = jnp.mean(states * states, axis=-1, keepdims=True)
            normed = states * lax.rsqrt(mean + 1e-05) * gain_ref[b : b + 1, :]
            normed_ref[pl.ds(base, SPAN), b * WIDTH : (b + 1) * WIDTH] = normed.astype(BF16)
        return tuple(after)

    lax.fori_loop(0, GROUPS, group, tuple(entry), unroll=8)


def replay(kept, init, y_maps, x_maps, off, grp, gain, q):
    steps = SPAN * GROUPS
    return pl.pallas_call(
        replay_kernel,
        out_shape=(
            jax.ShapeDtypeStruct((steps, 2 * WIDTH), F32),
            jax.ShapeDtypeStruct((steps, 2 * WIDTH), BF16),
        ),
        in_specs=[VMEM] * 12,
        out_specs=(VMEM, VMEM),
        compiler_params=pltpu.CompilerParams(vmem_limit_bytes=16_000_000),
        name="replay",
    )(kept, init, *y_maps, *x_maps, off, grp, gain, pltpu.with_memory_space_constraint(q, pltpu.VMEM))


def weight_rows(k, c):
    z = places()[2]
    return pl.multiple_of((lax.rem(z + k, 4) * 2 + c) * 2 * WIDTH, 2 * WIDTH)


def products(parts, gate_ref, up_ref, n):
    wide = 2 * WIDTH
    gate = up = None
    for ref, row in parts:
        chunk = ref[...]
        g = jnp.dot(chunk, gate_ref[pl.ds(row, wide), n : n + wide], preferred_element_type=F32)
        u = jnp.dot(chunk, up_ref[pl.ds(row, wide), n : n + wide], preferred_element_type=F32)
        gate = g if gate is None else gate + g
        up = u if up is None else up + u
    return gate, up


AHEAD = (0, 3, 1, 2)


def mine_kernel(m0, m1, m3, m2, gate_ref, up_ref, gate_out, up_out):
    core = places()[3]
    parts = [(ref, weight_rows(k, core)) for ref, k in zip((m0, m1, m3, m2), AHEAD)]
    wide = 2 * WIDTH
    for n in range(0, gate_ref.shape[1], wide):
        gate_out[:, n : n + wide], up_out[:, n : n + wide] = products(parts, gate_ref, up_ref, n)


def forward_kernel(theirs_ref, gate_in, up_in, gate_ref, up_ref, down_ref, send_ref, hidden):
    core = places()[3]
    parts = [(theirs_ref.at[i], weight_rows(k, 1 - core)) for i, k in enumerate(AHEAD)]
    wide = 2 * WIDTH
    for n in range(0, gate_ref.shape[1], wide):
        gate, up = products(parts, gate_ref, up_ref, n)
        gate = gate + gate_in[:, n : n + wide]
        up = up + up_in[:, n : n + wide]
        hidden[:, n : n + wide] = (gate / (1.0 + jnp.exp(-gate)) * up).astype(BF16)
    for k in range(4):
        columns = down_ref[:, pl.ds(weight_rows(k, 1 - core), wide)]
        send_ref[k] = jnp.dot(hidden[...], columns, preferred_element_type=F32).astype(BF16)


def keep_kernel(hidden, down_ref, keep_ref):
    core = places()[3]
    for k in range(4):
        columns = down_ref[:, pl.ds(weight_rows(k, core), 2 * WIDTH)]
        keep_ref[k] = jnp.dot(hidden[...], columns, preferred_element_type=F32)


def forward(mine, gate_weight, up_weight, down_weight):
    steps, units = mine[0].shape[0], gate_weight.shape[1]
    gate_weight, up_weight, down_weight = [
        pltpu.with_memory_space_constraint(w, pltpu.VMEM) for w in (gate_weight, up_weight, down_weight)
    ]
    params = pltpu.CompilerParams(vmem_limit_bytes=16_000_000)
    theirs = other_core(jnp.stack(mine))
    part = pltpu.VMEM((steps, units), F32)
    gate, up = pl.pallas_call(
        mine_kernel,
        out_shape=(part, part),
        in_specs=[VMEM] * 6,
        out_specs=(VMEM, VMEM),
        compiler_params=params,
        name="mine",
    )(*mine, gate_weight, up_weight)
    sent, hidden = pl.pallas_call(
        forward_kernel,
        out_shape=(pltpu.VMEM((4, steps, 2 * WIDTH), BF16), pltpu.VMEM((steps, units), BF16)),
        in_specs=[VMEM] * 6,
        out_specs=(VMEM, VMEM),
        compiler_params=params,
        name="forward",
    )(theirs, gate, up, gate_weight, up_weight, down_weight)
    kept = pl.pallas_call(
        keep_kernel,
        out_shape=pltpu.VMEM((4, steps, 2 * WIDTH), F32),
        in_specs=[VMEM] * 2,
        out_specs=VMEM,
        compiler_params=params,
        name="keep",
    )(hidden, down_weight)
    return kept, sent


def x_back(v, k):
    return lax.ppermute(v, "tm", [(y * 4 + x, y * 4 + (x + k) % 4) for y in range(4) for x in range(4)])


def y_back(v, k):
    return lax.ppermute(v, "tm", [(y * 4 + x, (y + k) % 4 * 4 + x) for y in range(4) for x in range(4)])


def z_back(v, k):
    return lax.ppermute(v, "block", [(z * 2 + c, (z + k) % 4 * 2 + c) for z in range(4) for c in range(2)])


def other_core(v):
    return lax.ppermute(v, "block", [(s, s ^ 1) for s in range(8)])


def body(
    noise,
    retain,
    control_weight,
    input_weight,
    initial_state,
    norm_gain,
    gate_weight,
    up_weight,
    down_weight,
):
    q, off, own, grp, kept = compose(noise.T, retain.T, control_weight, input_weight)
    x_maps = [x_back(own, k) for k in (1, 2, 3)]
    total = row_map([own, *x_maps])
    y_maps = [y_back(total, k) for k in (1, 2, 3)]
    states, normed = replay(
        kept, initial_state.reshape(2, WIDTH), y_maps, x_maps, off, grp, norm_gain.reshape(2, WIDTH), q
    )
    mine = [normed] + [z_back(normed, k) for k in (1, 3, 2)]
    keep, sent = forward(mine, gate_weight, up_weight, down_weight)
    chip = keep + other_core(sent).astype(F32)
    low = chip.astype(BF16)
    mixed = chip[0]
    for k in (2, 1, 3):
        mixed = mixed + z_back(low[k], k).astype(F32)
    return (states + mixed).astype(BF16)


def solution(mesh):
    placed = (
        P("tm", None),
        P("tm", "block"),
        P(None, "block", None, None),
        P(None, "block"),
        P("block"),
        P("block"),
        P(None, "block"),
        P(None, "block"),
        P("block", None),
    )
    return jax.shard_map(body, mesh=mesh, in_specs=placed, out_specs=P("tm", "block"), check_vma=False)
```

```python
import functools
import math

import jax
import jax.numpy as jnp
from jax import lax
from jax.experimental import pallas as pl
from jax.experimental.pallas import tpu as pltpu
from jax.sharding import PartitionSpec as P

F32 = jnp.float32
BF16 = jnp.bfloat16
GROUPS = 16
SPAN = 16
WIDTH = 128
ROWS = 144
VECTOR_STEPS = 5
PITCH = 129
MAP_ROWS = 144
VMEM = pl.BlockSpec(memory_space=pltpu.VMEM)
SMEM = pl.BlockSpec(memory_space=pltpu.SMEM)
ANY = pl.BlockSpec(memory_space=pl.ANY)


def split3(v):
    hi = v.astype(BF16)
    rest = v - hi.astype(F32)
    mid = rest.astype(BF16)
    return hi, mid, (rest - mid.astype(F32)).astype(BF16)


def pack_map(ref, b, matrix, offset, kept):
    ref[b, :WIDTH, :] = matrix.astype(BF16)
    row = lax.broadcasted_iota(jnp.int32, (16, WIDTH), 0)
    tail = jnp.zeros((16, WIDTH), F32)
    kept_row = jnp.full((1, WIDTH), 1.0, F32) * kept
    for k, part in enumerate((*split3(offset), *split3(kept_row))):
        tail = jnp.where(row == k, jnp.broadcast_to(part.astype(F32), (16, WIDTH)), tail)
    ref[b, WIDTH:, :] = tail.astype(BF16)


def unpack_map(ref, b):
    matrix = ref[b, :WIDTH, :]
    tail = ref[b, WIDTH:, :].astype(F32)
    offset = tail[0:1] + tail[1:2] + tail[2:3]
    kept = tail[3:4] + tail[4:5] + tail[5:6]
    return matrix, offset, kept


def two_parts(h):
    row = lax.broadcasted_iota(jnp.int32, (16, WIDTH), 0)
    hi = h.astype(BF16).astype(F32)
    lo = h - hi
    return jnp.where(
        row == 0, jnp.broadcast_to(hi, (16, WIDTH)), jnp.broadcast_to(lo, (16, WIDTH))
    ).astype(BF16)


def parts_times(parts, matrix):
    out = jnp.dot(parts, matrix, preferred_element_type=F32)
    return out[0:1] + out[1:2]


def row_times(h, matrix):
    return parts_times(two_parts(h), matrix)


def places():
    tm, block = lax.axis_index("tm"), lax.axis_index("block")
    return lax.div(tm, 4), lax.rem(tm, 4), lax.div(block, 2), lax.rem(block, 2)


def compose_kernel(
    noise_ref, retain_s, retain_ref, cw_ref, iw_ref, q_ref, off_ref, send_ref, grp_ref, kept_ref, skw, am, kept_s, sem
):
    steps = noise_ref.shape[1]
    loads = [
        pltpu.make_async_copy(cw_ref.at[pl.ds(32 * k, 32)], q_ref.at[k], sem.at[k]) for k in range(4)
    ]
    for load in loads:
        load.start()
    rows = lax.broadcasted_iota(jnp.int32, (WIDTH, WIDTH), 0)
    cols = lax.broadcasted_iota(jnp.int32, (WIDTH, WIDTH), 1)
    eye = (rows == cols).astype(F32)
    noise = noise_ref[...].T
    def drive_rows():
        drive = jnp.dot(noise, iw_ref[...], precision=lax.Precision.HIGHEST, preferred_element_type=F32)
        kept = retain_ref[...]
        scale = jnp.sqrt(1.0 - kept * kept)
        for b in range(2):
            spread = jnp.broadcast_to(scale[b : b + 1, :], (WIDTH, steps)).T
            off_ref[b * steps : (b + 1) * steps, :] = drive[:, b * WIDTH : (b + 1) * WIDTH] * spread

    def skew_body(base, i, carry):
        for b in range(2):
            raw = q_ref[base // 16, i * 2 + b]
            diff = (raw.T.astype(F32) - raw.astype(F32)) * (1.0 / math.sqrt(2.0))
            skw[pl.ds((b * 64 + base + i) * PITCH, WIDTH), :] = diff
        return carry

    for k in range(4):
        loads[k].wait()
        if k == 1:
            drive_rows()
        lax.fori_loop(0, 16, functools.partial(skew_body, 16 * k), 0, unroll=16)
    low = (noise.astype(BF16).astype(F32) * (1.0 / 64.0)).astype(BF16)

    def build_body(j, carry):
        w = jnp.concatenate(
            [skw[pl.ds(b * 64 * PITCH + j, 64, stride=PITCH), :] for b in range(2)], axis=1
        ).astype(BF16)
        out = jnp.dot(low, w, preferred_element_type=F32)
        for b in range(2):
            am[pl.ds(b * steps * PITCH + j, steps, stride=PITCH), :] = out[:, b * WIDTH : (b + 1) * WIDTH]
        return carry

    lax.fori_loop(0, WIDTH, build_body, 0, unroll=64)
    tail_rows = ROWS - WIDTH
    tail_row = lax.broadcasted_iota(jnp.int32, (tail_rows, WIDTH), 0)
    zero = jnp.zeros((WIDTH, WIDTH), BF16)

    def run(c):
        return skw.at[pl.ds(pl.multiple_of(c * ROWS, 16), ROWS), :]

    def step_matrix(t, b):
        return am[pl.ds((b * steps + t) * PITCH, WIDTH), :]

    def finish(s, g, b, matrix, tail):
        t = g * SPAN + s
        c = g * 2 + b
        rate = retain_s[b, t]
        push = off_ref[pl.ds(b * steps + t, 1), :]
        matrix = matrix * rate
        placed = jnp.where(tail_row == 0, jnp.broadcast_to(push, (tail_rows, WIDTH)), 0.0)
        tail = placed if tail is None else tail * rate + placed
        run(c)[:WIDTH, :] = matrix
        run(c)[WIDTH:, :] = tail
        q_ref[s, c] = matrix.astype(BF16)
        off_ref[pl.ds(b * steps + t, 1), :] = tail[:1]
        return rate

    def first(g, carry):
        for b in range(2):
            kept_s[g, b] = finish(0, g, b, eye + step_matrix(g * SPAN, b), None)
        return carry

    lax.fori_loop(0, GROUPS, first, 0, unroll=4)

    def step(s, carry):
        def group(g, inner):
            t = g * SPAN + s
            now = [run(g * 2 + b)[...] for b in range(2)]
            low0, low1 = [step_matrix(t, b).astype(BF16) for b in range(2)]
            w = jnp.concatenate(
                [jnp.concatenate([low0, zero], axis=1), jnp.concatenate([zero, low1], axis=1)], axis=0
            )
            both = jnp.concatenate([x.astype(BF16) for x in now], axis=1)
            turned = jnp.dot(both, w, preferred_element_type=F32)
            for b in range(2):
                y = now[b] + turned[:, b * WIDTH : (b + 1) * WIDTH]
                rate = finish(s, g, b, y[:WIDTH], y[WIDTH:])
                kept_s[g, b] = kept_s[g, b] * rate
            return inner

        lax.fori_loop(0, GROUPS, group, 0, unroll=16)
        return carry

    lax.fori_loop(1, SPAN, step, 0)

    keeps = [[kept_s[g, b] for b in range(2)] for g in range(GROUPS)]
    for g in range(GROUPS):
        for b in range(2):
            c = g * 2 + b
            m = run(c)[:WIDTH, :] - eye * keeps[g][b]
            run(c)[:WIDTH, :] = m
            grp_ref[c] = m.astype(BF16)
            kept_ref[c : c + 1, :] = jnp.full((1, WIDTH), 1.0, F32) * keeps[g][b]
    stride = 1
    while stride < GROUPS:
        for g1 in range(0, GROUPS, 2 * stride):
            g2 = g1 + stride
            for b in range(2):
                one, two = run(g1 * 2 + b)[...], run(g2 * 2 + b)[...]
                prod = jnp.dot(one.astype(BF16), two[:WIDTH].astype(BF16), preferred_element_type=F32)
                k1, k2 = keeps[g1][b], keeps[g2][b]
                run(g1 * 2 + b)[:WIDTH, :] = prod[:WIDTH] + one[:WIDTH] * k2 + two[:WIDTH] * k1
                run(g1 * 2 + b)[WIDTH:, :] = prod[WIDTH:] + one[WIDTH:] * k2 + two[WIDTH:]
                keeps[g1][b] = k1 * k2
        stride *= 2
    for b in range(2):
        pack_map(send_ref, b, run(b)[:WIDTH, :], run(b)[WIDTH : WIDTH + 1, :], keeps[0][b])


def compose(noise, retain, control_weight, input_weight):
    steps = noise.shape[1]
    return pl.pallas_call(
        compose_kernel,
        out_shape=(
            pltpu.VMEM((SPAN, 2 * GROUPS, WIDTH, WIDTH), BF16),
            pltpu.VMEM((2 * steps, WIDTH), F32),
            pltpu.VMEM((2, MAP_ROWS, WIDTH), BF16),
            pltpu.VMEM((2 * GROUPS, WIDTH, WIDTH), BF16),
            pltpu.VMEM((2 * GROUPS, WIDTH), F32),
        ),
        in_specs=[VMEM, SMEM, VMEM, ANY, VMEM],
        out_specs=(VMEM, VMEM, VMEM, VMEM, VMEM),
        scratch_shapes=[
            pltpu.VMEM((128 * PITCH + 8, WIDTH), F32),
            pltpu.VMEM((2 * steps * PITCH + 8, WIDTH), F32),
            pltpu.SMEM((GROUPS, 2), F32),
            pltpu.SemaphoreType.DMA((4,)),
        ],
        compiler_params=pltpu.CompilerParams(vmem_limit_bytes=44_500_000),
        name="compose",
    )(noise, retain, retain, control_weight.reshape(-1, WIDTH, WIDTH), input_weight)


def row_kernel(m0, m1, m2, m3, out_ref, held):
    x = places()[1]
    for k, ref in enumerate((m0, m1, m2, m3)):
        held[lax.rem(x + 4 - k, 4)] = ref[...]
    for b in range(2):
        parts = []
        for k in range(4):
            matrix, offset, kept = unpack_map(held.at[k], b)
            parts.append((matrix.astype(F32), offset, kept))
        while len(parts) > 1:
            merged = []
            for (m1_, o1, k1), (m2_, o2, k2) in zip(parts[::2], parts[1::2]):
                low = m2_.astype(BF16)
                prod = jnp.dot(m1_.astype(BF16), low, preferred_element_type=F32)
                merged.append((prod + m1_ * k2 + m2_ * k1, row_times(o1, low) + o1 * k2 + o2, k1 * k2))
            parts = merged
        pack_map(out_ref, b, *parts[0])


def row_map(maps):
    return pl.pallas_call(
        row_kernel,
        out_shape=jax.ShapeDtypeStruct((2, MAP_ROWS, WIDTH), BF16),
        in_specs=[VMEM] * 4,
        out_specs=VMEM,
        scratch_shapes=[pltpu.VMEM((4, 2, MAP_ROWS, WIDTH), BF16)],
        compiler_params=pltpu.CompilerParams(vmem_limit_bytes=8_000_000),
        name="row_map",
    )(*maps)


def replay_kernel(kept_ref, init_ref, y1, y2, y3, x1, x2, x3, off_ref, grp_ref, gain_ref, q_ref,
                  states_ref, normed_ref):
    steps = SPAN * GROUPS
    y, x = places()[:2]
    entry = []
    for b in range(2):
        h = init_ref[b : b + 1, :]
        for place, refs in ((y, (y1, y2, y3)), (x, (x1, x2, x3))):
            for k in (3, 2, 1):
                matrix, offset, kept = unpack_map(refs[k - 1], b)
                h = jnp.where(k <= place, h * kept + row_times(h, matrix) + offset, h)
        entry.append(h)

    def group(g, starts):
        after = []
        for b in range(2):
            c = g * 2 + b
            h = starts[b]
            spread = jnp.broadcast_to(h, (WIDTH, WIDTH)).T
            last = off_ref[pl.ds(b * steps + g * SPAN + SPAN - 1, 1), :]
            parts = two_parts(h)
            moved = h * kept_ref[pl.ds(c, 1), :] + parts_times(parts, grp_ref[c])
            after.append(moved + last)
            rows = [jnp.sum(q_ref[s, c].astype(F32) * spread, axis=0, keepdims=True) for s in range(VECTOR_STEPS)]
            for s in range(VECTOR_STEPS, SPAN - 1, 2):
                pair = parts_times(parts, jnp.concatenate([q_ref[s, c], q_ref[s + 1, c]], axis=1))
                rows += [pair[:, :WIDTH], pair[:, WIDTH:]]
            rows.append(moved)
            base = pl.multiple_of(g * SPAN, SPAN)
            states = jnp.concatenate(rows, axis=0) + off_ref[pl.ds(b * steps + base, SPAN), :]
            states_ref[pl.ds(base, SPAN), b * WIDTH : (b + 1) * WIDTH] = states
            mean = jnp.mean(states * states, axis=-1, keepdims=True)
            normed = states * lax.rsqrt(mean + 1e-05) * gain_ref[b : b + 1, :]
            normed_ref[pl.ds(base, SPAN), b * WIDTH : (b + 1) * WIDTH] = normed.astype(BF16)
        return tuple(after)

    lax.fori_loop(0, GROUPS, group, tuple(entry), unroll=16)


def replay(kept, init, y_maps, x_maps, off, grp, gain, q):
    steps = SPAN * GROUPS
    return pl.pallas_call(
        replay_kernel,
        out_shape=(
            jax.ShapeDtypeStruct((steps, 2 * WIDTH), F32),
            jax.ShapeDtypeStruct((steps, 2 * WIDTH), BF16),
        ),
        in_specs=[VMEM] * 12,
        out_specs=(VMEM, VMEM),
        compiler_params=pltpu.CompilerParams(vmem_limit_bytes=16_000_000),
        name="replay",
    )(kept, init, *y_maps, *x_maps, off, grp, gain, pltpu.with_memory_space_constraint(q, pltpu.VMEM))


def weight_rows(k, c):
    z = places()[2]
    return pl.multiple_of((lax.rem(z + k, 4) * 2 + c) * 2 * WIDTH, 2 * WIDTH)


def products(parts, gate_ref, up_ref, n):
    wide = 2 * WIDTH
    gate = up = None
    for ref, row in parts:
        chunk = ref[...]
        g = jnp.dot(chunk, gate_ref[pl.ds(row, wide), n : n + wide], preferred_element_type=F32)
        u = jnp.dot(chunk, up_ref[pl.ds(row, wide), n : n + wide], preferred_element_type=F32)
        gate = g if gate is None else gate + g
        up = u if up is None else up + u
    return gate, up


AHEAD = (0, 3, 1, 2)


def mine_kernel(m0, m1, m3, m2, gate_ref, up_ref, gate_out, up_out):
    core = places()[3]
    parts = [(ref, weight_rows(k, core)) for ref, k in zip((m0, m1, m3, m2), AHEAD)]
    wide = 2 * WIDTH
    for n in range(0, gate_ref.shape[1], wide):
        gate_out[:, n : n + wide], up_out[:, n : n + wide] = products(parts, gate_ref, up_ref, n)


def forward_kernel(theirs_ref, gate_in, up_in, gate_ref, up_ref, down_ref, send_ref, hidden):
    core = places()[3]
    parts = [(theirs_ref.at[i], weight_rows(k, 1 - core)) for i, k in enumerate(AHEAD)]
    wide = 2 * WIDTH
    for n in range(0, gate_ref.shape[1], wide):
        gate, up = products(parts, gate_ref, up_ref, n)
        gate = gate + gate_in[:, n : n + wide]
        up = up + up_in[:, n : n + wide]
        hidden[:, n : n + wide] = (gate / (1.0 + jnp.exp(-gate)) * up).astype(BF16)
    for k in range(4):
        columns = down_ref[:, pl.ds(weight_rows(k, 1 - core), wide)]
        send_ref[k] = jnp.dot(hidden[...], columns, preferred_element_type=F32).astype(BF16)


def keep_kernel(hidden, down_ref, keep_ref):
    core = places()[3]
    for k in range(4):
        columns = down_ref[:, pl.ds(weight_rows(k, core), 2 * WIDTH)]
        keep_ref[k] = jnp.dot(hidden[...], columns, preferred_element_type=F32)


def forward(mine, gate_weight, up_weight, down_weight):
    steps, units = mine[0].shape[0], gate_weight.shape[1]
    gate_weight, up_weight, down_weight = [
        pltpu.with_memory_space_constraint(w, pltpu.VMEM) for w in (gate_weight, up_weight, down_weight)
    ]
    params = pltpu.CompilerParams(vmem_limit_bytes=16_000_000)
    theirs = other_core(jnp.stack(mine))
    part = pltpu.VMEM((steps, units), F32)
    gate, up = pl.pallas_call(
        mine_kernel,
        out_shape=(part, part),
        in_specs=[VMEM] * 6,
        out_specs=(VMEM, VMEM),
        compiler_params=params,
        name="mine",
    )(*mine, gate_weight, up_weight)
    sent, hidden = pl.pallas_call(
        forward_kernel,
        out_shape=(pltpu.VMEM((4, steps, 2 * WIDTH), BF16), pltpu.VMEM((steps, units), BF16)),
        in_specs=[VMEM] * 6,
        out_specs=(VMEM, VMEM),
        compiler_params=params,
        name="forward",
    )(theirs, gate, up, gate_weight, up_weight, down_weight)
    kept = pl.pallas_call(
        keep_kernel,
        out_shape=pltpu.VMEM((4, steps, 2 * WIDTH), F32),
        in_specs=[VMEM] * 2,
        out_specs=VMEM,
        compiler_params=params,
        name="keep",
    )(hidden, down_weight)
    return kept, sent


def x_back(v, k):
    return lax.ppermute(v, "tm", [(y * 4 + x, y * 4 + (x + k) % 4) for y in range(4) for x in range(4)])


def y_back(v, k):
    return lax.ppermute(v, "tm", [(y * 4 + x, (y + k) % 4 * 4 + x) for y in range(4) for x in range(4)])


def z_back(v, k):
    return lax.ppermute(v, "block", [(z * 2 + c, (z + k) % 4 * 2 + c) for z in range(4) for c in range(2)])


def other_core(v):
    return lax.ppermute(v, "block", [(s, s ^ 1) for s in range(8)])


def body(
    noise,
    retain,
    control_weight,
    input_weight,
    initial_state,
    norm_gain,
    gate_weight,
    up_weight,
    down_weight,
):
    q, off, own, grp, kept = compose(noise.T, retain.T, control_weight, input_weight)
    x_maps = [x_back(own, k) for k in (1, 2, 3)]
    total = row_map([own, *x_maps])
    y_maps = [y_back(total, k) for k in (1, 2, 3)]
    states, normed = replay(
        kept, initial_state.reshape(2, WIDTH), y_maps, x_maps, off, grp, norm_gain.reshape(2, WIDTH), q
    )
    mine = [normed] + [z_back(normed, k) for k in (1, 3, 2)]
    keep, sent = forward(mine, gate_weight, up_weight, down_weight)
    chip = keep + other_core(sent).astype(F32)
    low = chip.astype(BF16)
    mixed = lax.optimization_barrier(states + chip[0])
    for k in (2, 1, 3):
        mixed = mixed + z_back(low[k], k).astype(F32)
    return mixed.astype(BF16)


def solution(mesh):
    placed = (
        P("tm", None),
        P("tm", "block"),
        P(None, "block", None, None),
        P(None, "block"),
        P("block"),
        P("block"),
        P(None, "block"),
        P(None, "block"),
        P("block", None),
    )
    return jax.shard_map(body, mesh=mesh, in_specs=placed, out_specs=P("tm", "block"), check_vma=False)
```
